32 devices in a mesh: row: 2 (over z_hi), tm: 8 (over y, x, core), space: 2 (over z_lo).
Axes of the slice: x: 2, y: 2, z: 4 (z_hi: 2, z_lo: 2; z = z_hi * 2 + z_lo), core: 2. Of those that a mesh axis runs over, the one named last changes fastest.
Arguments:
- block_input: bfloat16 [2, 32, 256, 1024], P('row', 'tm', 'space'), may hold values from -6 to 6
- action_table: bfloat16 [8, 1024], P(None, 'tm'), may hold values from -3 to 3
- norm_gain: bfloat16 [3, 1024], P(None, 'tm'), may hold values from 0.5 to 1.5
- norm_bias: bfloat16 [3, 1024], P(None, 'tm'), may hold values from -2 to 2
- space_qkv: bfloat16 [1024, 3072], P('tm'), may hold values from -0.1875 to 0.1875
- space_out: bfloat16 [1024, 1024], P('tm'), may hold values from -0.75 to 0.75
- time_qkv: bfloat16 [1024, 3072], P('tm'), may hold values from -0.1875 to 0.1875
- time_out: bfloat16 [1024, 1024], P('tm'), may hold values from -0.375 to 0.375
- ffn_in: bfloat16 [1024, 4096], P('tm'), may hold values from -0.1875 to 0.1875
- ffn_bias_in: bfloat16 [4096], P('tm'), may hold values from -2 to 2
- ffn_out: bfloat16 [4096, 1024], P('tm'), may hold values from -0.09375 to 0.09375
- ffn_bias_out: bfloat16 [1024], P('tm'), may hold values from -2 to 2
- out_grad: bfloat16 [2, 32, 256, 1024], P('row', 'tm', 'space'), may hold values from -6 to 6
- frame_segment: int32 [2, 32], P('row'), may hold values from 0 to 1, as said below
- frame_action: int32 [2, 32], P('row', 'tm'), may hold values from 0 to 7
Outputs:
- block_output: bfloat16 [2, 32, 256, 1024], P('row', 'tm', 'space')
- input_grad: float32 [2, 32, 256, 1024], P('row', 'tm', 'space')
- action_table_grad: float32 [8, 1024], P(None, 'tm')
- norm_gain_grad: float32 [3, 1024], P(None, 'tm')
- norm_bias_grad: float32 [3, 1024], P(None, 'tm')
- space_qkv_grad: float32 [1024, 3072], P('tm')
- space_out_grad: float32 [1024, 1024], P('tm')
- time_qkv_grad: float32 [1024, 3072], P('tm')
- time_out_grad: float32 [1024, 1024], P('tm')
- ffn_in_grad: float32 [1024, 4096], P('tm')
- ffn_bias_in_grad: float32 [4096], P('tm')
- ffn_out_grad: float32 [4096, 1024], P('tm')
- ffn_bias_out_grad: float32 [1024], P('tm')
The draws below stay inside these ranges and needn't reach their ends.
Inputs may be any that keep to these rules, and one draw needn't show every extreme that they name: `frame_segment`: in each row the ids never fall, start at 0 and rise by one from clip to clip; each clip spans 12 to 20 frames, and in every row one clip spans exactly 20 frames.
All inputs are finite; a program needn't handle non-finite values.
Results may differ from the reference program's by a relative error of at most 0.019.
Values may be sent and summed in bfloat16 or wider, within the bound.
A program may use at most 256 MiB of HBM per device.

```python
import math
from functools import partial
import jax
import jax.numpy as jnp
from jax import lax

MODEL = 1024
HEADS = 16
HEAD_DIM = 64
FFN = 4096
ACTIONS = 8
GRID = 256
SEG_MOST = 20
ROWS = 2
FRAMES = 32


def draw_frame_segment(key, part):
    key = jax.random.fold_in(key, 11)
    sign_key, shift_key = jax.random.split(key)
    mean_len = SEG_MOST - 4
    pair_count = FRAMES // (2 * mean_len)
    first_shift = jax.random.randint(sign_key, (ROWS, 1), 0, 2) * 8 - 4
    other_shift = jax.random.randint(shift_key, (ROWS, pair_count), -4, 5)[:, 1:]
    shifts = jnp.concatenate((first_shift, other_shift), axis=1)
    lengths = jnp.stack((mean_len + shifts, mean_len - shifts), axis=-1).reshape(ROWS, 2 * pair_count)
    ends = jnp.cumsum(lengths, axis=1)
    frame_ids = jnp.arange(FRAMES)
    return jnp.sum((frame_ids[None, :, None] >= ends[:, None, :]).astype(jnp.int32), axis=-1).astype(jnp.int32)


def touch_ends(values, rng, low, largest):
    spot = [jax.random.randint(jax.random.fold_in(rng, axis), (), 0, length) for axis, length in enumerate(values.shape)]
    longest = values.shape.index(max(values.shape))
    beside = spot[:longest] + [(spot[longest] + 1) % values.shape[longest]] + spot[longest + 1:]
    return values.at[tuple(spot)].set(low).at[tuple(beside)].set(largest)


def block_scale(key, extent, cuts, low, top_value):
    loudness, own = 1.0, jax.random.fold_in(key, 6)
    for position, shards_of in cuts:
        heights = jnp.exp(jax.random.uniform(jax.random.fold_in(own, position), (shards_of,), jnp.float32, low / len(cuts), top_value / len(cuts)))
        loudness = loudness * jnp.repeat(heights, extent[position] // shards_of).reshape([-1 if axis == position else 1 for axis in range(len(extent))])
    return loudness


def gaussian(key, extent, width, most, shards=(), held_as=jnp.bfloat16):
    values = jax.random.normal(key, extent, jnp.float32) * width
    if len(shards) > 0:
        values = block_scale(key, extent, shards, -0.22, 0.18) * values
    return jnp.clip(values, min=-most, max=most).astype(held_as)


def setup_inputs(seed: int = 0) -> dict:
    key_list = jax.random.split(jax.random.key(seed), 16)
    block_input = gaussian(key_list[0], (ROWS, FRAMES, GRID, MODEL), 1.0, 6.0, ((0, 2), (1, 8), (2, 2)))
    action_table = gaussian(key_list[1], (ACTIONS, MODEL), 0.5, 3.0, ((1, 8),))
    norm_gain = jnp.clip(1.0 + 0.1 * jax.random.normal(key_list[2], (3, MODEL), jnp.float32), 0.5, 1.5).astype(jnp.bfloat16)
    norm_bias = gaussian(key_list[3], (3, MODEL), 0.3, 2.0, ((1, 8),))
    space_qkv = gaussian(key_list[4], (MODEL, 3 * MODEL), MODEL ** -0.5, 0.1875, ((0, 8),))
    space_out = gaussian(key_list[5], (MODEL, MODEL), (MODEL // 16) ** -0.5, 0.75, ((0, 8),))
    time_qkv = gaussian(key_list[6], (MODEL, 3 * MODEL), MODEL ** -0.5, 0.1875, ((0, 8),))
    time_out = gaussian(key_list[7], (MODEL, MODEL), (MODEL // 4) ** -0.5, 0.375, ((0, 8),))
    ffn_in = gaussian(key_list[8], (MODEL, FFN), MODEL ** -0.5, 0.1875, ((0, 8),))
    ffn_bias_in = gaussian(key_list[9], (FFN,), 0.3, 2.0, ((0, 8),))
    ffn_out = gaussian(key_list[10], (FFN, MODEL), FFN ** -0.5, 0.09375, ((0, 8),))
    ffn_bias_out = gaussian(key_list[11], (MODEL,), 0.3, 2.0, ((0, 8),))
    out_grad = gaussian(key_list[12], (ROWS, FRAMES, GRID, MODEL), 1.0, 6.0, ((0, 2), (1, 8), (2, 2)))
    frame_segment = draw_frame_segment(jax.random.fold_in(key_list[15], 71), 0)
    frame_action = touch_ends(jax.random.randint(key_list[14], (ROWS, FRAMES), 0, ACTIONS), jax.random.fold_in(key_list[14], 1), 0, ACTIONS - 1).astype(jnp.int32)
    return {"block_input": block_input, "action_table": action_table, "norm_gain": norm_gain, "norm_bias": norm_bias, "space_qkv": space_qkv, "space_out": space_out, "time_qkv": time_qkv, "time_out": time_out, "ffn_in": ffn_in, "ffn_bias_in": ffn_bias_in, "ffn_out": ffn_out, "ffn_bias_out": ffn_bias_out, "out_grad": out_grad, "frame_segment": frame_segment, "frame_action": frame_action}


@jax.custom_vjp
def low(v):
    return lax.optimization_barrier(v.astype(jnp.bfloat16)).astype(jnp.float32)

@jax.custom_vjp
def low_back(v):
    return v

def low_keep(v):
    return (low(v), None)

def low_pass(kept, grad):
    return (grad,)

def back_keep(v):
    return (v, None)

def back_low(kept, grad):
    return (low(grad),)
low.defvjp(low_keep, low_pass)
low_back.defvjp(back_keep, back_low)
EPSILON = 1e-05
NEG_FILL = -1e+30
HIGHEST = lax.Precision.HIGHEST

def layer_norm(values, gain_row, shift_row):
    row_mean = lax.optimization_barrier(jnp.mean(values, axis=-1, keepdims=True))
    centred = values - row_mean
    spread = lax.optimization_barrier(jnp.mean(centred * centred, axis=-1, keepdims=True))
    return centred * lax.rsqrt(spread + EPSILON) * gain_row + shift_row

def project(values, weight):
    return jnp.einsum('nd,df->nf', values, weight, precision=HIGHEST)

def space_frame(packed):
    score_scale = 1.0 / math.sqrt(HEAD_DIM)
    query_heads = packed[:, :MODEL].reshape(GRID, HEADS, HEAD_DIM)
    key_heads = packed[:, MODEL:2 * MODEL].reshape(GRID, HEADS, HEAD_DIM)
    value_heads = packed[:, 2 * MODEL:].reshape(GRID, HEADS, HEAD_DIM)
    scores = low_back(jnp.einsum('qhe,khe->hqk', query_heads, key_heads, precision=HIGHEST) * score_scale)
    attn_probs = low(jax.nn.softmax(scores, axis=-1))
    mixed_rows = jnp.einsum('hqk,khe->qhe', attn_probs, value_heads, precision=HIGHEST)
    return low_back(low(mixed_rows.reshape(GRID, MODEL)))

def time_row(row_pair):
    packed, segment_row = row_pair
    score_scale = 1.0 / math.sqrt(HEAD_DIM)
    query_heads = packed[:, :, :MODEL].reshape(FRAMES, GRID, HEADS, HEAD_DIM)
    key_heads = packed[:, :, MODEL:2 * MODEL].reshape(FRAMES, GRID, HEADS, HEAD_DIM)
    value_heads = packed[:, :, 2 * MODEL:].reshape(FRAMES, GRID, HEADS, HEAD_DIM)
    frame_ids = jnp.arange(FRAMES)
    allowed = (frame_ids[None, :] <= frame_ids[:, None]) & (segment_row[None, :] == segment_row[:, None])
    scores = low_back(jnp.einsum('fphe,gphe->phfg', query_heads, key_heads, precision=HIGHEST) * score_scale)
    scores = jnp.where(allowed[None, None], scores, NEG_FILL)
    attn_probs = low(jax.nn.softmax(scores, axis=-1))
    mixed_rows = jnp.einsum('phfg,gphe->fphe', attn_probs, value_heads, precision=HIGHEST)
    return low_back(low(mixed_rows.reshape(FRAMES, GRID, MODEL)))

def forward(frame_segment, frame_action, inputs, action_table, norm_gain, norm_bias, space_qkv, space_out, time_qkv, time_out, ffn_in, ffn_bias_in, ffn_out, ffn_bias_out):
    one_hot = (frame_action[:, :, None] == jnp.arange(ACTIONS)[None, None, :]).astype(jnp.float32)
    embedded = jnp.einsum('rfa,ad->rfd', one_hot, action_table, precision=HIGHEST)
    hidden_zero = (inputs + embedded[:, :, None, :]).reshape(-1, MODEL)
    normed = low(layer_norm(hidden_zero, norm_gain[0], norm_bias[0]))
    packed = low_back(low(project(normed, space_qkv)))
    mixed_rows = lax.map(jax.checkpoint(space_frame), packed.reshape(ROWS * FRAMES, GRID, 3 * MODEL))
    hidden_one = hidden_zero + low_back(project(mixed_rows.reshape(-1, MODEL), space_out))
    normed = low(layer_norm(hidden_one, norm_gain[1], norm_bias[1]))
    packed = low_back(low(project(normed, time_qkv)))
    mixed_rows = lax.map(jax.checkpoint(time_row), (packed.reshape(ROWS, FRAMES, GRID, 3 * MODEL), frame_segment))
    hidden_two = hidden_one + low_back(project(mixed_rows.reshape(-1, MODEL), time_out))
    normed = low(layer_norm(hidden_two, norm_gain[2], norm_bias[2]))
    pre_act = low_back(project(normed, ffn_in) + ffn_bias_in)
    activated = low(jax.nn.gelu(pre_act))
    result = hidden_two + low_back(project(activated, ffn_out) + ffn_bias_out)
    return result.reshape(ROWS, FRAMES, GRID, MODEL)

def reference(block_input, action_table, norm_gain, norm_bias, space_qkv, space_out, time_qkv, time_out, ffn_in, ffn_bias_in, ffn_out, ffn_bias_out, out_grad, frame_segment, frame_action):
    params = tuple((entry_array.astype(jnp.float32) for entry_array in (block_input, action_table, norm_gain, norm_bias, space_qkv, space_out, time_qkv, time_out, ffn_in, ffn_bias_in, ffn_out, ffn_bias_out)))
    result, pullback = jax.vjp(partial(forward, frame_segment, frame_action), *params)
    grads_all = pullback(out_grad.astype(jnp.float32))
    return (result.astype(jnp.bfloat16), grads_all[0], grads_all[1], grads_all[2], grads_all[3], grads_all[4], grads_all[5], grads_all[6], grads_all[7], grads_all[8], grads_all[9], grads_all[10], grads_all[11])
```

```python
import math

import jax
import jax.numpy as jnp
from jax import lax
from jax.experimental import pallas as pl
from jax.experimental.pallas import tpu as pltpu
from jax.sharding import PartitionSpec as P

MODEL = 1024
HEADS = 16
HEAD_DIM = 64
ACTIONS = 8
TILE = 256
PAIR = 2 * HEAD_DIM
PAIRS = HEADS // 2
SCALE = 1.0 / math.sqrt(HEAD_DIM)

EPSILON = 1e-05
NEG_FILL = -1e30
BF = jnp.bfloat16
F32 = jnp.float32


def layer_norm(values, gain_row, shift_row):
    row_mean = jnp.mean(values, axis=-1, keepdims=True)
    centred = values - row_mean
    spread = jnp.mean(centred * centred, axis=-1, keepdims=True)
    return centred * lax.rsqrt(spread + EPSILON) * gain_row + shift_row


def forward_dot(values, weight):
    return jnp.dot(values, weight, preferred_element_type=F32)


def weight_grad(left_rows, right_rows):
    return lax.dot_general(
        left_rows, right_rows, (((0,), (0,)), ((), ())), preferred_element_type=F32
    )


def back_dot(grad_rows, weight):
    return lax.dot_general(
        grad_rows, weight, (((1,), (1,)), ((), ())), preferred_element_type=F32
    )


def dot_nt(a, b):
    return lax.dot_general(a, b, (((1,), (1,)), ((), ())), preferred_element_type=F32)


def dot_nn(a, b):
    return lax.dot_general(a, b, (((1,), (0,)), ((), ())), preferred_element_type=F32)


def dot_tn(a, b):
    return lax.dot_general(a, b, (((0,), (0,)), ((), ())), preferred_element_type=F32)


def of_head(half, values):
    lane = lax.broadcasted_iota(jnp.int32, values.shape, 1)
    keep = (lane < HEAD_DIM) if half == 0 else (lane >= HEAD_DIM)
    return jnp.where(keep, values, jnp.zeros_like(values))


def join_heads(first, second):
    lane = lax.broadcasted_iota(jnp.int32, first.shape, 1)
    return jnp.where(lane < HEAD_DIM, first, second)


def pair_cols(pair, part):
    return pl.ds(pl.multiple_of(part * MODEL + pair * PAIR, PAIR), PAIR)


def attn_fwd_kernel(tiles, masked, packed_ref, *refs):
    if masked:
        col_ref, row_ref, mixed_ref, probs_ref = refs
    else:
        mixed_ref, probs_ref = refs

    def one_pair(pair, carry):
        for t in range(tiles):
            mine = pl.ds(t * TILE, TILE)
            width = (t + 1) * TILE
            seen = pl.ds(0, width)
            query = packed_ref[mine, pair_cols(pair, 0)] * jnp.asarray(SCALE, BF)
            key = packed_ref[seen, pair_cols(pair, 1)]
            value = packed_ref[seen, pair_cols(pair, 2)]
            if masked:
                same = col_ref[mine, :] == row_ref[:, seen]
                order = lax.broadcasted_iota(
                    jnp.int32, (TILE, width), 0
                ) + t * TILE >= lax.broadcasted_iota(jnp.int32, (TILE, width), 1)
                allowed = same & order
            outs = []
            for half in range(2):
                scores = dot_nt(of_head(half, query), key)
                if masked:
                    scores = jnp.where(allowed, scores, NEG_FILL)
                top = jnp.max(scores, axis=1, keepdims=True)
                raised = jnp.exp(scores - top)
                total = jnp.sum(raised, axis=1, keepdims=True)
                probs = (raised * (1.0 / total)).astype(BF)
                probs_ref[2 * pair + half, mine, seen] = probs
                outs.append(dot_nn(probs, value))
            mixed_ref[mine, pair_cols(pair, 0)] = join_heads(*outs).astype(BF)
        return carry

    lax.fori_loop(0, PAIRS, one_pair, 0, unroll=2)


def attn_bwd_kernel(tiles, packed_ref, probs_ref, grad_ref, out_ref, key_acc, value_acc):
    def one_pair(pair, carry):
        for t in reversed(range(tiles)):
            mine = pl.ds(t * TILE, TILE)
            seen = pl.ds(0, (t + 1) * TILE)
            query = packed_ref[mine, pair_cols(pair, 0)] * jnp.asarray(SCALE, BF)
            key = packed_ref[seen, pair_cols(pair, 1)]
            value = packed_ref[seen, pair_cols(pair, 2)]
            grad = grad_ref[mine, pair_cols(pair, 0)]
            dqs, dks, dvs = [], [], []
            for half in range(2):
                probs_low = probs_ref[2 * pair + half, mine, seen]
                probs = probs_low.astype(F32)
                dprobs = dot_nt(of_head(half, grad), value)
                delta = jnp.sum(dprobs * probs, axis=1, keepdims=True)
                dscores = (probs * (dprobs - delta)).astype(BF)
                dqs.append(dot_nn(dscores, key))
                dks.append(dot_tn(dscores, query))
                dvs.append(dot_tn(probs_low, grad))
            out_ref[mine, pair_cols(pair, 0)] = (join_heads(*dqs) * SCALE).astype(BF)
            dkey, dvalue = join_heads(*dks), join_heads(*dvs)
            if tiles == 1:
                out_ref[seen, pair_cols(pair, 1)] = dkey.astype(BF)
                out_ref[seen, pair_cols(pair, 2)] = dvalue.astype(BF)
            elif t == tiles - 1:
                key_acc[...] = dkey
                value_acc[...] = dvalue
            else:
                key_acc[seen, :] += dkey
                value_acc[seen, :] += dvalue
        if tiles > 1:
            out_ref[:, pair_cols(pair, 1)] = key_acc[...].astype(BF)
            out_ref[:, pair_cols(pair, 2)] = value_acc[...].astype(BF)
        return carry

    lax.fori_loop(0, PAIRS, one_pair, 0, unroll=2)


def blocks(rows, span):
    return {
        "packed": pl.BlockSpec((span, 3 * MODEL), lambda t: (t, 0)),
        "mixed": pl.BlockSpec((span, MODEL), lambda t: (t, 0)),
        "probs": pl.BlockSpec((HEADS, span, span), lambda t: (0, t, 0)),
        "col": pl.BlockSpec((span, 1), lambda t: (t, 0)),
        "row": pl.BlockSpec((1, span), lambda t: (0, t)),
    }


def attention(packed, span, groups=None):
    rows = packed.shape[0]
    at = blocks(rows, span)
    masked = groups is not None
    extra = (groups[:, None], groups[None, :]) if masked else ()
    specs = [at["packed"]] + ([at["col"], at["row"]] if masked else [])
    return pl.pallas_call(
        lambda *refs: attn_fwd_kernel(span // TILE, masked, *refs),
        grid=(rows // span,),
        in_specs=specs,
        out_specs=[at["mixed"], at["probs"]],
        out_shape=[
            jax.ShapeDtypeStruct((rows, MODEL), BF),
            jax.ShapeDtypeStruct((HEADS, rows, span), BF),
        ],
        compiler_params=pltpu.CompilerParams(vmem_limit_bytes=48 * 2**20),
        cost_estimate=pl.CostEstimate(
            flops=8 * HEADS * rows * span * HEAD_DIM,
            bytes_accessed=rows * (8 * MODEL + 2 * HEADS * span),
            transcendentals=HEADS * rows * span,
        ),
        name="attention_forward",
    )(packed, *extra)


def attention_back(packed, probs, grad, span):
    rows = packed.shape[0]
    at = blocks(rows, span)
    return pl.pallas_call(
        lambda *refs: attn_bwd_kernel(span // TILE, *refs),
        grid=(rows // span,),
        in_specs=[at["packed"], at["probs"], at["mixed"]],
        out_specs=at["packed"],
        out_shape=jax.ShapeDtypeStruct((rows, 3 * MODEL), BF),
        scratch_shapes=[pltpu.VMEM((span, PAIR), F32), pltpu.VMEM((span, PAIR), F32)],
        compiler_params=pltpu.CompilerParams(vmem_limit_bytes=48 * 2**20),
        cost_estimate=pl.CostEstimate(
            flops=16 * HEADS * rows * span * HEAD_DIM,
            bytes_accessed=rows * (14 * MODEL + 2 * HEADS * span),
            transcendentals=0,
        ),
        name="attention_backward",
    )(packed, probs, grad)


def hop(block, axis, flip):
    size = lax.axis_size(axis)
    return lax.ppermute(block, axis, [(i, i ^ flip) for i in range(size)])


def add_low(one, other):
    return (one.astype(F32) + other.astype(F32)).astype(BF)


def lay_kernel(rows, places, *refs):
    parts, whole_ref, done = refs[: len(places)], refs[-2], refs[-1]
    me = lax.axis_index("tm")
    copies = []
    for i, (flip, start) in enumerate(places):
        at = pl.multiple_of((me ^ flip) * rows + start, 32)
        target = whole_ref.at[pl.ds(at, parts[i].shape[0]), :]
        copies.append(pltpu.make_async_copy(parts[i], target, done.at[i]))
        copies[-1].start()
    for copy in copies:
        copy.wait()


def gather_rows(block):
    if lax.axis_size("tm") != 8:
        return lax.all_gather(block, "tm", axis=0, tiled=True)
    rows = block.shape[0]
    half = rows // 2
    me = lax.axis_index("tm")
    by_two, by_four = hop(block, "tm", 2), hop(block, "tm", 4)
    low_six, high_six = hop(by_two[:half], "tm", 4), hop(by_four[half:], "tm", 2)
    pieces = ((block, 0, 0), (by_two, 2, 0), (by_four, 4, 0), (low_six, 6, 0), (high_six, 6, half))
    parts, places = [], []
    for piece, flip, start in pieces:
        for core in range(2):
            parts.append(hop(piece, "tm", 1) if core else piece)
            places.append((flip + core, start))
    return pl.pallas_call(
        lambda *refs: lay_kernel(rows, places, *refs),
        in_specs=[pl.BlockSpec(memory_space=pl.ANY)] * len(parts),
        out_specs=pl.BlockSpec(memory_space=pl.ANY),
        out_shape=jax.ShapeDtypeStruct((8 * rows,) + block.shape[1:], block.dtype),
        scratch_shapes=[pltpu.SemaphoreType.DMA((len(parts),))],
        cost_estimate=pl.CostEstimate(
            flops=0, bytes_accessed=32 * rows * block.shape[1], transcendentals=0
        ),
        name="lay_rows",
    )(*parts)


def scatter_rows(whole):
    size = lax.axis_size("tm")
    whole = whole.astype(BF)
    if size != 8:
        return lax.psum_scatter(whole, "tm", scatter_dimension=0, tiled=True)
    rows = whole.shape[0] // 8
    half = rows // 2
    me = lax.axis_index("tm")

    def share(flip):
        return lax.dynamic_slice(whole, ((me ^ flip) * rows, 0), (rows, whole.shape[1]))

    chip = {flip: add_low(share(flip), hop(share(flip + 1), "tm", 1)) for flip in (0, 2, 4, 6)}
    two, two_six = hop(chip[2][:half], "tm", 2), hop(chip[6][:half], "tm", 2)
    four, four_six = hop(chip[4][half:], "tm", 4), hop(chip[6][half:], "tm", 4)
    top = add_low(chip[0][:half], two)
    top_far = add_low(chip[4][:half], two_six)
    low = add_low(chip[0][half:], four)
    low_far = add_low(chip[2][half:], four_six)
    return jnp.concatenate(
        (add_low(top, hop(top_far, "tm", 4)), add_low(low, hop(low_far, "tm", 2))), axis=0
    )


def sum_planes(block):
    rows = block.shape[0]
    half, quarter = rows // 2, rows // 4
    cols = block.shape[1]
    mine, ours = lax.axis_index("space"), lax.axis_index("row")

    def cut(array, start, length):
        return lax.dynamic_slice(array, (start, 0), (length, cols))

    one = add_low(
        cut(block, mine * half, half), hop(cut(block, (1 - mine) * half, half), "space", 1)
    )
    two = add_low(
        cut(one, ours * quarter, quarter), hop(cut(one, (1 - ours) * quarter, quarter), "row", 1)
    )
    other = hop(two, "row", 1)
    both = jnp.where(
        ours == 0, jnp.concatenate((two, other), axis=0), jnp.concatenate((other, two), axis=0)
    )
    far = hop(both, "space", 1)
    return jnp.where(
        mine == 0, jnp.concatenate((both, far), axis=0), jnp.concatenate((far, both), axis=0)
    ).astype(F32)


def reduce_grad(whole):
    return sum_planes(scatter_rows(whole))


def gather_small(flat):
    size = lax.axis_size("tm")
    if size != 8:
        return lax.all_gather(flat, "tm", axis=0)
    me = lax.axis_index("tm")
    whole = jnp.zeros((size,) + flat.shape, flat.dtype)
    for flip in range(size):
        part = hop(flat, "tm", flip) if flip else flat
        whole = lax.dynamic_update_slice(whole, part[None], (me ^ flip,) + (0,) * flat.ndim)
    return whole


def scatter_small(shares):
    size = lax.axis_size("tm")
    if size != 8:
        own = lax.psum_scatter(shares, "tm", scatter_dimension=0, tiled=True)[0]
        return lax.psum(own, ("row", "space"))
    me = lax.axis_index("tm")
    own = lax.dynamic_index_in_dim(shares, me, 0, keepdims=False)
    for flip in range(1, size):
        own = own + hop(
            lax.dynamic_index_in_dim(shares, me ^ flip, 0, keepdims=False), "tm", flip
        )
    own = own + hop(own, "space", 1)
    return own + hop(own, "row", 1)


def body(
    block_input,
    action_table,
    norm_gain,
    norm_bias,
    space_qkv,
    space_out,
    time_qkv,
    time_out,
    ffn_in,
    ffn_bias_in,
    ffn_out,
    ffn_bias_out,
    out_grad,
    frame_segment,
    frame_action,
):
    tm, halves = lax.axis_size("tm"), lax.axis_size("space")
    slot, side = lax.axis_index("tm"), lax.axis_index("space")
    frame_count, half_grid = block_input.shape[1], block_input.shape[2]
    own_frames = frame_count // halves
    grid_all = half_grid * halves
    cut = half_grid // tm
    all_frames = frame_count * tm
    rows_dev = frame_count * half_grid
    width = MODEL // tm
    hidden_units = ffn_bias_in.shape[0]

    small = gather_small(
        jnp.concatenate(
            [a.reshape(-1, width) for a in (action_table, norm_gain, norm_bias)]
            + [ffn_bias_out.reshape(1, width), ffn_bias_in.reshape(-1, width)]
        )
    )
    lines = ACTIONS + 7
    by_row = small[:, :lines].transpose(1, 0, 2).reshape(lines, MODEL)
    table_full = by_row[:ACTIONS]
    gains = by_row[ACTIONS : ACTIONS + 3].astype(F32)
    shifts = by_row[ACTIONS + 3 : ACTIONS + 6].astype(F32)
    bias_out = by_row[ACTIONS + 6].astype(F32)
    bias_in = small[:, lines:].reshape(-1).astype(F32)

    inputs = lax.all_to_all(block_input[0], "space", 0, 1, tiled=True)
    actions = lax.dynamic_slice(frame_action[0], (side * own_frames,), (own_frames,))
    one_hot = (actions[:, None] == jnp.arange(ACTIONS)[None, :]).astype(BF)
    embedded = forward_dot(one_hot, table_full)

    space_in_w = gather_rows(space_qkv)
    space_out_w = gather_rows(space_out)
    time_in_w = gather_rows(time_qkv)
    time_out_w = gather_rows(time_out)
    ffn_in_w = gather_rows(ffn_in)
    ffn_out_w = gather_rows(ffn_out)

    hidden_zero = (inputs.astype(F32) + embedded[:, None, :]).reshape(rows_dev, MODEL)
    normed_one = layer_norm(hidden_zero, gains[0], shifts[0]).astype(BF)
    packed_one = forward_dot(normed_one, space_in_w).astype(BF)
    space_mixed, space_probs = attention(packed_one, grid_all)
    hidden_one_own = (hidden_zero + forward_dot(space_mixed, space_out_w)).astype(BF)

    sent = hidden_one_own.reshape(own_frames, halves * tm, cut, MODEL)
    came = lax.all_to_all(sent, ("space", "tm"), 1, 0)
    hidden_one = (
        came.reshape(halves, tm, own_frames, cut, MODEL)
        .transpose(1, 0, 2, 3, 4)
        .reshape(rows_dev, MODEL)
        .astype(F32)
    )
    grad_out_low = lax.all_to_all(out_grad[0], "tm", 1, 0, tiled=True).reshape(rows_dev, MODEL)
    grad_out = grad_out_low.astype(F32)
    groups = (
        frame_segment[0].astype(jnp.int32)[:, None] * cut + jnp.arange(cut, dtype=jnp.int32)
    ).reshape(rows_dev)

    normed_two = layer_norm(hidden_one, gains[1], shifts[1]).astype(BF)
    packed_two = forward_dot(normed_two, time_in_w).astype(BF)
    time_mixed, time_probs = attention(packed_two, rows_dev, groups)
    hidden_two = hidden_one + forward_dot(time_mixed, time_out_w)
    normed_three = layer_norm(hidden_two, gains[2], shifts[2]).astype(BF)
    pre_act = forward_dot(normed_three, ffn_in_w) + bias_in
    activated, gelu_pull = jax.vjp(jax.nn.gelu, pre_act)
    act_low = activated.astype(BF)
    block_out = (hidden_two + forward_dot(act_low, ffn_out_w) + bias_out).astype(BF)
    block_output = lax.all_to_all(
        block_out.reshape(all_frames, cut, MODEL), "tm", 0, 1, tiled=True
    )[None]

    ffn_out_grad = reduce_grad(weight_grad(act_low, grad_out_low))
    bias_out_grad = jnp.sum(grad_out, axis=0)
    grad_pre = gelu_pull(back_dot(grad_out_low, ffn_out_w))[0]
    grad_pre_low = grad_pre.astype(BF)
    ffn_in_grad = reduce_grad(weight_grad(normed_three, grad_pre_low))
    bias_in_grad = jnp.sum(grad_pre_low.astype(F32), axis=0)
    norm_pull = jax.vjp(layer_norm, hidden_two, gains[2], shifts[2])[1]
    grad_hidden, gain_three, shift_three = norm_pull(back_dot(grad_pre_low, ffn_in_w))
    grad_two = grad_out + grad_hidden
    time_branch = grad_two.astype(BF)
    time_out_grad = reduce_grad(weight_grad(time_mixed, time_branch))
    time_grad_mixed = back_dot(time_branch, time_out_w).astype(BF)
    grad_packed_two = attention_back(packed_two, time_probs, time_grad_mixed, rows_dev)
    time_qkv_grad = reduce_grad(weight_grad(normed_two, grad_packed_two))
    norm_pull = jax.vjp(layer_norm, hidden_one, gains[1], shifts[1])[1]
    grad_hidden, gain_two, shift_two = norm_pull(back_dot(grad_packed_two, time_in_w))
    grad_one_low = (grad_two + grad_hidden).astype(BF)

    sent = (
        grad_one_low.reshape(tm, halves, own_frames, cut, MODEL)
        .transpose(1, 0, 2, 3, 4)
        .reshape(halves * tm, own_frames, cut, MODEL)
    )
    space_branch = lax.all_to_all(sent, ("space", "tm"), 0, 1).reshape(rows_dev, MODEL)
    space_out_grad = reduce_grad(weight_grad(space_mixed, space_branch))
    space_grad_mixed = back_dot(space_branch, space_out_w).astype(BF)
    grad_packed_one = attention_back(packed_one, space_probs, space_grad_mixed, grid_all)
    space_qkv_grad = reduce_grad(weight_grad(normed_one, grad_packed_one))
    norm_pull = jax.vjp(layer_norm, hidden_zero, gains[0], shifts[0])[1]
    grad_hidden, gain_one, shift_one = norm_pull(back_dot(grad_packed_one, space_in_w))
    grad_zero = space_branch.astype(F32) + grad_hidden
    frame_grad = jnp.sum(grad_zero.reshape(own_frames, grid_all, MODEL), axis=1)
    action_grad = jnp.dot(one_hot.astype(F32).T, frame_grad, precision=lax.Precision.HIGHEST)
    input_grad = lax.all_to_all(
        grad_zero.astype(BF).reshape(own_frames, grid_all, MODEL), "space", 1, 0, tiled=True
    ).astype(F32)[None]

    by_row = jnp.concatenate(
        (
            action_grad,
            jnp.stack((gain_one, gain_two, gain_three, shift_one, shift_two, shift_three)),
            bias_out_grad[None],
        )
    )
    shares = jnp.concatenate(
        (
            by_row.reshape(lines, tm, width).transpose(1, 0, 2),
            bias_in_grad.reshape(tm, -1, width),
        ),
        axis=1,
    )
    small_grads = scatter_small(shares)
    return (
        block_output,
        input_grad,
        small_grads[:ACTIONS],
        small_grads[ACTIONS : ACTIONS + 3],
        small_grads[ACTIONS + 3 : ACTIONS + 6],
        space_qkv_grad,
        space_out_grad,
        time_qkv_grad,
        time_out_grad,
        ffn_in_grad,
        small_grads[lines:].reshape(hidden_units),
        ffn_out_grad,
        small_grads[ACTIONS + 6],
    )


def solution(mesh):
    placed = (
        P("row", "tm", "space", None),
        P(None, "tm"),
        P(None, "tm"),
        P(None, "tm"),
        P("tm", None),
        P("tm", None),
        P("tm", None),
        P("tm", None),
        P("tm", None),
        P("tm"),
        P("tm", None),
        P("tm"),
        P("row", "tm", "space", None),
        P("row", None),
        P("row", "tm"),
    )
    return jax.shard_map(
        body,
        mesh=mesh,
        in_specs=placed,
        out_specs=(
            P("row", "tm", "space", None),
            P("row", "tm", "space", None),
            P(None, "tm"),
            P(None, "tm"),
            P(None, "tm"),
            P("tm", None),
            P("tm", None),
            P("tm", None),
            P("tm", None),
            P("tm", None),
            P("tm"),
            P("tm", None),
            P("tm"),
        ),
        check_vma=False,
    )
```

```python
import math

import jax
import jax.numpy as jnp
from jax import lax
from jax.experimental import pallas as pl
from jax.experimental.pallas import tpu as pltpu
from jax.sharding import PartitionSpec as P

MODEL = 1024
HEADS = 16
HEAD_DIM = 64
ACTIONS = 8
TILE = 256
PAIR = 2 * HEAD_DIM
PAIRS = HEADS // 2
SCALE = 1.0 / math.sqrt(HEAD_DIM)

EPSILON = 1e-05
NEG_FILL = -1e30
BF = jnp.bfloat16
F32 = jnp.float32


def layer_norm(values, gain_row, shift_row):
    row_mean = jnp.mean(values, axis=-1, keepdims=True)
    centred = values - row_mean
    spread = jnp.mean(centred * centred, axis=-1, keepdims=True)
    return centred * lax.rsqrt(spread + EPSILON) * gain_row + shift_row


def forward_dot(values, weight):
    return jnp.dot(values, weight, preferred_element_type=F32)


def weight_grad(left_rows, right_rows):
    return lax.dot_general(
        left_rows, right_rows, (((0,), (0,)), ((), ())), preferred_element_type=F32
    )


def back_dot(grad_rows, weight):
    return lax.dot_general(
        grad_rows, weight, (((1,), (1,)), ((), ())), preferred_element_type=F32
    )


def dot_nt(a, b):
    return lax.dot_general(a, b, (((1,), (1,)), ((), ())), preferred_element_type=F32)


def dot_nn(a, b):
    return lax.dot_general(a, b, (((1,), (0,)), ((), ())), preferred_element_type=F32)


def dot_tn(a, b):
    return lax.dot_general(a, b, (((0,), (0,)), ((), ())), preferred_element_type=F32)


def of_head(half, values):
    lane = lax.broadcasted_iota(jnp.int32, values.shape, 1)
    keep = (lane < HEAD_DIM) if half == 0 else (lane >= HEAD_DIM)
    return jnp.where(keep, values, jnp.zeros_like(values))


def join_heads(first, second):
    lane = lax.broadcasted_iota(jnp.int32, first.shape, 1)
    return jnp.where(lane < HEAD_DIM, first, second)


def pair_cols(pair, part):
    return pl.ds(pl.multiple_of(part * MODEL + pair * PAIR, PAIR), PAIR)


def attn_fwd_kernel(tiles, masked, packed_ref, *refs):
    if masked:
        col_ref, row_ref, mixed_ref, probs_ref = refs
    else:
        mixed_ref, probs_ref = refs

    def one_pair(pair, carry):
        for t in range(tiles):
            mine = pl.ds(t * TILE, TILE)
            width = (t + 1) * TILE
            seen = pl.ds(0, width)
            query = packed_ref[mine, pair_cols(pair, 0)] * jnp.asarray(SCALE, BF)
            key = packed_ref[seen, pair_cols(pair, 1)]
            value = packed_ref[seen, pair_cols(pair, 2)]
            if masked:
                same = col_ref[mine, :] == row_ref[:, seen]
                order = lax.broadcasted_iota(
                    jnp.int32, (TILE, width), 0
                ) + t * TILE >= lax.broadcasted_iota(jnp.int32, (TILE, width), 1)
                allowed = same & order
            outs = []
            for half in range(2):
                scores = dot_nt(of_head(half, query), key)
                if masked:
                    scores = jnp.where(allowed, scores, NEG_FILL)
                top = jnp.max(scores, axis=1, keepdims=True)
                raised = jnp.exp(scores - top)
                total = jnp.sum(raised, axis=1, keepdims=True)
                probs = (raised * (1.0 / total)).astype(BF)
                probs_ref[2 * pair + half, mine, seen] = probs
                outs.append(dot_nn(probs, value))
            mixed_ref[mine, pair_cols(pair, 0)] = join_heads(*outs).astype(BF)
        return carry

    lax.fori_loop(0, PAIRS, one_pair, 0, unroll=2)


def attn_bwd_kernel(tiles, packed_ref, probs_ref, grad_ref, out_ref, key_acc, value_acc):
    def one_pair(pair, carry):
        for t in reversed(range(tiles)):
            mine = pl.ds(t * TILE, TILE)
            seen = pl.ds(0, (t + 1) * TILE)
            query = packed_ref[mine, pair_cols(pair, 0)] * jnp.asarray(SCALE, BF)
            key = packed_ref[seen, pair_cols(pair, 1)]
            value = packed_ref[seen, pair_cols(pair, 2)]
            grad = grad_ref[mine, pair_cols(pair, 0)]
            dqs, dks, dvs = [], [], []
            for half in range(2):
                probs_low = probs_ref[2 * pair + half, mine, seen]
                probs = probs_low.astype(F32)
                dprobs = dot_nt(of_head(half, grad), value)
                delta = jnp.sum(dprobs * probs, axis=1, keepdims=True)
                dscores = (probs * (dprobs - delta)).astype(BF)
                dqs.append(dot_nn(dscores, key))
                dks.append(dot_tn(dscores, query))
                dvs.append(dot_tn(probs_low, grad))
            out_ref[mine, pair_cols(pair, 0)] = (join_heads(*dqs) * SCALE).astype(BF)
            dkey, dvalue = join_heads(*dks), join_heads(*dvs)
            if tiles == 1:
                out_ref[seen, pair_cols(pair, 1)] = dkey.astype(BF)
                out_ref[seen, pair_cols(pair, 2)] = dvalue.astype(BF)
            elif t == tiles - 1:
                key_acc[...] = dkey
                value_acc[...] = dvalue
            else:
                key_acc[seen, :] += dkey
                value_acc[seen, :] += dvalue
        if tiles > 1:
            out_ref[:, pair_cols(pair, 1)] = key_acc[...].astype(BF)
            out_ref[:, pair_cols(pair, 2)] = value_acc[...].astype(BF)
        return carry

    lax.fori_loop(0, PAIRS, one_pair, 0, unroll=2)


def blocks(rows, span):
    return {
        "packed": pl.BlockSpec((span, 3 * MODEL), lambda t: (t, 0)),
        "mixed": pl.BlockSpec((span, MODEL), lambda t: (t, 0)),
        "probs": pl.BlockSpec((HEADS, span, span), lambda t: (0, t, 0)),
        "col": pl.BlockSpec((span, 1), lambda t: (t, 0)),
        "row": pl.BlockSpec((1, span), lambda t: (0, t)),
    }


def attention(packed, span, groups=None):
    rows = packed.shape[0]
    at = blocks(rows, span)
    masked = groups is not None
    extra = (groups[:, None], groups[None, :]) if masked else ()
    specs = [at["packed"]] + ([at["col"], at["row"]] if masked else [])
    return pl.pallas_call(
        lambda *refs: attn_fwd_kernel(span // TILE, masked, *refs),
        grid=(rows // span,),
        in_specs=specs,
        out_specs=[at["mixed"], at["probs"]],
        out_shape=[
            jax.ShapeDtypeStruct((rows, MODEL), BF),
            jax.ShapeDtypeStruct((HEADS, rows, span), BF),
        ],
        compiler_params=pltpu.CompilerParams(vmem_limit_bytes=48 * 2**20),
        cost_estimate=pl.CostEstimate(
            flops=8 * HEADS * rows * span * HEAD_DIM,
            bytes_accessed=rows * (8 * MODEL + 2 * HEADS * span),
            transcendentals=HEADS * rows * span,
        ),
        name="attention_forward",
    )(packed, *extra)


def attention_back(packed, probs, grad, span):
    rows = packed.shape[0]
    at = blocks(rows, span)
    return pl.pallas_call(
        lambda *refs: attn_bwd_kernel(span // TILE, *refs),
        grid=(rows // span,),
        in_specs=[at["packed"], at["probs"], at["mixed"]],
        out_specs=at["packed"],
        out_shape=jax.ShapeDtypeStruct((rows, 3 * MODEL), BF),
        scratch_shapes=[pltpu.VMEM((span, PAIR), F32), pltpu.VMEM((span, PAIR), F32)],
        compiler_params=pltpu.CompilerParams(vmem_limit_bytes=48 * 2**20),
        cost_estimate=pl.CostEstimate(
            flops=16 * HEADS * rows * span * HEAD_DIM,
            bytes_accessed=rows * (14 * MODEL + 2 * HEADS * span),
            transcendentals=0,
        ),
        name="attention_backward",
    )(packed, probs, grad)


def hop(block, axis, flip):
    size = lax.axis_size(axis)
    return lax.ppermute(block, axis, [(i, i ^ flip) for i in range(size)])


def add_low(one, other):
    return (one.astype(F32) + other.astype(F32)).astype(BF)


def lay_kernel(rows, places, splits, *refs):
    count, outs = len(places), len(splits)
    parts, whole = refs[:count], refs[count : count + outs]
    stage = refs[count + outs : 2 * count + outs]
    came, left = refs[-2:]
    me = lax.axis_index("tm")
    inward = [pltpu.make_async_copy(parts[i], stage[i], came.at[i]) for i in range(count)]
    for copy in inward:
        copy.start()
    outward = []
    for i, (flip, start) in enumerate(places):
        at = pl.multiple_of((me ^ flip) * rows + start, 32)
        inward[i].wait()
        first = 0
        for j, columns in enumerate(splits):
            outward.append(
                pltpu.make_async_copy(
                    stage[i].at[:, pl.ds(first, columns)],
                    whole[j].at[pl.ds(at, parts[i].shape[0]), :],
                    left.at[i, j],
                )
            )
            outward[-1].start()
            first += columns
    for copy in outward:
        copy.wait()


def first_hops(block):
    if lax.axis_size("tm") != 8:
        return None
    return hop(block, "tm", 2), hop(block, "tm", 4)


def gather_rows(block, came, splits):
    if came is None:
        whole = lax.all_gather(block, "tm", axis=0, tiled=True)
        return jnp.split(whole, [sum(splits[:i]) for i in range(1, len(splits))], axis=1)
    rows = block.shape[0]
    half = rows // 2
    by_two, by_four = came
    low_six, high_six = hop(by_two[:half], "tm", 4), hop(by_four[half:], "tm", 2)
    pieces = ((block, 0, 0), (by_two, 2, 0), (by_four, 4, 0), (low_six, 6, 0), (high_six, 6, half))
    parts, places = [], []
    for piece, flip, start in pieces:
        for core in range(2):
            parts.append(hop(piece, "tm", 1) if core else piece)
            places.append((flip + core, start))
    return pl.pallas_call(
        lambda *refs: lay_kernel(rows, places, splits, *refs),
        in_specs=[pl.BlockSpec(memory_space=pl.ANY)] * len(parts),
        out_specs=[pl.BlockSpec(memory_space=pl.ANY)] * len(splits),
        out_shape=[jax.ShapeDtypeStruct((8 * rows, n), block.dtype) for n in splits],
        scratch_shapes=[pltpu.VMEM(part.shape, part.dtype) for part in parts]
        + [
            pltpu.SemaphoreType.DMA((len(parts),)),
            pltpu.SemaphoreType.DMA((len(parts), len(splits))),
        ],
        compiler_params=pltpu.CompilerParams(vmem_limit_bytes=20 * 2**20),
        cost_estimate=pl.CostEstimate(
            flops=0, bytes_accessed=32 * rows * block.shape[1], transcendentals=0
        ),
        name="lay_rows",
    )(*parts)


def after(value, *others):
    return lax.optimization_barrier((value,) + others)[0]


UNIT = 128
WIDE = 256
ORDERS = ((3, 7, 1, 5), (5, 7, 1, 3), (2, 6, 0, 4), (4, 6, 0, 2))


def product_kernel(order_ref, *refs):
    lefts, right_ref, out_ref, turned = refs[:4], refs[4], refs[5], refs[6]

    @pl.when(pl.program_id(2) == 0)
    def _():
        for i in range(4):
            turned[pl.ds(i * UNIT, UNIT), :] = lefts[i][...].T

    out_ref[...] = dot_nn(turned[...], right_ref[...]).astype(BF)


def product(left, right):
    tokens, width = left.shape
    subs = width // (8 * UNIT)
    half = right.shape[1] // 2
    tiles = half // WIDE
    flips = jnp.array(sum(ORDERS, ()), jnp.int32)
    order = (lax.axis_index("tm").astype(jnp.int32) ^ flips) * subs
    specs = [
        pl.BlockSpec((tokens, UNIT), lambda g, u, j, order, i=i: (0, order[4 * g + i] + u))
        for i in range(4)
    ]
    specs.append(pl.BlockSpec((tokens, WIDE), lambda g, u, j, order: (0, (g % 2) * tiles + j)))
    return pl.pallas_call(
        product_kernel,
        grid_spec=pltpu.PrefetchScalarGridSpec(
            num_scalar_prefetch=1,
            grid=(4, subs, tiles),
            in_specs=specs,
            out_specs=pl.BlockSpec(
                (None, None, 4 * UNIT, WIDE), lambda g, u, j, order: (g, u * tiles + j, 0, 0)
            ),
            scratch_shapes=[pltpu.VMEM((4 * UNIT, tokens), BF)],
        ),
        out_shape=jax.ShapeDtypeStruct((4, subs * tiles, 4 * UNIT, WIDE), BF),
        compiler_params=pltpu.CompilerParams(vmem_limit_bytes=32 * 2**20),
        cost_estimate=pl.CostEstimate(
            flops=2 * tokens * width * right.shape[1],
            bytes_accessed=2 * (4 * tokens * width + 2 * tokens * right.shape[1])
            + 2 * width * right.shape[1],
            transcendentals=0,
        ),
        name="weight_product",
    )(order, *([left] * 4), right)


def reduce_kernel(counts, places, *refs):
    chunks, outs = len(counts), len(set(place[0] for place in places))
    tiles_ref, out_refs = refs[:chunks], refs[chunks : chunks + outs]
    (own, from_core, from_chip, from_owner, share, from_space, from_row, final) = refs[
        chunks + outs : chunks + outs + 8
    ]
    (load_sem, core_sem, chip_sem, owner_sem, space_sem, row_sem, back_sem, last_sem) = refs[
        chunks + outs + 8 :
    ]
    me, side, level = lax.axis_index("tm"), lax.axis_index("space"), lax.axis_index("row")
    total = sum(counts)
    source = [(c, k) for c in range(chunks) for k in range(counts[c])]
    r = UNIT

    def tm_at(flip):
        return {"tm": me ^ flip}

    barrier = pltpu.get_barrier_semaphore()
    for device in (tm_at(1), tm_at(2), tm_at(4), {"space": 1 - side}, {"row": 1 - level}):
        pl.semaphore_signal(barrier, inc=1, device_id=device, device_id_type=pl.DeviceIdType.MESH)
    pl.semaphore_wait(barrier, 5)

    def remote(src, dst, sems, device):
        return pltpu.make_async_remote_copy(
            src_ref=src,
            dst_ref=dst,
            send_sem=sems.at[0],
            recv_sem=sems.at[1],
            device_id=device,
            device_id_type=pl.DeviceIdType.MESH,
        )

    sent = []

    def start(copy):
        copy.start()
        sent.append(copy)
        return copy

    loads, cores, chips, owners, spaces, rows, backs, lasts = ({} for _ in range(8))

    def stage_core(t):
        c, k = source[t]
        for h in range(2):
            cores[t, h] = start(
                remote(tiles_ref[c].at[h, k], from_core.at[t, h], core_sem.at[t, h], tm_at(1))
            )
            loads[t, h] = pltpu.make_async_copy(
                tiles_ref[c].at[2 + h, k], own.at[t, h], load_sem.at[t, h]
            )
            loads[t, h].start()

    def stage_chip(t):
        for h in range(2):
            loads[t, h].wait()
            cores[t, h].wait_recv()
            own[t, h] = add_low(own[t, h], from_core[t, h])
            chips[t, h] = start(
                remote(
                    own.at[t, h, pl.ds(0, 2 * r)],
                    from_chip.at[t, h],
                    chip_sem.at[t, h],
                    tm_at(4 if h else 2),
                )
            )

    def stage_owner(t):
        for h in range(2):
            chips[t, h].wait_recv()
            own[t, h, pl.ds(2 * r, 2 * r)] = add_low(
                own[t, h, pl.ds(2 * r, 2 * r)], from_chip[t, h]
            )
            owners[t, h] = start(
                remote(
                    own.at[t, h, pl.ds(3 * r, r)],
                    from_owner.at[t, h],
                    owner_sem.at[t, h],
                    tm_at(2 if h else 4),
                )
            )

    def stage_space(t):
        for h in range(2):
            owners[t, h].wait_recv()
            share[t, h] = add_low(own[t, h, pl.ds(2 * r, r)], from_owner[t, h])
        spaces[t] = start(
            remote(share.at[t, 1 - side], from_space.at[t], space_sem.at[t], {"space": 1 - side})
        )

    def stage_row(t):
        spaces[t].wait_recv()
        share[t, side] = add_low(share[t, side], from_space[t])
        other = pl.multiple_of((1 - level) * (r // 2), r // 2)
        rows[t] = start(
            remote(
                share.at[t, side, pl.ds(other, r // 2)],
                from_row.at[t],
                row_sem.at[t],
                {"row": 1 - level},
            )
        )

    def stage_back(t):
        rows[t].wait_recv()
        mine = pl.ds(pl.multiple_of(level * (r // 2), r // 2), r // 2)
        final[t, side, mine] = add_low(share[t, side, mine], from_row[t])
        backs[t] = start(
            remote(
                final.at[t, side, mine], final.at[t, side, mine], back_sem.at[t], {"row": 1 - level}
            )
        )

    def stage_last(t):
        backs[t].wait_recv()
        lasts[t] = start(
            remote(final.at[t, side], final.at[t, side], last_sem.at[t], {"space": 1 - side})
        )

    def stage_out(t):
        lasts[t].wait_recv()
        out, row, column, half = places[t]
        for h in range(2):
            out_refs[out][pl.ds(row, r), pl.ds(column + h * half, WIDE)] = final[t, h].astype(F32)

    stages = (
        stage_core,
        stage_chip,
        stage_owner,
        stage_space,
        stage_row,
        stage_back,
        stage_last,
        stage_out,
    )
    for step in range(total + len(stages) - 1):
        for number, stage in enumerate(stages):
            if 0 <= step - number < total:
                stage(step - number)
    for copy in sent:
        copy.wait_send()


def reduce_products(pairs, number):
    if lax.axis_size("tm") != 8:
        result = []
        for left, right in pairs:
            whole = weight_grad(left, right).astype(BF)
            block = lax.psum_scatter(whole, "tm", scatter_dimension=0, tiled=True)
            result.append(lax.psum(block, ("row", "space")).astype(F32))
        return result
    tiles = [product(left, right) for left, right in pairs]
    counts = [block.shape[1] for block in tiles]
    places, shapes = [], []
    for which, (left, right) in enumerate(pairs):
        half = right.shape[1] // 2
        shapes.append((left.shape[1] // 8, right.shape[1]))
        for sub in range(left.shape[1] // (8 * UNIT)):
            for j in range(half // WIDE):
                places.append((which, sub * UNIT, j * WIDE, half))
    n = sum(counts)
    vmem = pltpu.VMEM
    dma = pltpu.SemaphoreType.DMA
    return pl.pallas_call(
        lambda *refs: reduce_kernel(counts, places, *refs),
        in_specs=[pl.BlockSpec(memory_space=pl.ANY)] * len(tiles),
        out_specs=[pl.BlockSpec(memory_space=pltpu.VMEM)] * len(pairs),
        out_shape=[jax.ShapeDtypeStruct(shape, F32) for shape in shapes],
        scratch_shapes=[
            vmem((n, 2, 4 * UNIT, WIDE), BF),
            vmem((n, 2, 4 * UNIT, WIDE), BF),
            vmem((n, 2, 2 * UNIT, WIDE), BF),
            vmem((n, 2, UNIT, WIDE), BF),
            vmem((n, 2, UNIT, WIDE), BF),
            vmem((n, UNIT, WIDE), BF),
            vmem((n, UNIT // 2, WIDE), BF),
            vmem((n, 2, UNIT, WIDE), BF),
            dma((n, 2)),
            dma((n, 2, 2)),
            dma((n, 2, 2)),
            dma((n, 2, 2)),
            dma((n, 2)),
            dma((n, 2)),
            dma((n, 2)),
            dma((n, 2)),
        ],
        compiler_params=pltpu.CompilerParams(
            vmem_limit_bytes=56 * 2**20, collective_id=number, has_side_effects=True
        ),
        cost_estimate=pl.CostEstimate(
            flops=1024, bytes_accessed=n * 8 * UNIT * WIDE, transcendentals=0
        ),
        name="reduce_tiles",
    )(*tiles)


def gather_small(flat):
    size = lax.axis_size("tm")
    if size != 8:
        return lax.all_gather(flat, "tm", axis=0)
    me = lax.axis_index("tm")
    whole = jnp.zeros((size,) + flat.shape, flat.dtype)
    for flip in range(size):
        part = hop(flat, "tm", flip) if flip else flat
        whole = lax.dynamic_update_slice(whole, part[None], (me ^ flip,) + (0,) * flat.ndim)
    return whole


def scatter_small(shares):
    size = lax.axis_size("tm")
    if size != 8:
        own = lax.psum_scatter(shares, "tm", scatter_dimension=0, tiled=True)[0]
        return lax.psum(own, ("row", "space"))
    me = lax.axis_index("tm")
    own = lax.dynamic_index_in_dim(shares, me, 0, keepdims=False)
    for flip in range(1, size):
        own = own + hop(
            lax.dynamic_index_in_dim(shares, me ^ flip, 0, keepdims=False), "tm", flip
        )
    own = own + hop(own, "space", 1)
    return own + hop(own, "row", 1)


def body(
    block_input,
    action_table,
    norm_gain,
    norm_bias,
    space_qkv,
    space_out,
    time_qkv,
    time_out,
    ffn_in,
    ffn_bias_in,
    ffn_out,
    ffn_bias_out,
    out_grad,
    frame_segment,
    frame_action,
):
    tm, halves = lax.axis_size("tm"), lax.axis_size("space")
    slot, side = lax.axis_index("tm"), lax.axis_index("space")
    frame_count, half_grid = block_input.shape[1], block_input.shape[2]
    own_frames = frame_count // halves
    grid_all = half_grid * halves
    cut = half_grid // tm
    all_frames = frame_count * tm
    rows_dev = frame_count * half_grid
    width = MODEL // tm
    hidden_units = ffn_bias_in.shape[0]

    small = gather_small(
        jnp.concatenate(
            [a.reshape(-1, width) for a in (action_table, norm_gain, norm_bias)]
            + [ffn_bias_out.reshape(1, width), ffn_bias_in.reshape(-1, width)]
        )
    )
    lines = ACTIONS + 7
    by_row = small[:, :lines].transpose(1, 0, 2).reshape(lines, MODEL)
    table_full = by_row[:ACTIONS]
    gains = by_row[ACTIONS : ACTIONS + 3].astype(F32)
    shifts = by_row[ACTIONS + 3 : ACTIONS + 6].astype(F32)
    bias_out = by_row[ACTIONS + 6].astype(F32)
    bias_in = small[:, lines:].reshape(-1).astype(F32)

    inputs = lax.all_to_all(block_input[0], "space", 0, 1, tiled=True)
    actions = lax.dynamic_slice(frame_action[0], (side * own_frames,), (own_frames,))
    one_hot = (actions[:, None] == jnp.arange(ACTIONS)[None, :]).astype(BF)
    embedded = forward_dot(one_hot, table_full)

    blocks_in = [
        jnp.concatenate((space_qkv, space_out), axis=1),
        jnp.concatenate((time_qkv, time_out), axis=1),
        ffn_in,
        ffn_out,
    ]
    came = []
    for i, block in enumerate(blocks_in):
        if i and came[-1] is not None:
            blocks_in[i] = after(block, *came[-1])
        came.append(first_hops(blocks_in[i]))
    space_in_w, space_out_w = gather_rows(blocks_in[0], came[0], (3 * MODEL, MODEL))
    time_in_w, time_out_w = gather_rows(blocks_in[1], came[1], (3 * MODEL, MODEL))
    (ffn_in_w,) = gather_rows(blocks_in[2], came[2], (ffn_in.shape[1],))
    (ffn_out_w,) = gather_rows(blocks_in[3], came[3], (MODEL,))

    hidden_zero = (inputs.astype(F32) + embedded[:, None, :]).reshape(rows_dev, MODEL)
    normed_one = layer_norm(hidden_zero, gains[0], shifts[0]).astype(BF)
    packed_one = forward_dot(normed_one, space_in_w).astype(BF)
    space_mixed, space_probs = attention(packed_one, grid_all)
    hidden_one_own = (hidden_zero + forward_dot(space_mixed, space_out_w)).astype(BF)

    sent = hidden_one_own.reshape(own_frames, halves * tm, cut, MODEL)
    came = lax.all_to_all(sent, ("space", "tm"), 1, 0)
    hidden_one = (
        came.reshape(halves, tm, own_frames, cut, MODEL)
        .transpose(1, 0, 2, 3, 4)
        .reshape(rows_dev, MODEL)
        .astype(F32)
    )
    grad_out_low = lax.all_to_all(out_grad[0], "tm", 1, 0, tiled=True).reshape(rows_dev, MODEL)
    grad_out = grad_out_low.astype(F32)
    groups = (
        frame_segment[0].astype(jnp.int32)[:, None] * cut + jnp.arange(cut, dtype=jnp.int32)
    ).reshape(rows_dev)

    normed_two = layer_norm(hidden_one, gains[1], shifts[1]).astype(BF)
    packed_two = forward_dot(normed_two, time_in_w).astype(BF)
    time_mixed, time_probs = attention(packed_two, rows_dev, groups)
    hidden_two = hidden_one + forward_dot(time_mixed, time_out_w)
    normed_three = layer_norm(hidden_two, gains[2], shifts[2]).astype(BF)
    pre_act = forward_dot(normed_three, ffn_in_w) + bias_in
    activated, gelu_pull = jax.vjp(jax.nn.gelu, pre_act)
    act_low, slope = lax.optimization_barrier(
        (activated.astype(BF), gelu_pull(jnp.ones_like(pre_act))[0].astype(BF))
    )
    block_out = (hidden_two + forward_dot(act_low, ffn_out_w) + bias_out).astype(BF)
    block_output = lax.all_to_all(
        block_out.reshape(all_frames, cut, MODEL), "tm", 0, 1, tiled=True
    )[None]

    bias_out_grad = jnp.sum(grad_out, axis=0)
    grad_pre_low = (back_dot(grad_out_low, ffn_out_w) * slope.astype(F32)).astype(BF)
    bias_in_grad = jnp.sum(grad_pre_low.astype(F32), axis=0)
    norm_pull = jax.vjp(layer_norm, hidden_two, gains[2], shifts[2])[1]
    grad_hidden, gain_three, shift_three = norm_pull(back_dot(grad_pre_low, ffn_in_w))
    grad_two = grad_out + grad_hidden
    time_branch = grad_two.astype(BF)
    ffn_out_grad, ffn_in_grad = reduce_products(
        ((act_low, grad_out_low), (normed_three, grad_pre_low)), 1
    )
    time_grad_mixed = back_dot(time_branch, time_out_w).astype(BF)
    grad_packed_two = attention_back(packed_two, time_probs, time_grad_mixed, rows_dev)
    norm_pull = jax.vjp(layer_norm, hidden_one, gains[1], shifts[1])[1]
    grad_hidden, gain_two, shift_two = norm_pull(back_dot(grad_packed_two, time_in_w))
    grad_one_low = (grad_two + grad_hidden).astype(BF)

    sent = (
        grad_one_low.reshape(tm, halves, own_frames, cut, MODEL)
        .transpose(1, 0, 2, 3, 4)
        .reshape(halves * tm, own_frames, cut, MODEL)
    )
    space_branch = lax.all_to_all(sent, ("space", "tm"), 0, 1).reshape(rows_dev, MODEL)
    space_grad_mixed = back_dot(space_branch, space_out_w).astype(BF)
    grad_packed_one = attention_back(packed_one, space_probs, space_grad_mixed, grid_all)
    norm_pull = jax.vjp(layer_norm, hidden_zero, gains[0], shifts[0])[1]
    grad_hidden, gain_one, shift_one = norm_pull(back_dot(grad_packed_one, space_in_w))
    time_qkv_grad, time_out_grad, space_out_grad, space_qkv_grad = reduce_products(
        (
            (normed_two, grad_packed_two),
            (time_mixed, time_branch),
            (space_mixed, space_branch),
            (normed_one, grad_packed_one),
        ),
        2,
    )
    grad_zero = space_branch.astype(F32) + grad_hidden
    frame_grad = jnp.sum(grad_zero.reshape(own_frames, grid_all, MODEL), axis=1)
    action_grad = jnp.dot(one_hot.astype(F32).T, frame_grad, precision=lax.Precision.HIGHEST)
    input_grad = lax.all_to_all(
        grad_zero.astype(BF).reshape(own_frames, grid_all, MODEL), "space", 1, 0, tiled=True
    ).astype(F32)[None]

    by_row = jnp.concatenate(
        (
            action_grad,
            jnp.stack((gain_one, gain_two, gain_three, shift_one, shift_two, shift_three)),
            bias_out_grad[None],
        )
    )
    shares = jnp.concatenate(
        (
            by_row.reshape(lines, tm, width).transpose(1, 0, 2),
            bias_in_grad.reshape(tm, -1, width),
        ),
        axis=1,
    )
    small_grads = scatter_small(shares)
    return (
        block_output,
        input_grad,
        small_grads[:ACTIONS],
        small_grads[ACTIONS : ACTIONS + 3],
        small_grads[ACTIONS + 3 : ACTIONS + 6],
        space_qkv_grad,
        space_out_grad,
        time_qkv_grad,
        time_out_grad,
        ffn_in_grad,
        small_grads[lines:].reshape(hidden_units),
        ffn_out_grad,
        small_grads[ACTIONS + 6],
    )


def solution(mesh):
    placed = (
        P("row", "tm", "space", None),
        P(None, "tm"),
        P(None, "tm"),
        P(None, "tm"),
        P("tm", None),
        P("tm", None),
        P("tm", None),
        P("tm", None),
        P("tm", None),
        P("tm"),
        P("tm", None),
        P("tm"),
        P("row", "tm", "space", None),
        P("row", None),
        P("row", "tm"),
    )
    return jax.shard_map(
        body,
        mesh=mesh,
        in_specs=placed,
        out_specs=(
            P("row", "tm", "space", None),
            P("row", "tm", "space", None),
            P(None, "tm"),
            P(None, "tm"),
            P(None, "tm"),
            P("tm", None),
            P("tm", None),
            P("tm", None),
            P("tm", None),
            P("tm", None),
            P("tm"),
            P("tm", None),
            P("tm"),
        ),
        check_vma=False,
    )
```

```python
import math

import jax
import jax.numpy as jnp
from jax import lax
from jax.experimental import pallas as pl
from jax.experimental.pallas import tpu as pltpu
from jax.sharding import PartitionSpec as P

MODEL = 1024
HEADS = 16
HEAD_DIM = 64
ACTIONS = 8
TILE = 256
PAIR = 2 * HEAD_DIM
PAIRS = HEADS // 2
SCALE = 1.0 / math.sqrt(HEAD_DIM)

EPSILON = 1e-05
NEG_FILL = -1e30
BF = jnp.bfloat16
F32 = jnp.float32


def layer_norm(values, gain_row, shift_row):
    row_mean = jnp.mean(values, axis=-1, keepdims=True)
    centred = values - row_mean
    spread = jnp.mean(centred * centred, axis=-1, keepdims=True)
    return centred * lax.rsqrt(spread + EPSILON) * gain_row + shift_row


def forward_dot(values, weight):
    return jnp.dot(values, weight, preferred_element_type=F32)


def weight_grad(left_rows, right_rows):
    return lax.dot_general(
        left_rows, right_rows, (((0,), (0,)), ((), ())), preferred_element_type=F32
    )


def back_dot(grad_rows, weight):
    return lax.dot_general(
        grad_rows, weight, (((1,), (1,)), ((), ())), preferred_element_type=F32
    )


def dot_nt(a, b):
    return lax.dot_general(a, b, (((1,), (1,)), ((), ())), preferred_element_type=F32)


def dot_nn(a, b):
    return lax.dot_general(a, b, (((1,), (0,)), ((), ())), preferred_element_type=F32)


def dot_tn(a, b):
    return lax.dot_general(a, b, (((0,), (0,)), ((), ())), preferred_element_type=F32)


def of_head(half, values):
    lane = lax.broadcasted_iota(jnp.int32, values.shape, 1)
    keep = (lane < HEAD_DIM) if half == 0 else (lane >= HEAD_DIM)
    return jnp.where(keep, values, jnp.zeros_like(values))


def join_heads(first, second):
    lane = lax.broadcasted_iota(jnp.int32, first.shape, 1)
    return jnp.where(lane < HEAD_DIM, first, second)


def pair_cols(pair, part):
    if isinstance(pair, int):
        return pl.ds(part * MODEL + pair * PAIR, PAIR)
    return pl.ds(pl.multiple_of(part * MODEL + pair * PAIR, PAIR), PAIR)


def attn_fwd_kernel(tiles, masked, packed_ref, *refs):
    if masked:
        col_ref, row_ref, mixed_ref, probs_ref = refs
    else:
        mixed_ref, probs_ref = refs

    def one_pair(pair, carry):
        for t in range(tiles):
            mine = pl.ds(t * TILE, TILE)
            width = (t + 1) * TILE
            seen = pl.ds(0, width)
            query = packed_ref[mine, pair_cols(pair, 0)] * jnp.asarray(SCALE, BF)
            key = packed_ref[seen, pair_cols(pair, 1)]
            value = packed_ref[seen, pair_cols(pair, 2)]
            if masked:
                same = col_ref[mine, :] == row_ref[:, seen]
                order = lax.broadcasted_iota(
                    jnp.int32, (TILE, width), 0
                ) + t * TILE >= lax.broadcasted_iota(jnp.int32, (TILE, width), 1)
                allowed = same & order
            outs = []
            for half in range(2):
                scores = dot_nt(of_head(half, query), key)
                if masked:
                    scores = jnp.where(allowed, scores, NEG_FILL)
                top = jnp.max(scores, axis=1, keepdims=True)
                raised = jnp.exp(scores - top)
                total = jnp.sum(raised, axis=1, keepdims=True)
                probs = (raised * (1.0 / total)).astype(BF)
                probs_ref[2 * pair + half, mine, seen] = probs
                outs.append(dot_nn(probs, value))
            mixed_ref[mine, pair_cols(pair, 0)] = join_heads(*outs).astype(BF)
        return carry

    lax.fori_loop(0, PAIRS, one_pair, 0, unroll=2)


def attn_bwd_pair(base, tiles, pair, packed_ref, probs_ref, grad_ref, out_ref, accs=None):
    for t in reversed(range(tiles)):
        mine = pl.ds(base + t * TILE, TILE)
        seen = pl.ds(base, (t + 1) * TILE)
        query = packed_ref[mine, pair_cols(pair, 0)] * jnp.asarray(SCALE, BF)
        key = packed_ref[seen, pair_cols(pair, 1)]
        value = packed_ref[seen, pair_cols(pair, 2)]
        grad = grad_ref[mine, pair_cols(pair, 0)]
        dqs, dks, dvs = [], [], []
        for half in range(2):
            probs_low = probs_ref[2 * pair + half, mine, pl.ds(0, (t + 1) * TILE)]
            probs = probs_low.astype(F32)
            dprobs = dot_nt(of_head(half, grad), value)
            delta = jnp.sum(dprobs * probs, axis=1, keepdims=True)
            dscores = (probs * (dprobs - delta)).astype(BF)
            dqs.append(dot_nn(dscores, key))
            dks.append(dot_tn(dscores, query))
            dvs.append(dot_tn(probs_low, grad))
        out_ref[mine, pair_cols(pair, 0)] = (join_heads(*dqs) * SCALE).astype(BF)
        dkey, dvalue = join_heads(*dks), join_heads(*dvs)
        if tiles == 1:
            out_ref[seen, pair_cols(pair, 1)] = dkey.astype(BF)
            out_ref[seen, pair_cols(pair, 2)] = dvalue.astype(BF)
        elif t == tiles - 1:
            accs[0][...] = dkey
            accs[1][...] = dvalue
        else:
            accs[0][pl.ds(0, (t + 1) * TILE), :] += dkey
            accs[1][pl.ds(0, (t + 1) * TILE), :] += dvalue
    if tiles > 1:
        out_ref[:, pair_cols(pair, 1)] = accs[0][...].astype(BF)
        out_ref[:, pair_cols(pair, 2)] = accs[1][...].astype(BF)


def attn_bwd_kernel(tiles, packed_ref, probs_ref, grad_ref, out_ref, key_acc, value_acc):
    def one_pair(pair, carry):
        attn_bwd_pair(
            0, tiles, pair, packed_ref, probs_ref, grad_ref, out_ref, (key_acc, value_acc)
        )
        return carry

    lax.fori_loop(0, PAIRS, one_pair, 0, unroll=2)


def blocks(rows, span):
    return {
        "packed": pl.BlockSpec((span, 3 * MODEL), lambda t: (t, 0)),
        "mixed": pl.BlockSpec((span, MODEL), lambda t: (t, 0)),
        "probs": pl.BlockSpec((HEADS, span, span), lambda t: (0, t, 0)),
        "col": pl.BlockSpec((span, 1), lambda t: (t, 0)),
        "row": pl.BlockSpec((1, span), lambda t: (0, t)),
    }


def attention(packed, span, groups=None):
    rows = packed.shape[0]
    at = blocks(rows, span)
    masked = groups is not None
    extra = (groups[:, None], groups[None, :]) if masked else ()
    specs = [at["packed"]] + ([at["col"], at["row"]] if masked else [])
    return pl.pallas_call(
        lambda *refs: attn_fwd_kernel(span // TILE, masked, *refs),
        grid=(rows // span,),
        in_specs=specs,
        out_specs=[at["mixed"], at["probs"]],
        out_shape=[
            jax.ShapeDtypeStruct((rows, MODEL), BF),
            jax.ShapeDtypeStruct((HEADS, rows, span), BF),
        ],
        compiler_params=pltpu.CompilerParams(vmem_limit_bytes=48 * 2**20),
        cost_estimate=pl.CostEstimate(
            flops=8 * HEADS * rows * span * HEAD_DIM,
            bytes_accessed=rows * (8 * MODEL + 2 * HEADS * span),
            transcendentals=HEADS * rows * span,
        ),
        name="attention_forward",
    )(packed, *extra)


def attention_back(packed, probs, grad, span):
    rows = packed.shape[0]
    at = blocks(rows, span)
    return pl.pallas_call(
        lambda *refs: attn_bwd_kernel(span // TILE, *refs),
        grid=(rows // span,),
        in_specs=[at["packed"], at["probs"], at["mixed"]],
        out_specs=at["packed"],
        out_shape=jax.ShapeDtypeStruct((rows, 3 * MODEL), BF),
        scratch_shapes=[pltpu.VMEM((span, PAIR), F32), pltpu.VMEM((span, PAIR), F32)],
        compiler_params=pltpu.CompilerParams(vmem_limit_bytes=48 * 2**20),
        cost_estimate=pl.CostEstimate(
            flops=16 * HEADS * rows * span * HEAD_DIM,
            bytes_accessed=rows * (14 * MODEL + 2 * HEADS * span),
            transcendentals=0,
        ),
        name="attention_backward",
    )(packed, probs, grad)


def hop(block, axis, flip):
    size = lax.axis_size(axis)
    return lax.ppermute(block, axis, [(i, i ^ flip) for i in range(size)])


def add_low(one, other):
    return (one.astype(F32) + other.astype(F32)).astype(BF)


def lay_kernel(rows, places, splits, *refs):
    count, outs = len(places), len(splits)
    parts, whole = refs[:count], refs[count : count + outs]
    stage = refs[count + outs : 2 * count + outs]
    came, left = refs[-2:]
    me = lax.axis_index("tm")
    inward = [pltpu.make_async_copy(parts[i], stage[i], came.at[i]) for i in range(count)]
    for copy in inward:
        copy.start()
    outward = []
    for i, (flip, start) in enumerate(places):
        at = pl.multiple_of((me ^ flip) * rows + start, 32)
        inward[i].wait()
        first = 0
        for j, columns in enumerate(splits):
            outward.append(
                pltpu.make_async_copy(
                    stage[i].at[:, pl.ds(first, columns)],
                    whole[j].at[pl.ds(at, parts[i].shape[0]), :],
                    left.at[i, j],
                )
            )
            outward[-1].start()
            first += columns
    for copy in outward:
        copy.wait()


def first_hops(block):
    if lax.axis_size("tm") != 8:
        return None
    return hop(block, "tm", 2), hop(block, "tm", 4)


def second_hops(came):
    if came is None:
        return None
    half = came[0].shape[0] // 2
    return hop(came[0][:half], "tm", 4), hop(came[1][half:], "tm", 2)


def gather_rows(block, came, passed, splits):
    if came is None:
        whole = lax.all_gather(block, "tm", axis=0, tiled=True)
        return jnp.split(whole, [sum(splits[:i]) for i in range(1, len(splits))], axis=1)
    rows = block.shape[0]
    half = rows // 2
    by_two, by_four = came
    low_six, high_six = passed
    pieces = ((block, 0, 0), (by_two, 2, 0), (by_four, 4, 0), (low_six, 6, 0), (high_six, 6, half))
    parts, places = [], []
    for piece, flip, start in pieces:
        for core in range(2):
            parts.append(hop(piece, "tm", 1) if core else piece)
            places.append((flip + core, start))
    return pl.pallas_call(
        lambda *refs: lay_kernel(rows, places, splits, *refs),
        in_specs=[pl.BlockSpec(memory_space=pl.ANY)] * len(parts),
        out_specs=[pl.BlockSpec(memory_space=pl.ANY)] * len(splits),
        out_shape=[jax.ShapeDtypeStruct((8 * rows, n), block.dtype) for n in splits],
        scratch_shapes=[pltpu.VMEM(part.shape, part.dtype) for part in parts]
        + [
            pltpu.SemaphoreType.DMA((len(parts),)),
            pltpu.SemaphoreType.DMA((len(parts), len(splits))),
        ],
        compiler_params=pltpu.CompilerParams(vmem_limit_bytes=20 * 2**20),
        cost_estimate=pl.CostEstimate(
            flops=0, bytes_accessed=32 * rows * block.shape[1], transcendentals=0
        ),
        name="lay_rows",
    )(*parts)


def after(value, *others):
    return lax.optimization_barrier((value,) + others)[0]


def first_kernel(*refs):
    blocks, small_ref, tokens_ref = refs[:2], refs[2], refs[3]
    wholes, smalls_ref, frames_ref = refs[4:6], refs[6], refs[7]
    local, small_sem, frame_sem, near, far, core = refs[8:]
    me, side = lax.axis_index("tm"), lax.axis_index("space")
    rows = blocks[0].shape[0]
    half = rows // 2
    half_grid, own_frames = tokens_ref.shape[1], tokens_ref.shape[0] // 2

    barrier = pltpu.get_barrier_semaphore()
    for flip in range(1, 8):
        pl.semaphore_signal(
            barrier, inc=1, device_id={"tm": me ^ flip}, device_id_type=pl.DeviceIdType.MESH
        )
    pl.semaphore_signal(
        barrier, inc=1, device_id={"space": 1 - side}, device_id_type=pl.DeviceIdType.MESH
    )
    pl.semaphore_wait(barrier, 8)

    sent = []

    def send(src, dst, sems, device):
        copy = pltpu.make_async_remote_copy(
            src_ref=src,
            dst_ref=dst,
            send_sem=sems.at[0],
            recv_sem=sems.at[1],
            device_id=device,
            device_id_type=pl.DeviceIdType.MESH,
        )
        copy.start()
        sent.append(copy)
        return copy

    def place(w, flip, start, length):
        at = pl.multiple_of((me ^ flip) * rows + start, half)
        return wholes[w].at[pl.ds(at, length), :]

    arrived = {}
    for w in range(2):
        for number, (flip, start) in enumerate(((2, 0), (4, half), (2, half), (4, 0))):
            arrived[w, flip, start] = send(
                blocks[w].at[pl.ds(start, half), :],
                place(w, 0, start, half),
                near.at[w, number],
                {"tm": me ^ flip},
            )
    small_copies = [
        send(small_ref, smalls_ref.at[me], small_sem.at[flip], {"tm": me ^ flip})
        for flip in range(1, 8)
    ]
    columns = pl.ds(pl.multiple_of(side * half_grid, half_grid), half_grid)
    frame_copy = send(
        tokens_ref.at[pl.ds((1 - side) * own_frames, own_frames)],
        frames_ref.at[:, columns, :],
        frame_sem,
        {"space": 1 - side},
    )
    core_copies = [
        send(blocks[w], place(w, 0, 0, rows), core.at[w, 0], {"tm": me ^ 1}) for w in range(2)
    ]
    own = [
        pltpu.make_async_copy(small_ref, smalls_ref.at[me], local.at[0]),
        pltpu.make_async_copy(
            tokens_ref.at[pl.ds(side * own_frames, own_frames)],
            frames_ref.at[:, columns, :],
            local.at[1],
        ),
    ] + [pltpu.make_async_copy(blocks[w], place(w, 0, 0, rows), local.at[2 + w]) for w in range(2)]
    for copy in own:
        copy.start()
    for w in range(2):
        for number, (flip, start) in enumerate(((2, 0), (4, half), (2, half), (4, 0))):
            arrived[w, flip, start].wait_recv()
            block = place(w, flip, start, half)
            if number < 2:
                arrived[w, 6, start] = send(
                    block, block, far.at[w, number], {"tm": me ^ (6 - flip)}
                )
            core_copies.append(send(block, block, core.at[w, 1 + number], {"tm": me ^ 1}))
    for w in range(2):
        for number, start in enumerate((0, half)):
            arrived[w, 6, start].wait_recv()
            block = place(w, 6, start, half)
            core_copies.append(send(block, block, core.at[w, 5 + number], {"tm": me ^ 1}))
    for copy in small_copies + [frame_copy] + core_copies:
        copy.wait_recv()
    for copy in own:
        copy.wait()
    for copy in sent:
        copy.wait_send()


def first_gather(weights, small, tokens):
    if lax.axis_size("tm") != 8:
        return (
            *[lax.all_gather(weight, "tm", axis=0, tiled=True) for weight in weights],
            lax.all_gather(small, "tm", axis=0),
            lax.all_to_all(tokens, "space", 0, 1, tiled=True),
        )
    used = small.shape[0]
    small = jnp.pad(small, ((0, -used % 16), (0, 0)))
    frames, half_grid, model = tokens.shape
    dma = pltpu.SemaphoreType.DMA
    first, second, smalls, whole_frames = pl.pallas_call(
        first_kernel,
        in_specs=[pl.BlockSpec(memory_space=pltpu.VMEM)] * 4,
        out_specs=[pl.BlockSpec(memory_space=pl.ANY)] * 4,
        out_shape=[
            jax.ShapeDtypeStruct((8 * weight.shape[0], weight.shape[1]), weight.dtype)
            for weight in weights
        ]
        + [
            jax.ShapeDtypeStruct((8,) + small.shape, small.dtype),
            jax.ShapeDtypeStruct((frames // 2, 2 * half_grid, model), tokens.dtype),
        ],
        scratch_shapes=[
            dma((4,)),
            dma((8, 2)),
            dma((2,)),
            dma((2, 4, 2)),
            dma((2, 2, 2)),
            dma((2, 7, 2)),
        ],
        compiler_params=pltpu.CompilerParams(
            vmem_limit_bytes=16 * 2**20, collective_id=3, has_side_effects=True
        ),
        cost_estimate=pl.CostEstimate(flops=0, bytes_accessed=2**24, transcendentals=0),
        name="first_gather",
    )(*weights, small, tokens)
    return first, second, smalls[:, :used], whole_frames


UNIT = 128
WIDE = 256
SLOTS = 6
FINALS = 10
DELAYS = (0, 1, 3, 5, 7, 9, 11, 13)
ORDERS = ((3, 7, 1, 5), (5, 7, 1, 3), (2, 6, 0, 4), (4, 6, 0, 2))


def reduce_kernel(chunks, places, with_small, units, *refs):
    refs = list(refs)

    def take(count):
        taken = refs[:count]
        del refs[:count]
        return taken

    lefts, rights = take(chunks), take(chunks)
    small_ref = take(1)[0] if with_small else None
    packed_ref, probs_ref, grad_ref = take(3) if units else (None,) * 3
    out_refs = take(chunks)
    small_out = take(1)[0] if with_small else None
    packed_out = take(1)[0] if units else None
    (far, own, from_core, from_chip, from_owner, share, from_space, from_row, final) = take(9)
    (core_sem, chip_sem, owner_sem, space_sem, row_sem, back_sem, last_sem) = take(7)
    turned = take(len(refs))
    me, side, level = lax.axis_index("tm"), lax.axis_index("space"), lax.axis_index("row")
    total = len(places)
    r = UNIT

    def tm_at(flip):
        return {"tm": me ^ flip}

    barrier = pltpu.get_barrier_semaphore()
    for device in (tm_at(1), tm_at(2), tm_at(4), {"space": 1 - side}, {"row": 1 - level}):
        pl.semaphore_signal(barrier, inc=1, device_id=device, device_id_type=pl.DeviceIdType.MESH)
    pl.semaphore_wait(barrier, 5)

    def start(src, dst, sems, device):
        copy = pltpu.make_async_remote_copy(
            src_ref=src,
            dst_ref=dst,
            send_sem=sems.at[0],
            recv_sem=sems.at[1],
            device_id=device,
            device_id_type=pl.DeviceIdType.MESH,
        )
        copy.start()
        return copy

    cores, chips, owners, spaces, rows, backs, lasts = ({} for _ in range(7))

    def buffer_of(which):
        wide = lefts[which].shape[1] > 8 * UNIT
        return turned[1] if wide else turned[0]

    def part(t, h, order):
        which, row, column, half = places[t]
        if which == chunks:
            return jnp.concatenate([small_ref[me ^ flip] for flip in order], axis=0)
        rows_each = lefts[which].shape[1] // 8
        picked = [
            buffer_of(which)[pl.ds(pl.multiple_of((me ^ flip) * rows_each + row, r), r), :]
            for flip in order
        ]
        return dot_nn(
            jnp.concatenate(picked, axis=0), rights[which][:, pl.ds(column + h * half, WIDE)]
        )

    mine = {}

    def stage_core(t):
        which, slot = places[t][0], t % SLOTS
        if which < chunks and (t == 0 or places[t - 1][0] != which):
            buffer_of(which)[...] = lefts[which][...].T
        for h in range(2):
            if t >= SLOTS:
                cores[t - SLOTS, h].wait_send()
            far[slot, h] = part(t, h, ORDERS[h]).astype(BF)
            cores[t, h] = start(
                far.at[slot, h], from_core.at[slot, h], core_sem.at[slot, h], tm_at(1)
            )
        for h in range(2):
            if t >= SLOTS:
                chips[t - SLOTS, h].wait_send()
                owners[t - SLOTS, h].wait_send()
            own[slot, h] = part(t, h, ORDERS[2 + h]).astype(BF)

    def stage_chip(t):
        slot = t % SLOTS
        for h in range(2):
            cores[t, h].wait_recv()
            own[slot, h] = add_low(own[slot, h], from_core[slot, h])
            chips[t, h] = start(
                own.at[slot, h, pl.ds(0, 2 * r)],
                from_chip.at[slot, h],
                chip_sem.at[slot, h],
                tm_at(4 if h else 2),
            )

    def stage_owner(t):
        slot = t % SLOTS
        for h in range(2):
            chips[t, h].wait_recv()
            own[slot, h, pl.ds(2 * r, 2 * r)] = add_low(
                own[slot, h, pl.ds(2 * r, 2 * r)], from_chip[slot, h]
            )
            owners[t, h] = start(
                own.at[slot, h, pl.ds(3 * r, r)],
                from_owner.at[slot, h],
                owner_sem.at[slot, h],
                tm_at(2 if h else 4),
            )

    def stage_space(t):
        slot = t % SLOTS
        if t >= SLOTS:
            spaces[t - SLOTS].wait_send()
            rows[t - SLOTS].wait_send()
        for h in range(2):
            owners[t, h].wait_recv()
            share[slot, h] = add_low(own[slot, h, pl.ds(2 * r, r)], from_owner[slot, h])
        spaces[t] = start(
            share.at[slot, 1 - side], from_space.at[slot], space_sem.at[slot], {"space": 1 - side}
        )

    def stage_row(t):
        slot = t % SLOTS
        spaces[t].wait_recv()
        share[slot, side] = add_low(share[slot, side], from_space[slot])
        other = pl.multiple_of((1 - level) * (r // 2), r // 2)
        rows[t] = start(
            share.at[slot, side, pl.ds(other, r // 2)],
            from_row.at[slot],
            row_sem.at[slot],
            {"row": 1 - level},
        )

    def stage_back(t):
        slot = t % SLOTS
        rows[t].wait_recv()
        here = pl.ds(pl.multiple_of(level * (r // 2), r // 2), r // 2)
        last = t % FINALS
        final[last, side, here] = add_low(share[slot, side, here], from_row[slot])
        place = final.at[last, side, here]
        backs[t] = start(place, place, back_sem.at[last], {"row": 1 - level})

    def stage_last(t):
        slot = t % FINALS
        backs[t].wait_recv()
        place = final.at[slot, side]
        lasts[t] = start(place, place, last_sem.at[slot], {"space": 1 - side})

    def stage_out(t):
        slot = t % FINALS
        lasts[t].wait_recv()
        out, row, column, half = places[t]
        if out == chunks:
            small_out[...] = final[slot, 0].astype(F32)
        else:
            for h in range(2):
                out_refs[out][pl.ds(row, r), pl.ds(column + h * half, WIDE)] = final[
                    slot, h
                ].astype(F32)
        backs[t].wait_send()
        lasts[t].wait_send()

    stages = (
        stage_core,
        stage_chip,
        stage_owner,
        stage_space,
        stage_row,
        stage_back,
        stage_last,
        stage_out,
    )
    for step in range(total + DELAYS[-1]):
        for delay, stage in zip(DELAYS, stages):
            if 0 <= step - delay < total:
                stage(step - delay)
        if 0 < step <= units:
            frame, pair = divmod(step - 1, PAIRS)
            attn_bwd_pair(frame * TILE, 1, pair, packed_ref, probs_ref, grad_ref, packed_out)
    for t in range(max(0, total - SLOTS), total):
        for h in range(2):
            cores[t, h].wait_send()
            chips[t, h].wait_send()
            owners[t, h].wait_send()
        spaces[t].wait_send()
        rows[t].wait_send()


def reduce_products(pairs, number, small=None, attend=None):
    if lax.axis_size("tm") != 8:
        result = []
        for left, right in pairs:
            whole = weight_grad(left, right).astype(BF)
            block = lax.psum_scatter(whole, "tm", scatter_dimension=0, tiled=True)
            result.append(lax.psum(block, ("row", "space")).astype(F32))
        if small is not None:
            block = lax.psum_scatter(small, "tm", scatter_dimension=0, tiled=True)[0]
            result.append(lax.psum(block, ("row", "space")))
        if attend is not None:
            result.append(attention_back(*attend, TILE))
        return result
    places, shapes = [], []
    for which, (left, right) in enumerate(pairs):
        half = right.shape[1] // 2
        shapes.append((left.shape[1] // 8, right.shape[1]))
        for sub in range(left.shape[1] // (8 * UNIT)):
            for j in range(half // WIDE):
                places.append((which, sub * UNIT, j * WIDE, half))
    operands = [left for left, _ in pairs] + [right for _, right in pairs]
    outs = [jax.ShapeDtypeStruct(shape, F32) for shape in shapes]
    if small is not None:
        places.append((len(pairs), 0, 0, 0))
        padding = ((0, 0), (0, UNIT - small.shape[1]), (0, WIDE - small.shape[2]))
        operands.append(jnp.pad(small, padding))
        outs.append(jax.ShapeDtypeStruct((UNIT, WIDE), F32))
    units = 0
    if attend is not None:
        units = attend[0].shape[0] // TILE * PAIRS
        operands += list(attend)
        outs.append(jax.ShapeDtypeStruct(attend[0].shape, BF))
    widths = sorted({left.shape[1] for left, _ in pairs})
    tokens = pairs[0][0].shape[0]
    vmem = pltpu.VMEM
    dma = pltpu.SemaphoreType.DMA
    result = pl.pallas_call(
        lambda *refs: reduce_kernel(len(pairs), places, small is not None, units, *refs),
        in_specs=[pl.BlockSpec(memory_space=pltpu.VMEM)] * len(operands),
        out_specs=[pl.BlockSpec(memory_space=pltpu.VMEM)] * len(outs),
        out_shape=outs,
        scratch_shapes=[
            vmem((SLOTS, 2, 4 * UNIT, WIDE), BF),
            vmem((SLOTS, 2, 4 * UNIT, WIDE), BF),
            vmem((SLOTS, 2, 4 * UNIT, WIDE), BF),
            vmem((SLOTS, 2, 2 * UNIT, WIDE), BF),
            vmem((SLOTS, 2, UNIT, WIDE), BF),
            vmem((SLOTS, 2, UNIT, WIDE), BF),
            vmem((SLOTS, UNIT, WIDE), BF),
            vmem((SLOTS, UNIT // 2, WIDE), BF),
            vmem((FINALS, 2, UNIT, WIDE), BF),
            dma((SLOTS, 2, 2)),
            dma((SLOTS, 2, 2)),
            dma((SLOTS, 2, 2)),
            dma((SLOTS, 2)),
            dma((SLOTS, 2)),
            dma((FINALS, 2)),
            dma((FINALS, 2)),
        ]
        + [vmem((width, tokens), BF) for width in widths],
        compiler_params=pltpu.CompilerParams(
            vmem_limit_bytes=58 * 2**20, collective_id=number, has_side_effects=True
        ),
        cost_estimate=pl.CostEstimate(
            flops=1024, bytes_accessed=len(places) * 8 * UNIT * WIDE, transcendentals=0
        ),
        name="reduce_products",
    )(*operands)
    if small is not None:
        result = list(result)
        result[len(pairs)] = result[len(pairs)][: small.shape[1], : small.shape[2]]
    return result


def body(
    block_input,
    action_table,
    norm_gain,
    norm_bias,
    space_qkv,
    space_out,
    time_qkv,
    time_out,
    ffn_in,
    ffn_bias_in,
    ffn_out,
    ffn_bias_out,
    out_grad,
    frame_segment,
    frame_action,
):
    tm, halves = lax.axis_size("tm"), lax.axis_size("space")
    slot, side = lax.axis_index("tm"), lax.axis_index("space")
    frame_count, half_grid = block_input.shape[1], block_input.shape[2]
    own_frames = frame_count // halves
    grid_all = half_grid * halves
    cut = half_grid // tm
    all_frames = frame_count * tm
    rows_dev = frame_count * half_grid
    width = MODEL // tm
    hidden_units = ffn_bias_in.shape[0]

    space_in_w, space_out_w, small, inputs = first_gather(
        (space_qkv, space_out),
        jnp.concatenate(
            [a.reshape(-1, width) for a in (action_table, norm_gain, norm_bias)]
            + [ffn_bias_out.reshape(1, width), ffn_bias_in.reshape(-1, width)]
        ),
        block_input[0],
    )
    lines = ACTIONS + 7
    by_row = small[:, :lines].transpose(1, 0, 2).reshape(lines, MODEL)
    table_full = by_row[:ACTIONS]
    gains = by_row[ACTIONS : ACTIONS + 3].astype(F32)
    shifts = by_row[ACTIONS + 3 : ACTIONS + 6].astype(F32)
    bias_out = by_row[ACTIONS + 6].astype(F32)
    bias_in = small[:, lines:].reshape(-1).astype(F32)

    actions = lax.dynamic_slice(frame_action[0], (side * own_frames,), (own_frames,))
    one_hot = (actions[:, None] == jnp.arange(ACTIONS)[None, :]).astype(BF)
    embedded = forward_dot(one_hot, table_full)

    blocks_in = [jnp.concatenate((time_qkv, time_out), axis=1), ffn_in, ffn_out]
    came, passed = [], []
    for i, block in enumerate(blocks_in):
        if tm == 8:
            earlier = (passed[0] if i == 1 else came[1]) if i else (space_out_w,)
            blocks_in[i] = after(block, *earlier)
        came.append(first_hops(blocks_in[i]))
        passed.append(second_hops(came[i]))
    split = ((3 * MODEL, MODEL), (ffn_in.shape[1],), (MODEL,))
    gathered = [gather_rows(*all_of) for all_of in zip(blocks_in, came, passed, split)]
    time_in_w, time_out_w = gathered[0]
    (ffn_in_w,), (ffn_out_w,) = gathered[1:]
    if passed[1] is not None:
        out_grad = after(out_grad, *passed[1])

    hidden_zero = (inputs.astype(F32) + embedded[:, None, :]).reshape(rows_dev, MODEL)
    normed_one = layer_norm(hidden_zero, gains[0], shifts[0]).astype(BF)
    packed_one = forward_dot(normed_one, space_in_w).astype(BF)
    space_mixed, space_probs = attention(packed_one, grid_all)
    hidden_one_own = (hidden_zero + forward_dot(space_mixed, space_out_w)).astype(BF)

    sent = hidden_one_own.reshape(own_frames, halves * tm, cut, MODEL)
    blocks_t = lax.all_to_all(sent, ("space", "tm"), 1, 0)
    hidden_one = lax.optimization_barrier(
        blocks_t.reshape(halves, tm, own_frames, cut, MODEL)
        .transpose(1, 0, 2, 3, 4)
        .reshape(rows_dev, MODEL)
    ).astype(F32)
    grad_out_low = lax.all_to_all(out_grad[0], "tm", 1, 0, tiled=True).reshape(rows_dev, MODEL)
    grad_out = grad_out_low.astype(F32)
    groups = (
        frame_segment[0].astype(jnp.int32)[:, None] * cut + jnp.arange(cut, dtype=jnp.int32)
    ).reshape(rows_dev)

    normed_two = layer_norm(hidden_one, gains[1], shifts[1]).astype(BF)
    packed_two = forward_dot(normed_two, time_in_w).astype(BF)
    if came[1] is not None:
        packed_two = after(packed_two, *came[1])
    time_mixed, time_probs = attention(packed_two, rows_dev, groups)
    hidden_two = hidden_one + forward_dot(time_mixed, time_out_w)
    normed_three = layer_norm(hidden_two, gains[2], shifts[2]).astype(BF)
    pre_act = forward_dot(normed_three, ffn_in_w) + bias_in
    activated, gelu_pull = jax.vjp(jax.nn.gelu, pre_act)
    act_low, slope = lax.optimization_barrier(
        (activated.astype(BF), gelu_pull(jnp.ones_like(pre_act))[0].astype(BF))
    )
    block_out = (hidden_two + forward_dot(act_low, ffn_out_w) + bias_out).astype(BF)
    block_output = lax.all_to_all(
        block_out.reshape(all_frames, cut, MODEL), "tm", 0, 1, tiled=True
    )[None]

    bias_out_grad = jnp.sum(grad_out, axis=0)
    grad_pre_low = (back_dot(grad_out_low, ffn_out_w) * slope.astype(F32)).astype(BF)
    bias_in_grad = jnp.sum(grad_pre_low.astype(F32), axis=0)
    norm_pull = jax.vjp(layer_norm, hidden_two, gains[2], shifts[2])[1]
    grad_hidden, gain_three, shift_three = norm_pull(back_dot(grad_pre_low, ffn_in_w))
    grad_two = grad_out + grad_hidden
    time_branch = grad_two.astype(BF)
    time_grad_mixed = back_dot(time_branch, time_out_w).astype(BF)
    grad_packed_two = attention_back(packed_two, time_probs, time_grad_mixed, rows_dev)
    norm_pull = jax.vjp(layer_norm, hidden_one, gains[1], shifts[1])[1]
    grad_hidden, gain_two, shift_two = norm_pull(back_dot(grad_packed_two, time_in_w))
    grad_one_low = (grad_two + grad_hidden).astype(BF)

    sent = (
        grad_one_low.reshape(tm, halves, own_frames, cut, MODEL)
        .transpose(1, 0, 2, 3, 4)
        .reshape(halves * tm, own_frames, cut, MODEL)
    )
    space_branch = lax.all_to_all(sent, ("space", "tm"), 0, 1).reshape(rows_dev, MODEL)
    space_grad_mixed = back_dot(space_branch, space_out_w).astype(BF)
    ffn_out_grad, ffn_in_grad, time_qkv_grad, time_out_grad, grad_packed_one = reduce_products(
        (
            (act_low, grad_out_low),
            (normed_three, grad_pre_low),
            (normed_two, grad_packed_two),
            (time_mixed, time_branch),
        ),
        1,
        attend=(packed_one, space_probs, space_grad_mixed),
    )
    norm_pull = jax.vjp(layer_norm, hidden_zero, gains[0], shifts[0])[1]
    grad_hidden, gain_one, shift_one = norm_pull(back_dot(grad_packed_one, space_in_w))
    grad_zero = space_branch.astype(F32) + grad_hidden
    frame_grad = jnp.sum(grad_zero.reshape(own_frames, grid_all, MODEL), axis=1)
    action_grad = jnp.dot(one_hot.astype(F32).T, frame_grad, precision=lax.Precision.HIGHEST)
    input_grad = lax.all_to_all(
        grad_zero.astype(BF).reshape(own_frames, grid_all, MODEL), "space", 1, 0, tiled=True
    ).astype(F32)[None]

    by_row = jnp.concatenate(
        (
            action_grad,
            jnp.stack((gain_one, gain_two, gain_three, shift_one, shift_two, shift_three)),
            bias_out_grad[None],
        )
    )
    shares = jnp.concatenate(
        (
            by_row.reshape(lines, tm, width).transpose(1, 0, 2),
            bias_in_grad.reshape(tm, -1, width),
        ),
        axis=1,
    )
    space_out_grad, space_qkv_grad, small_grads = reduce_products(
        ((space_mixed, space_branch), (normed_one, grad_packed_one)), 2, small=shares
    )
    return (
        block_output,
        input_grad,
        small_grads[:ACTIONS],
        small_grads[ACTIONS : ACTIONS + 3],
        small_grads[ACTIONS + 3 : ACTIONS + 6],
        space_qkv_grad,
        space_out_grad,
        time_qkv_grad,
        time_out_grad,
        ffn_in_grad,
        small_grads[lines:].reshape(hidden_units),
        ffn_out_grad,
        small_grads[ACTIONS + 6],
    )


def solution(mesh):
    placed = (
        P("row", "tm", "space", None),
        P(None, "tm"),
        P(None, "tm"),
        P(None, "tm"),
        P("tm", None),
        P("tm", None),
        P("tm", None),
        P("tm", None),
        P("tm", None),
        P("tm"),
        P("tm", None),
        P("tm"),
        P("row", "tm", "space", None),
        P("row", None),
        P("row", "tm"),
    )
    return jax.shard_map(
        body,
        mesh=mesh,
        in_specs=placed,
        out_specs=(
            P("row", "tm", "space", None),
            P("row", "tm", "space", None),
            P(None, "tm"),
            P(None, "tm"),
            P(None, "tm"),
            P("tm", None),
            P("tm", None),
            P("tm", None),
            P("tm", None),
            P("tm", None),
            P("tm"),
            P("tm", None),
            P("tm"),
        ),
        check_vma=False,
    )
```

```python
import math

import jax
import jax.numpy as jnp
from jax import lax
from jax.experimental import pallas as pl
from jax.experimental.pallas import tpu as pltpu
from jax.sharding import PartitionSpec as P

MODEL = 1024
HEADS = 16
HEAD_DIM = 64
ACTIONS = 8
TILE = 256
PAIR = 2 * HEAD_DIM
PAIRS = HEADS // 2
SCALE = 1.0 / math.sqrt(HEAD_DIM)

EPSILON = 1e-05
NEG_FILL = -1e30
BF = jnp.bfloat16
F32 = jnp.float32


def layer_norm(values, gain_row, shift_row):
    row_mean = jnp.mean(values, axis=-1, keepdims=True)
    centred = values - row_mean
    spread = jnp.mean(centred * centred, axis=-1, keepdims=True)
    return centred * lax.rsqrt(spread + EPSILON) * gain_row + shift_row


def forward_dot(values, weight):
    return jnp.dot(values, weight, preferred_element_type=F32)


def weight_grad(left_rows, right_rows):
    return lax.dot_general(
        left_rows, right_rows, (((0,), (0,)), ((), ())), preferred_element_type=F32
    )


def back_dot(grad_rows, weight):
    return lax.dot_general(
        grad_rows, weight, (((1,), (1,)), ((), ())), preferred_element_type=F32
    )


def dot_nt(a, b):
    return lax.dot_general(a, b, (((1,), (1,)), ((), ())), preferred_element_type=F32)


def dot_nn(a, b):
    return lax.dot_general(a, b, (((1,), (0,)), ((), ())), preferred_element_type=F32)


def dot_tn(a, b):
    return lax.dot_general(a, b, (((0,), (0,)), ((), ())), preferred_element_type=F32)


def of_head(half, values):
    lane = lax.broadcasted_iota(jnp.int32, values.shape, 1)
    keep = (lane < HEAD_DIM) if half == 0 else (lane >= HEAD_DIM)
    return jnp.where(keep, values, jnp.zeros_like(values))


def join_heads(first, second):
    lane = lax.broadcasted_iota(jnp.int32, first.shape, 1)
    return jnp.where(lane < HEAD_DIM, first, second)


def pair_cols(pair, part):
    if isinstance(pair, int):
        return pl.ds(part * MODEL + pair * PAIR, PAIR)
    return pl.ds(pl.multiple_of(part * MODEL + pair * PAIR, PAIR), PAIR)


def start_swap(to_all, src_ref, dst_ref, sems, local_sem):
    me, size = lax.axis_index("tm"), sems.shape[0]
    whole, part = (dst_ref, src_ref) if to_all else (src_ref, dst_ref)
    frames, cut = part.shape[0], whole.shape[1]

    def some_frames(ref, device):
        return ref.at[pl.ds(pl.multiple_of(device * frames, frames), frames)]

    def some_places(ref, device):
        return ref.at[:, pl.ds(pl.multiple_of(device * cut, cut), cut), :]

    def ends(device):
        if to_all:
            return some_places(src_ref, device), some_frames(dst_ref, me)
        return some_frames(src_ref, device), some_places(dst_ref, me)

    barrier = pltpu.get_barrier_semaphore()
    for flip in range(1, size):
        pl.semaphore_signal(
            barrier, inc=1, device_id={"tm": me ^ flip}, device_id_type=pl.DeviceIdType.MESH
        )
    pl.semaphore_wait(barrier, size - 1)
    copies = []
    for flip in range(1, size):
        src, dst = ends(me ^ flip)
        copies.append(
            pltpu.make_async_remote_copy(
                src_ref=src,
                dst_ref=dst,
                send_sem=sems.at[flip, 0],
                recv_sem=sems.at[flip, 1],
                device_id={"tm": me ^ flip},
                device_id_type=pl.DeviceIdType.MESH,
            )
        )
    src, dst = ends(me)
    copies.append(pltpu.make_async_copy(src, dst, local_sem))
    for copy in copies:
        copy.start()
    return copies


def swap_plain(to_all, block):
    split, concat = (1, 0) if to_all else (0, 1)
    return lax.all_to_all(block, "tm", split, concat, tiled=True)


def swapped_shape(to_all, block, size):
    first, second, width = block.shape
    if to_all:
        return (first * size, second // size, width)
    return (first // size, second * size, width)


def attn_fwd_kernel(tiles, masked, packed_ref, *refs):
    if masked:
        col_ref, row_ref, mixed_ref, probs_ref = refs
    else:
        mixed_ref, probs_ref = refs

    def one_pair(pair, carry):
        for t in range(tiles):
            mine = pl.ds(t * TILE, TILE)
            width = (t + 1) * TILE
            seen = pl.ds(0, width)
            query = packed_ref[mine, pair_cols(pair, 0)] * jnp.asarray(SCALE, BF)
            key = packed_ref[seen, pair_cols(pair, 1)]
            value = packed_ref[seen, pair_cols(pair, 2)]
            if masked:
                same = col_ref[mine, :] == row_ref[:, seen]
                order = lax.broadcasted_iota(
                    jnp.int32, (TILE, width), 0
                ) + t * TILE >= lax.broadcasted_iota(jnp.int32, (TILE, width), 1)
                allowed = same & order
            outs = []
            for half in range(2):
                scores = dot_nt(of_head(half, query), key)
                if masked:
                    scores = jnp.where(allowed, scores, NEG_FILL)
                top = jnp.max(scores, axis=1, keepdims=True)
                raised = jnp.exp(scores - top)
                total = jnp.sum(raised, axis=1, keepdims=True)
                probs = (raised * (1.0 / total)).astype(BF)
                probs_ref[2 * pair + half, mine, seen] = probs
                outs.append(dot_nn(probs, value))
            mixed_ref[mine, pair_cols(pair, 0)] = join_heads(*outs).astype(BF)
        return carry

    lax.fori_loop(0, PAIRS, one_pair, 0, unroll=2)


def attn_bwd_tile(
    t, tiles, pair, packed_ref, probs_ref, grad_ref, out_ref, accs=None, base=0, probs_pair=None
):
    mine = pl.ds(base + t * TILE, TILE)
    seen = pl.ds(base, (t + 1) * TILE)
    query = packed_ref[mine, pair_cols(pair, 0)] * jnp.asarray(SCALE, BF)
    key = packed_ref[seen, pair_cols(pair, 1)]
    value = packed_ref[seen, pair_cols(pair, 2)]
    grad = grad_ref[mine, pair_cols(pair, 0)]
    dqs, dks, dvs = [], [], []
    for half in range(2):
        if probs_pair is None:
            probs_low = probs_ref[2 * pair + half, mine, pl.ds(0, (t + 1) * TILE)]
        else:
            probs_low = probs_pair[half]
        probs = probs_low.astype(F32)
        dprobs = dot_nt(of_head(half, grad), value)
        delta = jnp.sum(dprobs * probs, axis=1, keepdims=True)
        dscores = (probs * (dprobs - delta)).astype(BF)
        dqs.append(dot_nn(dscores, key))
        dks.append(dot_tn(dscores, query))
        dvs.append(dot_tn(probs_low, grad))
    out_ref[mine, pair_cols(pair, 0)] = (join_heads(*dqs) * SCALE).astype(BF)
    dkey, dvalue = join_heads(*dks), join_heads(*dvs)
    if tiles == 1:
        out_ref[seen, pair_cols(pair, 1)] = dkey.astype(BF)
        out_ref[seen, pair_cols(pair, 2)] = dvalue.astype(BF)
        return
    if t == tiles - 1:
        accs[0][...] = dkey
        accs[1][...] = dvalue
    else:
        accs[0][pl.ds(0, (t + 1) * TILE), :] += dkey
        accs[1][pl.ds(0, (t + 1) * TILE), :] += dvalue
    if t == 0:
        out_ref[:, pair_cols(pair, 1)] = accs[0][...].astype(BF)
        out_ref[:, pair_cols(pair, 2)] = accs[1][...].astype(BF)


def attn_bwd_kernel(tiles, swapped, packed_ref, probs_ref, grad_ref, *refs):
    copies = []
    if swapped:
        src_ref, out_ref, dst_ref, *accs, sems, local_sem = refs
        copies = start_swap(False, src_ref, dst_ref, sems, local_sem)
    else:
        out_ref, *accs = refs

    def one_pair(pair, carry):
        for t in reversed(range(tiles)):
            attn_bwd_tile(t, tiles, pair, packed_ref, probs_ref, grad_ref, out_ref, accs)
        return carry

    lax.fori_loop(0, PAIRS, one_pair, 0, unroll=2)
    for copy in copies:
        copy.wait()


def blocks(rows, span):
    return {
        "packed": pl.BlockSpec((span, 3 * MODEL), lambda t: (t, 0)),
        "mixed": pl.BlockSpec((span, MODEL), lambda t: (t, 0)),
        "probs": pl.BlockSpec((HEADS, span, span), lambda t: (0, t, 0)),
        "col": pl.BlockSpec((span, 1), lambda t: (t, 0)),
        "row": pl.BlockSpec((1, span), lambda t: (0, t)),
    }


def swap_parts(swap, to_all):
    if swap is None:
        return [], [], [], {}
    size = lax.axis_size("tm")
    dma = pltpu.SemaphoreType.DMA
    shape = swapped_shape(to_all, swap, size)
    return (
        [swap],
        [jax.ShapeDtypeStruct(shape, swap.dtype)],
        [dma((size, 2)), dma(())],
        {"collective_id": 4 + to_all, "has_side_effects": True},
    )


def attention(packed, span, groups=None):
    rows = packed.shape[0]
    at = blocks(rows, span)
    masked = groups is not None
    extra = (groups[:, None], groups[None, :]) if masked else ()
    specs = [at["packed"]] + ([at["col"], at["row"]] if masked else [])
    return pl.pallas_call(
        lambda *refs: attn_fwd_kernel(span // TILE, masked, *refs),
        grid=(rows // span,),
        in_specs=specs,
        out_specs=[at["mixed"], at["probs"]],
        out_shape=[
            jax.ShapeDtypeStruct((rows, MODEL), BF),
            jax.ShapeDtypeStruct((HEADS, rows, span), BF),
        ],
        compiler_params=pltpu.CompilerParams(vmem_limit_bytes=48 * 2**20),
        cost_estimate=pl.CostEstimate(
            flops=80 * HEADS * rows * span * HEAD_DIM,
            bytes_accessed=rows * (8 * MODEL + 2 * HEADS * span),
            transcendentals=HEADS * rows * span,
        ),
        name="attention_forward",
    )(packed, *extra)


def attention_back(packed, probs, grad, span, swap=None):
    rows = packed.shape[0]
    at = blocks(rows, span)
    apart = swap if swap is not None and lax.axis_size("tm") != 8 else None
    more, outs, scratch, parameters = swap_parts(None if apart is not None else swap, False)
    anywhere = pl.BlockSpec(memory_space=pl.ANY)
    result = pl.pallas_call(
        lambda *refs: attn_bwd_kernel(span // TILE, bool(more), *refs),
        grid=(rows // span,),
        in_specs=[at["packed"], at["probs"], at["mixed"]] + [anywhere] * len(more),
        out_specs=[at["packed"]] + [anywhere] * len(outs),
        out_shape=[jax.ShapeDtypeStruct((rows, 3 * MODEL), BF)] + outs,
        scratch_shapes=[pltpu.VMEM((span, PAIR), F32), pltpu.VMEM((span, PAIR), F32)] + scratch,
        compiler_params=pltpu.CompilerParams(vmem_limit_bytes=48 * 2**20, **parameters),
        cost_estimate=pl.CostEstimate(
            flops=90 * HEADS * rows * span * HEAD_DIM,
            bytes_accessed=rows * (14 * MODEL + 2 * HEADS * span),
            transcendentals=0,
        ),
        name="attention_backward",
    )(packed, probs, grad, *more)
    if apart is not None:
        return [*result, swap_plain(False, apart)]
    return result if swap is not None else result[0]


def back_norm_rows(grad, weight_ref, values, carried, gain):
    back = dot_nt(grad, weight_ref[...])
    centred = values - jnp.mean(values, axis=1, keepdims=True)
    spread = jnp.mean(centred * centred, axis=1, keepdims=True)
    scale = lax.rsqrt(spread + EPSILON)
    unit = centred * scale
    along = back * gain
    level = jnp.mean(along, axis=1, keepdims=True)
    slope = jnp.mean(along * unit, axis=1, keepdims=True)
    result = carried + scale * (along - level - unit * slope)
    sums = (jnp.sum(back * unit, axis=0, keepdims=True), jnp.sum(back, axis=0, keepdims=True))
    return result, sums


def back_norm_kernel(grad_ref, weight_ref, value_ref, carried_ref, gain_ref, out_ref, sum_ref):
    result, sums = back_norm_rows(
        grad_ref[...],
        weight_ref,
        value_ref[...].astype(F32),
        carried_ref[...].astype(F32),
        gain_ref[...],
    )
    out_ref[...] = result.astype(BF)

    @pl.when(pl.program_id(0) == 0)
    def _():
        sum_ref[...] = jnp.zeros_like(sum_ref)

    for i in range(2):
        sum_ref[i : i + 1, :] += sums[i]


def back_norm(grad, weight, values, carried, gain):
    rows, width = values.shape
    tile = min(rows, TILE)

    def by_rows(columns):
        return pl.BlockSpec((tile, columns), lambda i: (i, 0))

    def whole(*shape):
        return pl.BlockSpec(shape, lambda i: (0, 0))

    return pl.pallas_call(
        back_norm_kernel,
        grid=(rows // tile,),
        in_specs=[
            by_rows(grad.shape[1]),
            whole(*weight.shape),
            by_rows(width),
            by_rows(width),
            whole(1, width),
        ],
        out_specs=[by_rows(width), whole(2, width)],
        out_shape=[
            jax.ShapeDtypeStruct((rows, width), BF),
            jax.ShapeDtypeStruct((2, width), F32),
        ],
        compiler_params=pltpu.CompilerParams(vmem_limit_bytes=40 * 2**20),
        cost_estimate=pl.CostEstimate(
            flops=2 * rows * width * grad.shape[1],
            bytes_accessed=2 * grad.shape[1] * (rows + width),
            transcendentals=0,
        ),
        name="back_norm",
    )(grad, weight, values, carried, gain[None])


def act_kernel(normed_ref, weight_ref, bias_ref, act_ref, turned_ref, slope_ref):
    hidden = dot_nn(normed_ref[...], weight_ref[...]) + bias_ref[...]
    root, cubic = math.sqrt(2.0 / math.pi), 0.044715
    square = hidden * hidden
    tanh = jnp.tanh(root * hidden * (1.0 + cubic * square))
    half = 0.5 + 0.5 * tanh
    act = (hidden * half).astype(BF)
    act_ref[...] = act
    turned_ref[...] = act.T
    slope_ref[...] = (
        half + (0.5 * root) * hidden * (1.0 - tanh * tanh) * (1.0 + 3.0 * cubic * square)
    ).astype(BF)


def activate(normed, weight, bias):
    rows, units = normed.shape[0], weight.shape[1]
    tile = 512
    return pl.pallas_call(
        act_kernel,
        grid=(units // tile,),
        in_specs=[
            pl.BlockSpec(normed.shape, lambda j: (0, 0)),
            pl.BlockSpec((weight.shape[0], tile), lambda j: (0, j)),
            pl.BlockSpec((1, tile), lambda j: (0, j)),
        ],
        out_specs=[
            pl.BlockSpec((rows, tile), lambda j: (0, j)),
            pl.BlockSpec((tile, rows), lambda j: (j, 0)),
            pl.BlockSpec((rows, tile), lambda j: (0, j)),
        ],
        out_shape=[
            pltpu.HBM((rows, units), BF),
            pltpu.HBM((units, rows), BF),
            pltpu.HBM((rows, units), BF),
        ],
        compiler_params=pltpu.CompilerParams(vmem_limit_bytes=24 * 2**20),
        cost_estimate=pl.CostEstimate(
            flops=2 * rows * units * weight.shape[0],
            bytes_accessed=2 * units * (3 * rows + weight.shape[0]),
            transcendentals=rows * units,
        ),
        name="activate",
    )(normed, weight, bias[None])


def back_act_kernel(grad_ref, weight_ref, slope_ref, out_ref, sum_ref):
    back = (dot_nt(grad_ref[...], weight_ref[...]) * slope_ref[...].astype(F32)).astype(BF)
    out_ref[...] = back
    sum_ref[...] = jnp.sum(back.astype(F32), axis=0, keepdims=True)


def back_act(grad, weight, slope):
    rows, units = slope.shape
    tile = 512
    return pl.pallas_call(
        back_act_kernel,
        grid=(units // tile,),
        in_specs=[
            pl.BlockSpec(grad.shape, lambda j: (0, 0)),
            pl.BlockSpec((tile, grad.shape[1]), lambda j: (j, 0)),
            pl.BlockSpec((rows, tile), lambda j: (0, j)),
        ],
        out_specs=[
            pl.BlockSpec((rows, tile), lambda j: (0, j)),
            pl.BlockSpec((1, tile), lambda j: (0, j)),
        ],
        out_shape=[
            jax.ShapeDtypeStruct((rows, units), BF),
            jax.ShapeDtypeStruct((1, units), F32),
        ],
        compiler_params=pltpu.CompilerParams(vmem_limit_bytes=24 * 2**20),
        cost_estimate=pl.CostEstimate(
            flops=2 * rows * units * grad.shape[1],
            bytes_accessed=2 * units * (2 * rows + grad.shape[1]),
            transcendentals=0,
        ),
        name="back_act",
    )(grad, weight, slope)


def hop(block, axis, flip):
    size = lax.axis_size(axis)
    return lax.ppermute(block, axis, [(i, i ^ flip) for i in range(size)])


def add_low(one, other):
    return (one.astype(F32) + other.astype(F32)).astype(BF)


def lay_kernel(rows, places, splits, *refs):
    count, outs = len(places), len(splits)
    parts, whole = refs[:count], refs[count : count + outs]
    stage = refs[count + outs : 2 * count + outs]
    came, left = refs[-2:]
    me = lax.axis_index("tm")
    inward = [pltpu.make_async_copy(parts[i], stage[i], came.at[i]) for i in range(count)]
    for copy in inward:
        copy.start()
    outward = []
    for i, (flip, start) in enumerate(places):
        at = pl.multiple_of((me ^ flip) * rows + start, 32)
        inward[i].wait()
        first = 0
        for j, columns in enumerate(splits):
            outward.append(
                pltpu.make_async_copy(
                    stage[i].at[:, pl.ds(first, columns)],
                    whole[j].at[pl.ds(at, parts[i].shape[0]), :],
                    left.at[i, j],
                )
            )
            outward[-1].start()
            first += columns
    for copy in outward:
        copy.wait()


def first_hops(block):
    if lax.axis_size("tm") != 8:
        return None
    return hop(block, "tm", 2), hop(block, "tm", 4)


def second_hops(came):
    if came is None:
        return None
    half = came[0].shape[0] // 2
    return hop(came[0][:half], "tm", 4), hop(came[1][half:], "tm", 2)


def gather_rows(block, came, passed, splits):
    if came is None:
        whole = lax.all_gather(block, "tm", axis=0, tiled=True)
        return jnp.split(whole, [sum(splits[:i]) for i in range(1, len(splits))], axis=1)
    rows = block.shape[0]
    half = rows // 2
    by_two, by_four = came
    low_six, high_six = passed
    pieces = ((block, 0, 0), (by_two, 2, 0), (by_four, 4, 0), (low_six, 6, 0), (high_six, 6, half))
    parts, places = [], []
    for piece, flip, start in pieces:
        for core in range(2):
            parts.append(hop(piece, "tm", 1) if core else piece)
            places.append((flip + core, start))
    return pl.pallas_call(
        lambda *refs: lay_kernel(rows, places, splits, *refs),
        in_specs=[pl.BlockSpec(memory_space=pl.ANY)] * len(parts),
        out_specs=[pl.BlockSpec(memory_space=pltpu.HBM)] * len(splits),
        out_shape=[jax.ShapeDtypeStruct((8 * rows, n), block.dtype) for n in splits],
        scratch_shapes=[pltpu.VMEM(part.shape, part.dtype) for part in parts]
        + [
            pltpu.SemaphoreType.DMA((len(parts),)),
            pltpu.SemaphoreType.DMA((len(parts), len(splits))),
        ],
        compiler_params=pltpu.CompilerParams(vmem_limit_bytes=20 * 2**20),
        cost_estimate=pl.CostEstimate(
            flops=0, bytes_accessed=32 * rows * block.shape[1], transcendentals=0
        ),
        name="lay_rows",
    )(*parts)


def after(value, *others):
    return lax.optimization_barrier((value,) + others)[0]


def first_kernel(*refs):
    blocks, small_ref, tokens_ref = refs[:2], refs[2], refs[3]
    wholes, smalls_ref, frames_ref = refs[4:6], refs[6], refs[7]
    local, small_sem, frame_sem, near, far, core = refs[8:]
    me, side = lax.axis_index("tm"), lax.axis_index("space")
    rows = blocks[0].shape[0]
    half = rows // 2
    half_grid, own_frames = tokens_ref.shape[1], tokens_ref.shape[0] // 2

    barrier = pltpu.get_barrier_semaphore()
    for flip in range(1, 8):
        pl.semaphore_signal(
            barrier, inc=1, device_id={"tm": me ^ flip}, device_id_type=pl.DeviceIdType.MESH
        )
    pl.semaphore_signal(
        barrier, inc=1, device_id={"space": 1 - side}, device_id_type=pl.DeviceIdType.MESH
    )
    pl.semaphore_wait(barrier, 8)

    sent = []

    def send(src, dst, sems, device):
        copy = pltpu.make_async_remote_copy(
            src_ref=src,
            dst_ref=dst,
            send_sem=sems.at[0],
            recv_sem=sems.at[1],
            device_id=device,
            device_id_type=pl.DeviceIdType.MESH,
        )
        copy.start()
        sent.append(copy)
        return copy

    def place(w, flip, start, length):
        at = pl.multiple_of((me ^ flip) * rows + start, half)
        return wholes[w].at[pl.ds(at, length), :]

    arrived = {}
    for w in range(2):
        for number, (flip, start) in enumerate(((2, 0), (4, half), (2, half), (4, 0))):
            arrived[w, flip, start] = send(
                blocks[w].at[pl.ds(start, half), :],
                place(w, 0, start, half),
                near.at[w, number],
                {"tm": me ^ flip},
            )
    small_copies = [
        send(small_ref, smalls_ref.at[me], small_sem.at[flip], {"tm": me ^ flip})
        for flip in range(1, 8)
    ]
    columns = pl.ds(pl.multiple_of(side * half_grid, half_grid), half_grid)
    frame_copy = send(
        tokens_ref.at[pl.ds((1 - side) * own_frames, own_frames)],
        frames_ref.at[:, columns, :],
        frame_sem,
        {"space": 1 - side},
    )
    core_copies = [
        send(blocks[w], place(w, 0, 0, rows), core.at[w, 0], {"tm": me ^ 1}) for w in range(2)
    ]
    own = [
        pltpu.make_async_copy(small_ref, smalls_ref.at[me], local.at[0]),
        pltpu.make_async_copy(
            tokens_ref.at[pl.ds(side * own_frames, own_frames)],
            frames_ref.at[:, columns, :],
            local.at[1],
        ),
    ] + [pltpu.make_async_copy(blocks[w], place(w, 0, 0, rows), local.at[2 + w]) for w in range(2)]
    for copy in own:
        copy.start()
    for w in range(2):
        for number, (flip, start) in enumerate(((2, 0), (4, half), (2, half), (4, 0))):
            arrived[w, flip, start].wait_recv()
            block = place(w, flip, start, half)
            if number < 2:
                arrived[w, 6, start] = send(
                    block, block, far.at[w, number], {"tm": me ^ (6 - flip)}
                )
            core_copies.append(send(block, block, core.at[w, 1 + number], {"tm": me ^ 1}))
    for w in range(2):
        for number, start in enumerate((0, half)):
            arrived[w, 6, start].wait_recv()
            block = place(w, 6, start, half)
            core_copies.append(send(block, block, core.at[w, 5 + number], {"tm": me ^ 1}))
    for copy in small_copies + [frame_copy] + core_copies:
        copy.wait_recv()
    for copy in own:
        copy.wait()
    for copy in sent:
        copy.wait_send()


def first_gather(weights, small, tokens):
    if lax.axis_size("tm") != 8:
        return (
            *[lax.all_gather(weight, "tm", axis=0, tiled=True) for weight in weights],
            lax.all_gather(small, "tm", axis=0),
            lax.all_to_all(tokens, "space", 0, 1, tiled=True),
        )
    used = small.shape[0]
    small = jnp.pad(small, ((0, -used % 16), (0, 0)))
    frames, half_grid, model = tokens.shape
    dma = pltpu.SemaphoreType.DMA
    first, second, smalls, whole_frames = pl.pallas_call(
        first_kernel,
        in_specs=[pl.BlockSpec(memory_space=pltpu.VMEM)] * 4,
        out_specs=[pl.BlockSpec(memory_space=pltpu.HBM)] * 4,
        out_shape=[
            pltpu.HBM((8 * weight.shape[0], weight.shape[1]), weight.dtype) for weight in weights
        ]
        + [
            jax.ShapeDtypeStruct((8,) + small.shape, small.dtype),
            jax.ShapeDtypeStruct((frames // 2, 2 * half_grid, model), tokens.dtype),
        ],
        scratch_shapes=[
            dma((4,)),
            dma((8, 2)),
            dma((2,)),
            dma((2, 4, 2)),
            dma((2, 2, 2)),
            dma((2, 7, 2)),
        ],
        compiler_params=pltpu.CompilerParams(
            vmem_limit_bytes=16 * 2**20, collective_id=3, has_side_effects=True
        ),
        cost_estimate=pl.CostEstimate(flops=0, bytes_accessed=2**24, transcendentals=0),
        name="first_gather",
    )(*weights, small, tokens)
    return first, second, smalls[:, :used], whole_frames


UNIT = 128
WIDE = 256
ORDERS = ((3, 7, 1, 5), (5, 7, 1, 3), (2, 6, 0, 4), (4, 6, 0, 2))


OPERANDS = (
    "act_turned",
    "out_low",
    "normed_three",
    "grad_pre",
    "packed",
    "grad_mixed",
    "normed_two",
    "grad_packed_two",
    "time_mixed",
    "time_branch",
    "weight",
    "inputs",
    "branch",
    "space_mixed",
    "normed_one",
    "small",
)
SLOTS = 6
FINALS = 10
DELAYS = (0, 1, 3, 5, 7, 9, 11, 13)


def last_kernel(chunks, places, *refs):
    refs = list(refs)

    def take(count):
        taken = refs[:count]
        del refs[:count]
        return taken

    count = len(OPERANDS)
    far_off = dict(zip(OPERANDS, take(count)))
    probs_ref, embedded_ref, gain_ref, one_hot_ref = take(4)
    out_refs, small_out, frames_out = take(len(chunks)), take(1)[0], take(1)[0]
    near = dict(zip(OPERANDS, take(count)))
    (grad_packed, turned, lines, kept, probs_near) = take(5)
    (far, own, from_core, from_chip, from_owner, share, from_space, from_row, final) = take(9)
    (core_sem, chip_sem, owner_sem, space_sem, row_sem, back_sem, last_sem) = take(7)
    load_sem, probs_sem, frame_sem = take(3)
    me, side, level = lax.axis_index("tm"), lax.axis_index("space"), lax.axis_index("row")
    total = len(places)
    r = UNIT
    frames = grad_packed.shape[0] // TILE
    units = frames * PAIRS

    loads = {
        name: pltpu.make_async_copy(far_off[name], near[name], load_sem.at[i])
        for i, name in enumerate(OPERANDS)
    }
    for name in OPERANDS:
        loads[name].start()
    waited = set()

    def here(name):
        if name == "grad_packed_one":
            return grad_packed
        if name not in waited:
            waited.add(name)
            loads[name].wait()
        return near[name]

    def tm_at(flip):
        return {"tm": me ^ flip}

    barrier = pltpu.get_barrier_semaphore()
    for device in (tm_at(1), tm_at(2), tm_at(4), {"space": 1 - side}, {"row": 1 - level}):
        pl.semaphore_signal(barrier, inc=1, device_id=device, device_id_type=pl.DeviceIdType.MESH)
    pl.semaphore_wait(barrier, 5)

    def start(src, dst, sems, device):
        copy = pltpu.make_async_remote_copy(
            src_ref=src,
            dst_ref=dst,
            send_sem=sems.at[0],
            recv_sem=sems.at[1],
            device_id=device,
            device_id_type=pl.DeviceIdType.MESH,
        )
        copy.start()
        return copy

    cores, chips, owners, spaces, rows, backs, lasts = ({} for _ in range(7))

    def part(t, h, order):
        which, row, column, half = places[t]
        if which == len(chunks):
            return jnp.concatenate([lines[me ^ flip] for flip in order], axis=0)
        left, right = chunks[which]
        source = here(left) if left == "act_turned" else turned
        rows_each = source.shape[0] // 8
        picked = [
            source[pl.ds(pl.multiple_of((me ^ flip) * rows_each + row, r), r), :] for flip in order
        ]
        return dot_nn(
            jnp.concatenate(picked, axis=0), here(right)[:, pl.ds(column + h * half, WIDE)]
        )

    def stage_core(t):
        which, slot = places[t][0], t % SLOTS
        if which < len(chunks) and (t == 0 or places[t - 1][0] != which):
            if chunks[which][0] != "act_turned":
                turned[...] = here(chunks[which][0])[...].T
        for h in range(2):
            if t >= SLOTS:
                cores[t - SLOTS, h].wait_send()
            far[slot, h] = part(t, h, ORDERS[h]).astype(BF)
            cores[t, h] = start(
                far.at[slot, h], from_core.at[slot, h], core_sem.at[slot, h], tm_at(1)
            )
        for h in range(2):
            if t >= SLOTS:
                chips[t - SLOTS, h].wait_send()
                owners[t - SLOTS, h].wait_send()
            own[slot, h] = part(t, h, ORDERS[2 + h]).astype(BF)

    def stage_chip(t):
        slot = t % SLOTS
        for h in range(2):
            cores[t, h].wait_recv()
            own[slot, h] = add_low(own[slot, h], from_core[slot, h])
            chips[t, h] = start(
                own.at[slot, h, pl.ds(0, 2 * r)],
                from_chip.at[slot, h],
                chip_sem.at[slot, h],
                tm_at(4 if h else 2),
            )

    def stage_owner(t):
        slot = t % SLOTS
        for h in range(2):
            chips[t, h].wait_recv()
            own[slot, h, pl.ds(2 * r, 2 * r)] = add_low(
                own[slot, h, pl.ds(2 * r, 2 * r)], from_chip[slot, h]
            )
            owners[t, h] = start(
                own.at[slot, h, pl.ds(3 * r, r)],
                from_owner.at[slot, h],
                owner_sem.at[slot, h],
                tm_at(2 if h else 4),
            )

    def stage_space(t):
        slot = t % SLOTS
        if t >= SLOTS:
            spaces[t - SLOTS].wait_send()
            rows[t - SLOTS].wait_send()
        for h in range(2):
            owners[t, h].wait_recv()
            share[slot, h] = add_low(own[slot, h, pl.ds(2 * r, r)], from_owner[slot, h])
        spaces[t] = start(
            share.at[slot, 1 - side], from_space.at[slot], space_sem.at[slot], {"space": 1 - side}
        )

    def stage_row(t):
        slot = t % SLOTS
        spaces[t].wait_recv()
        share[slot, side] = add_low(share[slot, side], from_space[slot])
        other = pl.multiple_of((1 - level) * (r // 2), r // 2)
        rows[t] = start(
            share.at[slot, side, pl.ds(other, r // 2)],
            from_row.at[slot],
            row_sem.at[slot],
            {"row": 1 - level},
        )

    def stage_back(t):
        slot = t % SLOTS
        rows[t].wait_recv()
        mine = pl.ds(pl.multiple_of(level * (r // 2), r // 2), r // 2)
        last = t % FINALS
        final[last, side, mine] = add_low(share[slot, side, mine], from_row[slot])
        place = final.at[last, side, mine]
        backs[t] = start(place, place, back_sem.at[last], {"row": 1 - level})

    def stage_last(t):
        slot = t % FINALS
        backs[t].wait_recv()
        place = final.at[slot, side]
        lasts[t] = start(place, place, last_sem.at[slot], {"space": 1 - side})

    def stage_out(t):
        slot = t % FINALS
        lasts[t].wait_recv()
        out, row, column, half = places[t]
        if out == len(chunks):
            small_out[...] = final[slot, 0].astype(F32)
        else:
            for h in range(2):
                out_refs[out][pl.ds(row, r), pl.ds(column + h * half, WIDE)] = final[slot, h]
        backs[t].wait_send()
        lasts[t].wait_send()

    def probs_copy(unit):
        frame, pair = divmod(unit, PAIRS)
        return pltpu.make_async_copy(
            probs_ref.at[pl.ds(2 * pair, 2), pl.ds(frame * TILE, TILE), :],
            probs_near.at[unit % 2],
            probs_sem.at[unit % 2],
        )

    def attend(unit):
        frame, pair = divmod(unit, PAIRS)
        if unit + 1 < units:
            probs_copy(unit + 1).start()
        probs_copy(unit).wait()
        attn_bwd_tile(
            0,
            1,
            pair,
            here("packed"),
            None,
            here("grad_mixed"),
            grad_packed,
            base=frame * TILE,
            probs_pair=[probs_near[unit % 2, half] for half in range(2)],
        )

    def back_frame(frame):
        some = pl.ds(frame * TILE, TILE)
        values = here("inputs")[some, :].astype(F32) + embedded_ref[pl.ds(frame, 1), :]
        result, sums = back_norm_rows(
            grad_packed[some, :],
            here("weight"),
            values,
            here("branch")[some, :].astype(F32),
            gain_ref[...],
        )
        kept[frame] = result.astype(BF)
        column = jnp.sum(result, axis=0, keepdims=True)
        table = one_hot_ref[pl.ds(frame * ACTIONS, ACTIONS), :] * column
        width = MODEL // 8
        if frame == 0:
            lines[...] = here("small")[...]
        for k in range(8):
            at = slice(k * width, (k + 1) * width)
            lines[k, 0:ACTIONS, 0:width] += table[:, at]
            lines[k, ACTIONS : ACTIONS + 1, 0:width] += sums[0][:, at]
            lines[k, ACTIONS + 3 : ACTIONS + 4, 0:width] += sums[1][:, at]

    exchanged = []

    def exchange():
        half_grid = kept.shape[1] // 2
        own_frames = pl.ds(pl.multiple_of(side * frames, frames), frames)

        def columns(which):
            return pl.ds(pl.multiple_of(which * half_grid, half_grid), half_grid)

        exchanged.append(
            start(
                kept.at[:, columns(1 - side), :],
                frames_out.at[own_frames],
                frame_sem,
                {"space": 1 - side},
            )
        )
        frames_out[own_frames] = kept[:, columns(side), :]

    stages = (
        stage_core,
        stage_chip,
        stage_owner,
        stage_space,
        stage_row,
        stage_back,
        stage_last,
        stage_out,
    )
    probs_copy(0).start()
    for step in range(total + DELAYS[-1]):
        for delay, stage in zip(DELAYS, stages):
            if 0 <= step - delay < total:
                stage(step - delay)
        if 0 < step <= units:
            attend(step - 1)
        elif 0 <= step - 1 - units < frames:
            back_frame(step - 1 - units)
        elif step == 1 + units + frames:
            exchange()
    for t in range(max(0, total - SLOTS), total):
        for h in range(2):
            cores[t, h].wait_send()
            chips[t, h].wait_send()
            owners[t, h].wait_send()
        spaces[t].wait_send()
        rows[t].wait_send()
    exchanged[0].wait()


CHUNKS = (
    ("act_turned", "out_low"),
    ("normed_three", "grad_pre"),
    ("normed_two", "grad_packed_two"),
    ("time_mixed", "time_branch"),
    ("space_mixed", "branch"),
    ("normed_one", "grad_packed_one"),
)


def last_stage(given, probs, embedded, gain, one_hot):
    places, shapes = [], []
    for which, (left, right) in enumerate(CHUNKS):
        width = given[left].shape[0 if left == "act_turned" else 1]
        columns = 3 * MODEL if right == "grad_packed_one" else given[right].shape[1]
        shapes.append((width // 8, columns))
        for sub in range(width // (8 * UNIT)):
            for j in range(columns // 2 // WIDE):
                places.append((which, sub * UNIT, j * WIDE, columns // 2))
    places.append((len(CHUNKS), 0, 0, 0))
    small = given["small"]
    padding = ((0, 0), (0, UNIT - small.shape[1]), (0, WIDE - small.shape[2]))
    given = dict(given, small=jnp.pad(small, padding))
    tokens = given["packed"].shape[0]
    frames = tokens // TILE
    vmem = pltpu.VMEM
    dma = pltpu.SemaphoreType.DMA
    in_vmem, anywhere = pl.BlockSpec(memory_space=pltpu.VMEM), pl.BlockSpec(memory_space=pl.ANY)
    result = pl.pallas_call(
        lambda *refs: last_kernel(CHUNKS, places, *refs),
        in_specs=[anywhere] * (len(OPERANDS) + 1) + [in_vmem] * 3,
        out_specs=[in_vmem] * (len(shapes) + 2),
        out_shape=[jax.ShapeDtypeStruct(shape, BF) for shape in shapes]
        + [
            jax.ShapeDtypeStruct((UNIT, WIDE), F32),
            jax.ShapeDtypeStruct((2 * frames, TILE // 2, MODEL), BF),
        ],
        scratch_shapes=[vmem(given[name].shape, given[name].dtype) for name in OPERANDS]
        + [
            vmem((tokens, 3 * MODEL), BF),
            vmem((MODEL, tokens), BF),
            vmem((8, UNIT, WIDE), F32),
            vmem((frames, TILE, MODEL), BF),
            vmem((2, 2, TILE, TILE), BF),
            vmem((SLOTS, 2, 4 * UNIT, WIDE), BF),
            vmem((SLOTS, 2, 4 * UNIT, WIDE), BF),
            vmem((SLOTS, 2, 4 * UNIT, WIDE), BF),
            vmem((SLOTS, 2, 2 * UNIT, WIDE), BF),
            vmem((SLOTS, 2, UNIT, WIDE), BF),
            vmem((SLOTS, 2, UNIT, WIDE), BF),
            vmem((SLOTS, UNIT, WIDE), BF),
            vmem((SLOTS, UNIT // 2, WIDE), BF),
            vmem((FINALS, 2, UNIT, WIDE), BF),
            dma((SLOTS, 2, 2)),
            dma((SLOTS, 2, 2)),
            dma((SLOTS, 2, 2)),
            dma((SLOTS, 2)),
            dma((SLOTS, 2)),
            dma((FINALS, 2)),
            dma((FINALS, 2)),
            dma((len(OPERANDS),)),
            dma((2,)),
            dma((2,)),
        ],
        compiler_params=pltpu.CompilerParams(
            vmem_limit_bytes=60 * 2**20, collective_id=1, has_side_effects=True
        ),
        cost_estimate=pl.CostEstimate(
            flops=1024, bytes_accessed=len(places) * 8 * UNIT * WIDE, transcendentals=0
        ),
        name="last_stage",
    )(*[given[name] for name in OPERANDS], probs, embedded, gain[None], one_hot)
    grads = [grad.astype(F32) for grad in result[: len(shapes)]]
    return grads, result[-2][: small.shape[1], : small.shape[2]], result[-1]


def last_stage_plain(given, probs, embedded, gain, one_hot):
    tokens = given["packed"].shape[0]
    frames = tokens // TILE
    grad_packed = attention_back(given["packed"], probs, given["grad_mixed"], TILE)
    values = given["inputs"].astype(F32) + jnp.repeat(embedded, TILE, axis=0)
    result, sums = back_norm(grad_packed, given["weight"], values, given["branch"], gain)
    given = dict(given, grad_packed_one=grad_packed, act_turned=given["act_turned"].T)
    grads = []
    for left, right in CHUNKS:
        whole = weight_grad(given[left], given[right]).astype(BF)
        block = lax.psum_scatter(whole, "tm", scatter_dimension=0, tiled=True)
        grads.append(lax.psum(block, ("row", "space")).astype(F32))
    by_frame = jnp.sum(result.reshape(frames, TILE, MODEL).astype(F32), axis=1)
    table = jnp.dot(
        one_hot.reshape(frames, ACTIONS).T, by_frame, precision=lax.Precision.HIGHEST
    )
    none = jnp.zeros((2, MODEL), F32)
    rows = jnp.concatenate((table, sums[:1], none, sums[1:], none))
    size = lax.axis_size("tm")
    more = rows.reshape(-1, size, MODEL // size).transpose(1, 0, 2)
    small = given["small"].at[:, : more.shape[1]].add(more)
    block = lax.psum_scatter(small, "tm", scatter_dimension=0, tiled=True)[0]
    exchanged = lax.all_to_all(
        result.reshape(frames, TILE, MODEL), "space", 1, 0, tiled=True
    )
    return grads, lax.psum(block, ("row", "space")), exchanged


def body(
    block_input,
    action_table,
    norm_gain,
    norm_bias,
    space_qkv,
    space_out,
    time_qkv,
    time_out,
    ffn_in,
    ffn_bias_in,
    ffn_out,
    ffn_bias_out,
    out_grad,
    frame_segment,
    frame_action,
):
    tm, halves = lax.axis_size("tm"), lax.axis_size("space")
    slot, side = lax.axis_index("tm"), lax.axis_index("space")
    frame_count, half_grid = block_input.shape[1], block_input.shape[2]
    own_frames = frame_count // halves
    grid_all = half_grid * halves
    cut = half_grid // tm
    all_frames = frame_count * tm
    rows_dev = frame_count * half_grid
    width = MODEL // tm
    hidden_units = ffn_bias_in.shape[0]

    space_in_w, space_out_w, small, inputs = first_gather(
        (space_qkv, space_out),
        jnp.concatenate(
            [a.reshape(-1, width) for a in (action_table, norm_gain, norm_bias)]
            + [ffn_bias_out.reshape(1, width), ffn_bias_in.reshape(-1, width)]
        ),
        block_input[0],
    )
    lines = ACTIONS + 7
    by_row = small[:, :lines].transpose(1, 0, 2).reshape(lines, MODEL)
    table_full = by_row[:ACTIONS]
    gains = by_row[ACTIONS : ACTIONS + 3].astype(F32)
    shifts = by_row[ACTIONS + 3 : ACTIONS + 6].astype(F32)
    bias_out = by_row[ACTIONS + 6].astype(F32)
    bias_in = small[:, lines:].reshape(-1).astype(F32)

    actions = lax.dynamic_slice(frame_action[0], (side * own_frames,), (own_frames,))
    one_hot = (actions[:, None] == jnp.arange(ACTIONS)[None, :]).astype(BF)
    embedded = forward_dot(one_hot, table_full)

    time_block = jnp.concatenate((time_qkv, time_out), axis=1)
    if tm == 8:
        time_block = after(time_block, space_out_w)
    time_came = first_hops(time_block)

    hidden_zero = (inputs.astype(F32) + embedded[:, None, :]).reshape(rows_dev, MODEL)
    normed_one = layer_norm(hidden_zero, gains[0], shifts[0]).astype(BF)
    packed_one = forward_dot(normed_one, space_in_w).astype(BF)
    space_mixed, space_probs = attention(packed_one, grid_all)
    if tm == 8:
        space_mixed, *time_came = lax.optimization_barrier((space_mixed, *time_came))
    time_passed = second_hops(time_came)
    time_in_w, time_out_w = gather_rows(time_block, time_came, time_passed, (3 * MODEL, MODEL))
    in_block = after(ffn_in, *time_passed) if tm == 8 else ffn_in
    in_came = first_hops(in_block)
    hidden_one_own = (hidden_zero + forward_dot(space_mixed, space_out_w)).astype(BF)

    sent = hidden_one_own.reshape(own_frames, halves * tm, cut, MODEL)
    blocks_t = lax.all_to_all(sent, ("space", "tm"), 1, 0)
    hidden_one_low = lax.optimization_barrier(
        blocks_t.reshape(halves, tm, own_frames, cut, MODEL)
        .transpose(1, 0, 2, 3, 4)
        .reshape(rows_dev, MODEL)
    )
    hidden_one = hidden_one_low.astype(F32)
    groups = (
        frame_segment[0].astype(jnp.int32)[:, None] * cut + jnp.arange(cut, dtype=jnp.int32)
    ).reshape(rows_dev)

    normed_two = layer_norm(hidden_one, gains[1], shifts[1]).astype(BF)
    packed_two = forward_dot(normed_two, time_in_w).astype(BF)
    if tm == 8:
        packed_two, out_grad, *in_came = lax.optimization_barrier(
            (packed_two, out_grad, *in_came)
        )
    in_passed = second_hops(in_came)
    grad_out_low = swap_plain(True, out_grad[0])
    time_mixed, time_probs = attention(packed_two, rows_dev, groups)
    out_block = ffn_out
    if tm == 8:
        time_mixed, grad_out_low, out_block, *in_passed = lax.optimization_barrier(
            (time_mixed, grad_out_low, ffn_out, *in_passed)
        )
    grad_out_low = grad_out_low.reshape(rows_dev, MODEL)
    grad_out = grad_out_low.astype(F32)
    out_came = first_hops(out_block)
    (ffn_in_w,) = gather_rows(in_block, in_came, in_passed, (ffn_in.shape[1],))
    hidden_two = hidden_one + forward_dot(time_mixed, time_out_w)
    normed_three = layer_norm(hidden_two, gains[2], shifts[2]).astype(BF)
    act_low, act_turned, slope = activate(normed_three, ffn_in_w, bias_in)
    if tm == 8:
        slope, *out_came = lax.optimization_barrier((slope, *out_came))
    (ffn_out_w,) = gather_rows(out_block, out_came, second_hops(out_came), (MODEL,))
    bias_out_grad = jnp.sum(grad_out, axis=0)
    grad_pre_low, bias_in_grad = back_act(grad_out_low, ffn_out_w, slope)
    bias_in_grad = bias_in_grad[0]
    time_branch, sums_three = back_norm(
        grad_pre_low, ffn_in_w, hidden_two, grad_out_low, gains[2]
    )
    time_grad_mixed = back_dot(time_branch, time_out_w).astype(BF)
    block_out = (hidden_two + forward_dot(act_low, ffn_out_w) + bias_out).astype(BF)
    grad_packed_two, block_output = attention_back(
        packed_two,
        time_probs,
        time_grad_mixed,
        rows_dev,
        swap=block_out.reshape(all_frames, cut, MODEL),
    )
    block_output = block_output[None]
    grad_one_low, sums_two = back_norm(
        grad_packed_two, time_in_w, hidden_one_low, time_branch, gains[1]
    )

    sent = (
        grad_one_low.reshape(tm, halves, own_frames, cut, MODEL)
        .transpose(1, 0, 2, 3, 4)
        .reshape(halves * tm, own_frames, cut, MODEL)
    )
    space_branch = lax.all_to_all(sent, ("space", "tm"), 0, 1).reshape(rows_dev, MODEL)
    space_grad_mixed = back_dot(space_branch, space_out_w).astype(BF)
    none = jnp.zeros((1, MODEL), F32)
    by_row = jnp.concatenate(
        [jnp.zeros((ACTIONS, MODEL), F32)]
        + [
            row
            for i in range(2)
            for row in (none, sums_two[i : i + 1], sums_three[i : i + 1])
        ]
        + [bias_out_grad[None]]
    )
    shares = jnp.concatenate(
        (
            by_row.reshape(lines, tm, width).transpose(1, 0, 2),
            bias_in_grad.reshape(tm, -1, width),
        ),
        axis=1,
    )
    given = {
        "act_turned": act_turned,
        "out_low": grad_out_low,
        "normed_three": normed_three,
        "grad_pre": grad_pre_low,
        "packed": packed_one,
        "grad_mixed": space_grad_mixed,
        "normed_two": normed_two,
        "grad_packed_two": grad_packed_two,
        "time_mixed": time_mixed,
        "time_branch": time_branch,
        "weight": space_in_w,
        "inputs": inputs.reshape(rows_dev, MODEL),
        "branch": space_branch,
        "space_mixed": space_mixed,
        "normed_one": normed_one,
        "small": shares,
    }
    finish = last_stage if tm == 8 else last_stage_plain
    grads, small_grads, frames_grad = finish(
        given, space_probs, embedded, gains[0], one_hot.astype(F32).reshape(-1, 1)
    )
    ffn_out_grad, ffn_in_grad, time_qkv_grad, time_out_grad, space_out_grad, space_qkv_grad = grads
    input_grad = frames_grad.astype(F32)[None]
    return (
        block_output,
        input_grad,
        small_grads[:ACTIONS],
        small_grads[ACTIONS : ACTIONS + 3],
        small_grads[ACTIONS + 3 : ACTIONS + 6],
        space_qkv_grad,
        space_out_grad,
        time_qkv_grad,
        time_out_grad,
        ffn_in_grad,
        small_grads[lines:].reshape(hidden_units),
        ffn_out_grad,
        small_grads[ACTIONS + 6],
    )


def solution(mesh):
    placed = (
        P("row", "tm", "space", None),
        P(None, "tm"),
        P(None, "tm"),
        P(None, "tm"),
        P("tm", None),
        P("tm", None),
        P("tm", None),
        P("tm", None),
        P("tm", None),
        P("tm"),
        P("tm", None),
        P("tm"),
        P("row", "tm", "space", None),
        P("row", None),
        P("row", "tm"),
    )
    return jax.shard_map(
        body,
        mesh=mesh,
        in_specs=placed,
        out_specs=(
            P("row", "tm", "space", None),
            P("row", "tm", "space", None),
            P(None, "tm"),
            P(None, "tm"),
            P(None, "tm"),
            P("tm", None),
            P("tm", None),
            P("tm", None),
            P("tm", None),
            P("tm", None),
            P("tm"),
            P("tm", None),
            P("tm"),
        ),
        check_vma=False,
    )
```

```python
import math

import jax
import jax.numpy as jnp
from jax import lax
from jax.experimental import pallas as pl
from jax.experimental.pallas import tpu as pltpu
from jax.sharding import PartitionSpec as P

MODEL = 1024
HEADS = 16
HEAD_DIM = 64
ACTIONS = 8
TILE = 256
PAIR = 2 * HEAD_DIM
PAIRS = HEADS // 2
SCALE = 1.0 / math.sqrt(HEAD_DIM)

EPSILON = 1e-05
NEG_FILL = -1e30
BF = jnp.bfloat16
F32 = jnp.float32


def layer_norm(values, gain_row, shift_row):
    row_mean = jnp.mean(values, axis=-1, keepdims=True)
    centred = values - row_mean
    spread = jnp.mean(centred * centred, axis=-1, keepdims=True)
    return centred * lax.rsqrt(spread + EPSILON) * gain_row + shift_row


def forward_dot(values, weight):
    return jnp.dot(values, weight, preferred_element_type=F32)


def weight_grad(left_rows, right_rows):
    return lax.dot_general(
        left_rows, right_rows, (((0,), (0,)), ((), ())), preferred_element_type=F32
    )


def back_dot(grad_rows, weight):
    return lax.dot_general(
        grad_rows, weight, (((1,), (1,)), ((), ())), preferred_element_type=F32
    )


def dot_nt(a, b):
    return lax.dot_general(a, b, (((1,), (1,)), ((), ())), preferred_element_type=F32)


def dot_nn(a, b):
    return lax.dot_general(a, b, (((1,), (0,)), ((), ())), preferred_element_type=F32)


def dot_tn(a, b):
    return lax.dot_general(a, b, (((0,), (0,)), ((), ())), preferred_element_type=F32)


def of_head(half, values):
    lane = lax.broadcasted_iota(jnp.int32, values.shape, 1)
    keep = (lane < HEAD_DIM) if half == 0 else (lane >= HEAD_DIM)
    return jnp.where(keep, values, jnp.zeros_like(values))


def join_heads(first, second):
    lane = lax.broadcasted_iota(jnp.int32, first.shape, 1)
    return jnp.where(lane < HEAD_DIM, first, second)


def pair_cols(pair, part):
    if isinstance(pair, int):
        return pl.ds(part * MODEL + pair * PAIR, PAIR)
    return pl.ds(pl.multiple_of(part * MODEL + pair * PAIR, PAIR), PAIR)


def start_swap(to_all, src_ref, dst_ref, sems, local_sem):
    me, size = lax.axis_index("tm"), sems.shape[0]
    whole, part = (dst_ref, src_ref) if to_all else (src_ref, dst_ref)
    frames, cut = part.shape[0], whole.shape[1]

    def some_frames(ref, device):
        return ref.at[pl.ds(pl.multiple_of(device * frames, frames), frames)]

    def some_places(ref, device):
        return ref.at[:, pl.ds(pl.multiple_of(device * cut, cut), cut), :]

    def ends(device):
        if to_all:
            return some_places(src_ref, device), some_frames(dst_ref, me)
        return some_frames(src_ref, device), some_places(dst_ref, me)

    barrier = pltpu.get_barrier_semaphore()
    for flip in range(1, size):
        pl.semaphore_signal(
            barrier, inc=1, device_id={"tm": me ^ flip}, device_id_type=pl.DeviceIdType.MESH
        )
    pl.semaphore_wait(barrier, size - 1)
    copies = []
    for flip in range(1, size):
        src, dst = ends(me ^ flip)
        copies.append(
            pltpu.make_async_remote_copy(
                src_ref=src,
                dst_ref=dst,
                send_sem=sems.at[flip, 0],
                recv_sem=sems.at[flip, 1],
                device_id={"tm": me ^ flip},
                device_id_type=pl.DeviceIdType.MESH,
            )
        )
    src, dst = ends(me)
    copies.append(pltpu.make_async_copy(src, dst, local_sem))
    for copy in copies:
        copy.start()
    return copies


def swap_plain(to_all, block):
    split, concat = (1, 0) if to_all else (0, 1)
    return lax.all_to_all(block, "tm", split, concat, tiled=True)


def swapped_shape(to_all, block, size):
    first, second, width = block.shape
    if to_all:
        return (first * size, second // size, width)
    return (first // size, second * size, width)


def attn_fwd_kernel(tiles, masked, packed_ref, *refs):
    if masked:
        col_ref, row_ref, mixed_ref, probs_ref = refs
    else:
        mixed_ref, probs_ref = refs

    def one_pair(pair, carry):
        for t in range(tiles):
            mine = pl.ds(t * TILE, TILE)
            width = (t + 1) * TILE
            seen = pl.ds(0, width)
            query = packed_ref[mine, pair_cols(pair, 0)] * jnp.asarray(SCALE, BF)
            key = packed_ref[seen, pair_cols(pair, 1)]
            value = packed_ref[seen, pair_cols(pair, 2)]
            if masked:
                same = col_ref[mine, :] == row_ref[:, seen]
                order = lax.broadcasted_iota(
                    jnp.int32, (TILE, width), 0
                ) + t * TILE >= lax.broadcasted_iota(jnp.int32, (TILE, width), 1)
                allowed = same & order
            outs = []
            for half in range(2):
                scores = dot_nt(of_head(half, query), key)
                if masked:
                    scores = jnp.where(allowed, scores, NEG_FILL)
                top = jnp.max(scores, axis=1, keepdims=True)
                raised = jnp.exp(scores - top)
                total = jnp.sum(raised, axis=1, keepdims=True)
                probs = (raised * (1.0 / total)).astype(BF)
                probs_ref[2 * pair + half, mine, seen] = probs
                outs.append(dot_nn(probs, value))
            mixed_ref[mine, pair_cols(pair, 0)] = join_heads(*outs).astype(BF)
        return carry

    lax.fori_loop(0, PAIRS, one_pair, 0, unroll=2)


def attn_bwd_tile(
    t, tiles, pair, packed_ref, probs_ref, grad_ref, out_ref, accs=None, base=0, probs_pair=None
):
    mine = pl.ds(base + t * TILE, TILE)
    seen = pl.ds(base, (t + 1) * TILE)
    query = packed_ref[mine, pair_cols(pair, 0)] * jnp.asarray(SCALE, BF)
    key = packed_ref[seen, pair_cols(pair, 1)]
    value = packed_ref[seen, pair_cols(pair, 2)]
    grad = grad_ref[mine, pair_cols(pair, 0)]
    dqs, dks, dvs = [], [], []
    for half in range(2):
        if probs_pair is None:
            probs_low = probs_ref[2 * pair + half, mine, pl.ds(0, (t + 1) * TILE)]
        else:
            probs_low = probs_pair[half]
        probs = probs_low.astype(F32)
        dprobs = dot_nt(of_head(half, grad), value)
        delta = jnp.sum(dprobs * probs, axis=1, keepdims=True)
        dscores = (probs * (dprobs - delta)).astype(BF)
        dqs.append(dot_nn(dscores, key))
        dks.append(dot_tn(dscores, query))
        dvs.append(dot_tn(probs_low, grad))
    out_ref[mine, pair_cols(pair, 0)] = (join_heads(*dqs) * SCALE).astype(BF)
    dkey, dvalue = join_heads(*dks), join_heads(*dvs)
    if tiles == 1:
        out_ref[seen, pair_cols(pair, 1)] = dkey.astype(BF)
        out_ref[seen, pair_cols(pair, 2)] = dvalue.astype(BF)
        return
    if t == tiles - 1:
        accs[0][...] = dkey
        accs[1][...] = dvalue
    else:
        accs[0][pl.ds(0, (t + 1) * TILE), :] += dkey
        accs[1][pl.ds(0, (t + 1) * TILE), :] += dvalue
    if t == 0:
        out_ref[:, pair_cols(pair, 1)] = accs[0][...].astype(BF)
        out_ref[:, pair_cols(pair, 2)] = accs[1][...].astype(BF)


def attn_bwd_kernel(tiles, swapped, packed_ref, probs_ref, grad_ref, *refs):
    copies = []
    if swapped:
        src_ref, out_ref, dst_ref, *accs, sems, local_sem = refs
        copies = start_swap(False, src_ref, dst_ref, sems, local_sem)
    else:
        out_ref, *accs = refs

    def one_pair(pair, carry):
        for t in reversed(range(tiles)):
            attn_bwd_tile(t, tiles, pair, packed_ref, probs_ref, grad_ref, out_ref, accs)
        return carry

    lax.fori_loop(0, PAIRS, one_pair, 0, unroll=2)
    for copy in copies:
        copy.wait()


def blocks(rows, span):
    return {
        "packed": pl.BlockSpec((span, 3 * MODEL), lambda t: (t, 0)),
        "mixed": pl.BlockSpec((span, MODEL), lambda t: (t, 0)),
        "probs": pl.BlockSpec((HEADS, span, span), lambda t: (0, t, 0)),
        "col": pl.BlockSpec((span, 1), lambda t: (t, 0)),
        "row": pl.BlockSpec((1, span), lambda t: (0, t)),
    }


def swap_parts(swap, to_all):
    if swap is None:
        return [], [], [], {}
    size = lax.axis_size("tm")
    dma = pltpu.SemaphoreType.DMA
    shape = swapped_shape(to_all, swap, size)
    return (
        [swap],
        [jax.ShapeDtypeStruct(shape, swap.dtype)],
        [dma((size, 2)), dma(())],
        {"collective_id": 4 + to_all, "has_side_effects": True},
    )


def attention(packed, span, groups=None):
    rows = packed.shape[0]
    at = blocks(rows, span)
    masked = groups is not None
    extra = (groups[:, None], groups[None, :]) if masked else ()
    specs = [at["packed"]] + ([at["col"], at["row"]] if masked else [])
    return pl.pallas_call(
        lambda *refs: attn_fwd_kernel(span // TILE, masked, *refs),
        grid=(rows // span,),
        in_specs=specs,
        out_specs=[at["mixed"], at["probs"]],
        out_shape=[
            jax.ShapeDtypeStruct((rows, MODEL), BF),
            jax.ShapeDtypeStruct((HEADS, rows, span), BF),
        ],
        compiler_params=pltpu.CompilerParams(vmem_limit_bytes=48 * 2**20),
        cost_estimate=pl.CostEstimate(
            flops=80 * HEADS * rows * span * HEAD_DIM,
            bytes_accessed=rows * (8 * MODEL + 2 * HEADS * span),
            transcendentals=HEADS * rows * span,
        ),
        name="attention_forward",
    )(packed, *extra)


def attention_back(packed, probs, grad, span, swap=None):
    rows = packed.shape[0]
    at = blocks(rows, span)
    apart = swap if swap is not None and lax.axis_size("tm") != 8 else None
    more, outs, scratch, parameters = swap_parts(None if apart is not None else swap, False)
    anywhere = pl.BlockSpec(memory_space=pl.ANY)
    result = pl.pallas_call(
        lambda *refs: attn_bwd_kernel(span // TILE, bool(more), *refs),
        grid=(rows // span,),
        in_specs=[at["packed"], at["probs"], at["mixed"]] + [anywhere] * len(more),
        out_specs=[at["packed"]] + [anywhere] * len(outs),
        out_shape=[jax.ShapeDtypeStruct((rows, 3 * MODEL), BF)] + outs,
        scratch_shapes=[pltpu.VMEM((span, PAIR), F32), pltpu.VMEM((span, PAIR), F32)] + scratch,
        compiler_params=pltpu.CompilerParams(vmem_limit_bytes=48 * 2**20, **parameters),
        cost_estimate=pl.CostEstimate(
            flops=90 * HEADS * rows * span * HEAD_DIM,
            bytes_accessed=rows * (14 * MODEL + 2 * HEADS * span),
            transcendentals=0,
        ),
        name="attention_backward",
    )(packed, probs, grad, *more)
    if apart is not None:
        return [*result, swap_plain(False, apart)]
    return result if swap is not None else result[0]


def back_norm_rows(grad, weight_ref, values, carried, gain):
    back = dot_nt(grad, weight_ref[...])
    centred = values - jnp.mean(values, axis=1, keepdims=True)
    spread = jnp.mean(centred * centred, axis=1, keepdims=True)
    scale = lax.rsqrt(spread + EPSILON)
    unit = centred * scale
    along = back * gain
    level = jnp.mean(along, axis=1, keepdims=True)
    slope = jnp.mean(along * unit, axis=1, keepdims=True)
    result = carried + scale * (along - level - unit * slope)
    sums = (jnp.sum(back * unit, axis=0, keepdims=True), jnp.sum(back, axis=0, keepdims=True))
    return result, sums


def back_norm_kernel(grad_ref, weight_ref, value_ref, carried_ref, gain_ref, out_ref, sum_ref):
    result, sums = back_norm_rows(
        grad_ref[...],
        weight_ref,
        value_ref[...].astype(F32),
        carried_ref[...].astype(F32),
        gain_ref[...],
    )
    out_ref[...] = result.astype(BF)

    @pl.when(pl.program_id(0) == 0)
    def _():
        sum_ref[...] = jnp.zeros_like(sum_ref)

    for i in range(2):
        sum_ref[i : i + 1, :] += sums[i]


def back_norm(grad, weight, values, carried, gain):
    rows, width = values.shape
    tile = min(rows, TILE)

    def by_rows(columns):
        return pl.BlockSpec((tile, columns), lambda i: (i, 0))

    def whole(*shape):
        return pl.BlockSpec(shape, lambda i: (0, 0))

    return pl.pallas_call(
        back_norm_kernel,
        grid=(rows // tile,),
        in_specs=[
            by_rows(grad.shape[1]),
            whole(*weight.shape),
            by_rows(width),
            by_rows(width),
            whole(1, width),
        ],
        out_specs=[by_rows(width), whole(2, width)],
        out_shape=[
            jax.ShapeDtypeStruct((rows, width), BF),
            jax.ShapeDtypeStruct((2, width), F32),
        ],
        compiler_params=pltpu.CompilerParams(vmem_limit_bytes=40 * 2**20),
        cost_estimate=pl.CostEstimate(
            flops=2 * rows * width * grad.shape[1],
            bytes_accessed=2 * grad.shape[1] * (rows + width),
            transcendentals=0,
        ),
        name="back_norm",
    )(grad, weight, values, carried, gain[None])


def act_kernel(normed_ref, weight_ref, bias_ref, act_ref, turned_ref, slope_ref):
    hidden = dot_nn(normed_ref[...], weight_ref[...]) + bias_ref[...]
    root, cubic = math.sqrt(2.0 / math.pi), 0.044715
    square = hidden * hidden
    tanh = jnp.tanh(root * hidden * (1.0 + cubic * square))
    half = 0.5 + 0.5 * tanh
    act = (hidden * half).astype(BF)
    act_ref[...] = act
    turned_ref[...] = act.T
    slope_ref[...] = (
        half + (0.5 * root) * hidden * (1.0 - tanh * tanh) * (1.0 + 3.0 * cubic * square)
    ).astype(BF)


def activate(normed, weight, bias):
    rows, units = normed.shape[0], weight.shape[1]
    tile = 512
    return pl.pallas_call(
        act_kernel,
        grid=(units // tile,),
        in_specs=[
            pl.BlockSpec(normed.shape, lambda j: (0, 0)),
            pl.BlockSpec((weight.shape[0], tile), lambda j: (0, j)),
            pl.BlockSpec((1, tile), lambda j: (0, j)),
        ],
        out_specs=[
            pl.BlockSpec((rows, tile), lambda j: (0, j)),
            pl.BlockSpec((tile, rows), lambda j: (j, 0)),
            pl.BlockSpec((rows, tile), lambda j: (0, j)),
        ],
        out_shape=[
            pltpu.HBM((rows, units), BF),
            pltpu.HBM((units, rows), BF),
            pltpu.HBM((rows, units), BF),
        ],
        compiler_params=pltpu.CompilerParams(vmem_limit_bytes=24 * 2**20),
        cost_estimate=pl.CostEstimate(
            flops=2 * rows * units * weight.shape[0],
            bytes_accessed=2 * units * (3 * rows + weight.shape[0]),
            transcendentals=rows * units,
        ),
        name="activate",
    )(normed, weight, bias[None])


def back_act_kernel(grad_ref, weight_ref, slope_ref, out_ref, sum_ref):
    back = (dot_nt(grad_ref[...], weight_ref[...]) * slope_ref[...].astype(F32)).astype(BF)
    out_ref[...] = back
    sum_ref[...] = jnp.sum(back.astype(F32), axis=0, keepdims=True)


def back_act(grad, weight, slope):
    rows, units = slope.shape
    tile = 512
    return pl.pallas_call(
        back_act_kernel,
        grid=(units // tile,),
        in_specs=[
            pl.BlockSpec(grad.shape, lambda j: (0, 0)),
            pl.BlockSpec((tile, grad.shape[1]), lambda j: (j, 0)),
            pl.BlockSpec((rows, tile), lambda j: (0, j)),
        ],
        out_specs=[
            pl.BlockSpec((rows, tile), lambda j: (0, j)),
            pl.BlockSpec((1, tile), lambda j: (0, j)),
        ],
        out_shape=[
            jax.ShapeDtypeStruct((rows, units), BF),
            jax.ShapeDtypeStruct((1, units), F32),
        ],
        compiler_params=pltpu.CompilerParams(vmem_limit_bytes=24 * 2**20),
        cost_estimate=pl.CostEstimate(
            flops=2 * rows * units * grad.shape[1],
            bytes_accessed=2 * units * (2 * rows + grad.shape[1]),
            transcendentals=0,
        ),
        name="back_act",
    )(grad, weight, slope)


def hop(block, axis, flip):
    size = lax.axis_size(axis)
    return lax.ppermute(block, axis, [(i, i ^ flip) for i in range(size)])


def add_low(one, other):
    return (one.astype(F32) + other.astype(F32)).astype(BF)


def lay_kernel(rows, places, splits, *refs):
    count, outs = len(places), len(splits)
    parts, whole = refs[:count], refs[count : count + outs]
    stage = refs[count + outs : 2 * count + outs]
    came, left = refs[-2:]
    me = lax.axis_index("tm")
    inward = [pltpu.make_async_copy(parts[i], stage[i], came.at[i]) for i in range(count)]
    for copy in inward:
        copy.start()
    outward = []
    for i, (flip, start) in enumerate(places):
        at = pl.multiple_of((me ^ flip) * rows + start, 32)
        inward[i].wait()
        first = 0
        for j, columns in enumerate(splits):
            outward.append(
                pltpu.make_async_copy(
                    stage[i].at[:, pl.ds(first, columns)],
                    whole[j].at[pl.ds(at, parts[i].shape[0]), :],
                    left.at[i, j],
                )
            )
            outward[-1].start()
            first += columns
    for copy in outward:
        copy.wait()


def first_hops(block):
    if lax.axis_size("tm") != 8:
        return None
    return hop(block, "tm", 2), hop(block, "tm", 4)


def second_hops(came):
    if came is None:
        return None
    half = came[0].shape[0] // 2
    return hop(came[0][:half], "tm", 4), hop(came[1][half:], "tm", 2)


def gather_rows(block, came, passed, splits):
    if came is None:
        whole = lax.all_gather(block, "tm", axis=0, tiled=True)
        return jnp.split(whole, [sum(splits[:i]) for i in range(1, len(splits))], axis=1)
    rows = block.shape[0]
    half = rows // 2
    by_two, by_four = came
    low_six, high_six = passed
    pieces = ((block, 0, 0), (by_two, 2, 0), (by_four, 4, 0), (low_six, 6, 0), (high_six, 6, half))
    parts, places = [], []
    for piece, flip, start in pieces:
        for core in range(2):
            parts.append(hop(piece, "tm", 1) if core else piece)
            places.append((flip + core, start))
    return pl.pallas_call(
        lambda *refs: lay_kernel(rows, places, splits, *refs),
        in_specs=[pl.BlockSpec(memory_space=pl.ANY)] * len(parts),
        out_specs=[pl.BlockSpec(memory_space=pltpu.HBM)] * len(splits),
        out_shape=[jax.ShapeDtypeStruct((8 * rows, n), block.dtype) for n in splits],
        scratch_shapes=[pltpu.VMEM(part.shape, part.dtype) for part in parts]
        + [
            pltpu.SemaphoreType.DMA((len(parts),)),
            pltpu.SemaphoreType.DMA((len(parts), len(splits))),
        ],
        compiler_params=pltpu.CompilerParams(vmem_limit_bytes=20 * 2**20),
        cost_estimate=pl.CostEstimate(
            flops=0, bytes_accessed=32 * rows * block.shape[1], transcendentals=0
        ),
        name="lay_rows",
    )(*parts)


def after(value, *others):
    return lax.optimization_barrier((value,) + others)[0]


def first_kernel(*refs):
    blocks, small_ref, tokens_ref = refs[:2], refs[2], refs[3]
    wholes, smalls_ref, frames_ref = refs[4:6], refs[6], refs[7]
    local, small_sem, frame_sem, near, far, core = refs[8:]
    me, side = lax.axis_index("tm"), lax.axis_index("space")
    rows = blocks[0].shape[0]
    half = rows // 2
    half_grid, own_frames = tokens_ref.shape[1], tokens_ref.shape[0] // 2

    barrier = pltpu.get_barrier_semaphore()
    for flip in range(1, 8):
        pl.semaphore_signal(
            barrier, inc=1, device_id={"tm": me ^ flip}, device_id_type=pl.DeviceIdType.MESH
        )
    pl.semaphore_signal(
        barrier, inc=1, device_id={"space": 1 - side}, device_id_type=pl.DeviceIdType.MESH
    )
    pl.semaphore_wait(barrier, 8)

    sent = []

    def send(src, dst, sems, device):
        copy = pltpu.make_async_remote_copy(
            src_ref=src,
            dst_ref=dst,
            send_sem=sems.at[0],
            recv_sem=sems.at[1],
            device_id=device,
            device_id_type=pl.DeviceIdType.MESH,
        )
        copy.start()
        sent.append(copy)
        return copy

    def place(w, flip, start, length):
        at = pl.multiple_of((me ^ flip) * rows + start, half)
        return wholes[w].at[pl.ds(at, length), :]

    arrived = {}
    for w in range(2):
        for number, (flip, start) in enumerate(((2, 0), (4, half), (2, half), (4, 0))):
            arrived[w, flip, start] = send(
                blocks[w].at[pl.ds(start, half), :],
                place(w, 0, start, half),
                near.at[w, number],
                {"tm": me ^ flip},
            )
    small_copies = [
        send(small_ref, smalls_ref.at[me], small_sem.at[flip], {"tm": me ^ flip})
        for flip in range(1, 8)
    ]
    columns = pl.ds(pl.multiple_of(side * half_grid, half_grid), half_grid)
    frame_copy = send(
        tokens_ref.at[pl.ds((1 - side) * own_frames, own_frames)],
        frames_ref.at[:, columns, :],
        frame_sem,
        {"space": 1 - side},
    )
    core_copies = [
        send(blocks[w], place(w, 0, 0, rows), core.at[w, 0], {"tm": me ^ 1}) for w in range(2)
    ]
    own = [
        pltpu.make_async_copy(small_ref, smalls_ref.at[me], local.at[0]),
        pltpu.make_async_copy(
            tokens_ref.at[pl.ds(side * own_frames, own_frames)],
            frames_ref.at[:, columns, :],
            local.at[1],
        ),
    ] + [pltpu.make_async_copy(blocks[w], place(w, 0, 0, rows), local.at[2 + w]) for w in range(2)]
    for copy in own:
        copy.start()
    for w in range(2):
        for number, (flip, start) in enumerate(((2, 0), (4, half), (2, half), (4, 0))):
            arrived[w, flip, start].wait_recv()
            block = place(w, flip, start, half)
            if number < 2:
                arrived[w, 6, start] = send(
                    block, block, far.at[w, number], {"tm": me ^ (6 - flip)}
                )
            core_copies.append(send(block, block, core.at[w, 1 + number], {"tm": me ^ 1}))
    for w in range(2):
        for number, start in enumerate((0, half)):
            arrived[w, 6, start].wait_recv()
            block = place(w, 6, start, half)
            core_copies.append(send(block, block, core.at[w, 5 + number], {"tm": me ^ 1}))
    for copy in small_copies + [frame_copy] + core_copies:
        copy.wait_recv()
    for copy in own:
        copy.wait()
    for copy in sent:
        copy.wait_send()


def first_gather(weights, small, tokens):
    if lax.axis_size("tm") != 8:
        return (
            *[lax.all_gather(weight, "tm", axis=0, tiled=True) for weight in weights],
            lax.all_gather(small, "tm", axis=0),
            lax.all_to_all(tokens, "space", 0, 1, tiled=True),
        )
    used = small.shape[0]
    small = jnp.pad(small, ((0, -used % 16), (0, 0)))
    frames, half_grid, model = tokens.shape
    dma = pltpu.SemaphoreType.DMA
    first, second, smalls, whole_frames = pl.pallas_call(
        first_kernel,
        in_specs=[pl.BlockSpec(memory_space=pltpu.VMEM)] * 4,
        out_specs=[pl.BlockSpec(memory_space=pltpu.HBM)] * 4,
        out_shape=[
            pltpu.HBM((8 * weight.shape[0], weight.shape[1]), weight.dtype) for weight in weights
        ]
        + [
            jax.ShapeDtypeStruct((8,) + small.shape, small.dtype),
            jax.ShapeDtypeStruct((frames // 2, 2 * half_grid, model), tokens.dtype),
        ],
        scratch_shapes=[
            dma((4,)),
            dma((8, 2)),
            dma((2,)),
            dma((2, 4, 2)),
            dma((2, 2, 2)),
            dma((2, 7, 2)),
        ],
        compiler_params=pltpu.CompilerParams(
            vmem_limit_bytes=16 * 2**20, collective_id=3, has_side_effects=True
        ),
        cost_estimate=pl.CostEstimate(flops=0, bytes_accessed=2**24, transcendentals=0),
        name="first_gather",
    )(*weights, small, tokens)
    return first, second, smalls[:, :used], whole_frames


UNIT = 128
WIDE = 256
ORDERS = ((3, 7, 1, 5), (5, 7, 1, 3), (2, 6, 0, 4), (4, 6, 0, 2))


OPERANDS = (
    "act_turned",
    "out_low",
    "normed_three",
    "grad_pre",
    "packed",
    "grad_mixed",
    "normed_two",
    "grad_packed_two",
    "time_mixed",
    "time_branch",
    "weight",
    "inputs",
    "branch",
    "space_mixed",
    "normed_one",
    "small",
)
SMALL_ROWS, SMALL_COLUMNS = 32, 128
SLOTS = 6
FINALS = 10
DELAYS = (0, 1, 3, 5, 7, 9, 11, 13)


def last_kernel(chunks, places, *refs):
    refs = list(refs)

    def take(count):
        taken = refs[:count]
        del refs[:count]
        return taken

    count = len(OPERANDS)
    far_off = dict(zip(OPERANDS, take(count)))
    probs_ref, embedded_ref, gain_ref, one_hot_ref = take(4)
    out_refs, small_out, frames_out = take(len(chunks)), take(1)[0], take(1)[0]
    near = dict(zip(OPERANDS, take(count)))
    (grad_packed, turned, lines, kept, probs_near) = take(5)
    (far, own, from_core, from_chip, from_owner, share, from_space, from_row, final) = take(9)
    (core_sem, chip_sem, owner_sem, space_sem, row_sem, back_sem, last_sem) = take(7)
    load_sem, probs_sem, frame_sem = take(3)
    me, side, level = lax.axis_index("tm"), lax.axis_index("space"), lax.axis_index("row")
    total = len(places)
    r = UNIT
    frames = grad_packed.shape[0] // TILE
    units = frames * PAIRS

    loads = {
        name: pltpu.make_async_copy(far_off[name], near[name], load_sem.at[i])
        for i, name in enumerate(OPERANDS)
    }
    for name in OPERANDS:
        loads[name].start()
    waited = set()

    def here(name):
        if name == "grad_packed_one":
            return grad_packed
        if name not in waited:
            waited.add(name)
            loads[name].wait()
        return near[name]

    def tm_at(flip):
        return {"tm": me ^ flip}

    barrier = pltpu.get_barrier_semaphore()
    for device in (tm_at(1), tm_at(2), tm_at(4), {"space": 1 - side}, {"row": 1 - level}):
        pl.semaphore_signal(barrier, inc=1, device_id=device, device_id_type=pl.DeviceIdType.MESH)
    pl.semaphore_wait(barrier, 5)

    def start(src, dst, sems, device):
        copy = pltpu.make_async_remote_copy(
            src_ref=src,
            dst_ref=dst,
            send_sem=sems.at[0],
            recv_sem=sems.at[1],
            device_id=device,
            device_id_type=pl.DeviceIdType.MESH,
        )
        copy.start()
        return copy

    cores, chips, owners, spaces, rows, backs, lasts = ({} for _ in range(7))

    def size(t):
        return (SMALL_ROWS, SMALL_COLUMNS) if places[t][0] == len(chunks) else (UNIT, WIDE)

    def box(t, first, count=1):
        each, wide = size(t)
        return pl.ds(first * each, count * each), pl.ds(0, wide)

    def part(t, h, order):
        which, row, column, half = places[t]
        if which == len(chunks):
            return jnp.concatenate([lines[me ^ flip] for flip in order], axis=0)
        left, right = chunks[which]
        source = here(left) if left == "act_turned" else turned
        rows_each = source.shape[0] // 8
        picked = [
            source[pl.ds(pl.multiple_of((me ^ flip) * rows_each + row, r), r), :] for flip in order
        ]
        return dot_nn(
            jnp.concatenate(picked, axis=0), here(right)[:, pl.ds(column + h * half, WIDE)]
        )

    def stage_core(t):
        which, slot = places[t][0], t % SLOTS
        if which < len(chunks) and (t == 0 or places[t - 1][0] != which):
            if chunks[which][0] != "act_turned":
                turned[...] = here(chunks[which][0])[...].T
        for h in range(2):
            if t >= SLOTS:
                cores[t - SLOTS, h].wait_send()
            every = box(t, 0, 4)
            far[(slot, h, *every)] = part(t, h, ORDERS[h]).astype(BF)
            cores[t, h] = start(
                far.at[(slot, h, *every)],
                from_core.at[(slot, h, *every)],
                core_sem.at[slot, h],
                tm_at(1),
            )
        for h in range(2):
            if t >= SLOTS:
                chips[t - SLOTS, h].wait_send()
                owners[t - SLOTS, h].wait_send()
            own[(slot, h, *box(t, 0, 4))] = part(t, h, ORDERS[2 + h]).astype(BF)

    def stage_chip(t):
        slot = t % SLOTS
        for h in range(2):
            cores[t, h].wait_recv()
            every = (slot, h, *box(t, 0, 4))
            own[every] = add_low(own[every], from_core[every])
            near_half = (slot, h, *box(t, 0, 2))
            chips[t, h] = start(
                own.at[near_half],
                from_chip.at[near_half],
                chip_sem.at[slot, h],
                tm_at(4 if h else 2),
            )

    def stage_owner(t):
        slot = t % SLOTS
        for h in range(2):
            chips[t, h].wait_recv()
            upper = (slot, h, *box(t, 2, 2))
            own[upper] = add_low(own[upper], from_chip[(slot, h, *box(t, 0, 2))])
            owners[t, h] = start(
                own.at[(slot, h, *box(t, 3))],
                from_owner.at[(slot, h, *box(t, 0))],
                owner_sem.at[slot, h],
                tm_at(2 if h else 4),
            )

    def stage_space(t):
        slot = t % SLOTS
        if t >= SLOTS:
            spaces[t - SLOTS].wait_send()
            rows[t - SLOTS].wait_send()
        for h in range(2):
            owners[t, h].wait_recv()
            first = (slot, h, *box(t, 0))
            share[first] = add_low(own[(slot, h, *box(t, 2))], from_owner[first])
        spaces[t] = start(
            share.at[(slot, 1 - side, *box(t, 0))],
            from_space.at[(slot, *box(t, 0))],
            space_sem.at[slot],
            {"space": 1 - side},
        )

    def stage_row(t):
        slot = t % SLOTS
        spaces[t].wait_recv()
        first = (slot, side, *box(t, 0))
        share[first] = add_low(share[first], from_space[(slot, *box(t, 0))])
        half, wide = size(t)[0] // 2, pl.ds(0, size(t)[1])
        other = pl.ds(pl.multiple_of((1 - level) * half, half), half)
        rows[t] = start(
            share.at[slot, side, other, wide],
            from_row.at[slot, pl.ds(0, half), wide],
            row_sem.at[slot],
            {"row": 1 - level},
        )

    def stage_back(t):
        slot = t % SLOTS
        rows[t].wait_recv()
        half, wide = size(t)[0] // 2, pl.ds(0, size(t)[1])
        mine = pl.ds(pl.multiple_of(level * half, half), half)
        last = t % FINALS
        final[last, side, mine, wide] = add_low(
            share[slot, side, mine, wide], from_row[slot, pl.ds(0, half), wide]
        )
        place = final.at[last, side, mine, wide]
        backs[t] = start(place, place, back_sem.at[last], {"row": 1 - level})

    def stage_last(t):
        slot = t % FINALS
        backs[t].wait_recv()
        place = final.at[(slot, side, *box(t, 0))]
        lasts[t] = start(place, place, last_sem.at[slot], {"space": 1 - side})

    def stage_out(t):
        slot = t % FINALS
        lasts[t].wait_recv()
        out, row, column, half = places[t]
        if out == len(chunks):
            small_out[...] = final[(slot, 0, *box(t, 0))].astype(F32)
        else:
            for h in range(2):
                out_refs[out][pl.ds(row, r), pl.ds(column + h * half, WIDE)] = final[slot, h]
        backs[t].wait_send()
        lasts[t].wait_send()

    def probs_copy(unit):
        frame, pair = divmod(unit, PAIRS)
        return pltpu.make_async_copy(
            probs_ref.at[pl.ds(2 * pair, 2), pl.ds(frame * TILE, TILE), :],
            probs_near.at[unit % 2],
            probs_sem.at[unit % 2],
        )

    def attend(unit):
        frame, pair = divmod(unit, PAIRS)
        if unit + 1 < units:
            probs_copy(unit + 1).start()
        probs_copy(unit).wait()
        attn_bwd_tile(
            0,
            1,
            pair,
            here("packed"),
            None,
            here("grad_mixed"),
            grad_packed,
            base=frame * TILE,
            probs_pair=[probs_near[unit % 2, half] for half in range(2)],
        )

    def back_frame(frame):
        some = pl.ds(frame * TILE, TILE)
        values = here("inputs")[some, :].astype(F32) + embedded_ref[pl.ds(frame, 1), :]
        result, sums = back_norm_rows(
            grad_packed[some, :],
            here("weight"),
            values,
            here("branch")[some, :].astype(F32),
            gain_ref[...],
        )
        kept[frame] = result.astype(BF)
        column = jnp.sum(result, axis=0, keepdims=True)
        table = one_hot_ref[pl.ds(frame * ACTIONS, ACTIONS), :] * column
        width = MODEL // 8
        if frame == 0:
            lines[...] = here("small")[...]
        for k in range(8):
            at = slice(k * width, (k + 1) * width)
            lines[k, 0:ACTIONS, 0:width] += table[:, at]
            lines[k, ACTIONS : ACTIONS + 1, 0:width] += sums[0][:, at]
            lines[k, ACTIONS + 3 : ACTIONS + 4, 0:width] += sums[1][:, at]

    exchanged = []

    def exchange():
        half_grid = kept.shape[1] // 2
        own_frames = pl.ds(pl.multiple_of(side * frames, frames), frames)

        def columns(which):
            return pl.ds(pl.multiple_of(which * half_grid, half_grid), half_grid)

        exchanged.append(
            start(
                kept.at[:, columns(1 - side), :],
                frames_out.at[own_frames],
                frame_sem,
                {"space": 1 - side},
            )
        )
        frames_out[own_frames] = kept[:, columns(side), :]

    stages = (
        stage_core,
        stage_chip,
        stage_owner,
        stage_space,
        stage_row,
        stage_back,
        stage_last,
        stage_out,
    )
    probs_copy(0).start()
    for step in range(total + DELAYS[-1]):
        for delay, stage in zip(DELAYS, stages):
            if 0 <= step - delay < total:
                stage(step - delay)
        if 0 < step <= units:
            attend(step - 1)
        elif 0 <= step - 1 - units < frames:
            back_frame(step - 1 - units)
        elif step == 1 + units + frames:
            exchange()
    for t in range(max(0, total - SLOTS), total):
        for h in range(2):
            cores[t, h].wait_send()
            chips[t, h].wait_send()
            owners[t, h].wait_send()
        spaces[t].wait_send()
        rows[t].wait_send()
    exchanged[0].wait()


CHUNKS = (
    ("act_turned", "out_low"),
    ("normed_three", "grad_pre"),
    ("normed_two", "grad_packed_two"),
    ("time_mixed", "time_branch"),
    ("space_mixed", "branch"),
    ("normed_one", "grad_packed_one"),
)


def last_stage(given, probs, embedded, gain, one_hot):
    places, shapes = [], []
    for which, (left, right) in enumerate(CHUNKS):
        width = given[left].shape[0 if left == "act_turned" else 1]
        columns = 3 * MODEL if right == "grad_packed_one" else given[right].shape[1]
        shapes.append((width // 8, columns))
        for sub in range(width // (8 * UNIT)):
            for j in range(columns // 2 // WIDE):
                places.append((which, sub * UNIT, j * WIDE, columns // 2))
    places.append((len(CHUNKS), 0, 0, 0))
    small = given["small"]
    padding = ((0, 0), (0, SMALL_ROWS - small.shape[1]), (0, SMALL_COLUMNS - small.shape[2]))
    given = dict(given, small=jnp.pad(small, padding))
    tokens = given["packed"].shape[0]
    frames = tokens // TILE
    vmem = pltpu.VMEM
    dma = pltpu.SemaphoreType.DMA
    in_vmem, anywhere = pl.BlockSpec(memory_space=pltpu.VMEM), pl.BlockSpec(memory_space=pl.ANY)
    result = pl.pallas_call(
        lambda *refs: last_kernel(CHUNKS, places, *refs),
        in_specs=[anywhere] * (len(OPERANDS) + 1) + [in_vmem] * 3,
        out_specs=[in_vmem] * (len(shapes) + 2),
        out_shape=[jax.ShapeDtypeStruct(shape, BF) for shape in shapes]
        + [
            jax.ShapeDtypeStruct((SMALL_ROWS, SMALL_COLUMNS), F32),
            jax.ShapeDtypeStruct((2 * frames, TILE // 2, MODEL), BF),
        ],
        scratch_shapes=[vmem(given[name].shape, given[name].dtype) for name in OPERANDS]
        + [
            vmem((tokens, 3 * MODEL), BF),
            vmem((MODEL, tokens), BF),
            vmem((8, SMALL_ROWS, SMALL_COLUMNS), F32),
            vmem((frames, TILE, MODEL), BF),
            vmem((2, 2, TILE, TILE), BF),
            vmem((SLOTS, 2, 4 * UNIT, WIDE), BF),
            vmem((SLOTS, 2, 4 * UNIT, WIDE), BF),
            vmem((SLOTS, 2, 4 * UNIT, WIDE), BF),
            vmem((SLOTS, 2, 2 * UNIT, WIDE), BF),
            vmem((SLOTS, 2, UNIT, WIDE), BF),
            vmem((SLOTS, 2, UNIT, WIDE), BF),
            vmem((SLOTS, UNIT, WIDE), BF),
            vmem((SLOTS, UNIT // 2, WIDE), BF),
            vmem((FINALS, 2, UNIT, WIDE), BF),
            dma((SLOTS, 2, 2)),
            dma((SLOTS, 2, 2)),
            dma((SLOTS, 2, 2)),
            dma((SLOTS, 2)),
            dma((SLOTS, 2)),
            dma((FINALS, 2)),
            dma((FINALS, 2)),
            dma((len(OPERANDS),)),
            dma((2,)),
            dma((2,)),
        ],
        compiler_params=pltpu.CompilerParams(
            vmem_limit_bytes=60 * 2**20, collective_id=1, has_side_effects=True
        ),
        cost_estimate=pl.CostEstimate(
            flops=1024, bytes_accessed=len(places) * 8 * UNIT * WIDE, transcendentals=0
        ),
        name="last_stage",
    )(*[given[name] for name in OPERANDS], probs, embedded, gain[None], one_hot)
    grads = [grad.astype(F32) for grad in result[: len(shapes)]]
    return grads, result[-2][: small.shape[1], : small.shape[2]], result[-1]


def last_stage_plain(given, probs, embedded, gain, one_hot):
    tokens = given["packed"].shape[0]
    frames = tokens // TILE
    grad_packed = attention_back(given["packed"], probs, given["grad_mixed"], TILE)
    values = given["inputs"].astype(F32) + jnp.repeat(embedded, TILE, axis=0)
    result, sums = back_norm(grad_packed, given["weight"], values, given["branch"], gain)
    given = dict(given, grad_packed_one=grad_packed, act_turned=given["act_turned"].T)
    grads = []
    for left, right in CHUNKS:
        whole = weight_grad(given[left], given[right]).astype(BF)
        block = lax.psum_scatter(whole, "tm", scatter_dimension=0, tiled=True)
        grads.append(lax.psum(block, ("row", "space")).astype(F32))
    by_frame = jnp.sum(result.reshape(frames, TILE, MODEL).astype(F32), axis=1)
    table = jnp.dot(
        one_hot.reshape(frames, ACTIONS).T, by_frame, precision=lax.Precision.HIGHEST
    )
    none = jnp.zeros((2, MODEL), F32)
    rows = jnp.concatenate((table, sums[:1], none, sums[1:], none))
    size = lax.axis_size("tm")
    more = rows.reshape(-1, size, MODEL // size).transpose(1, 0, 2)
    small = given["small"].at[:, : more.shape[1]].add(more)
    block = lax.psum_scatter(small, "tm", scatter_dimension=0, tiled=True)[0]
    exchanged = lax.all_to_all(
        result.reshape(frames, TILE, MODEL), "space", 1, 0, tiled=True
    )
    return grads, lax.psum(block, ("row", "space")), exchanged


def body(
    block_input,
    action_table,
    norm_gain,
    norm_bias,
    space_qkv,
    space_out,
    time_qkv,
    time_out,
    ffn_in,
    ffn_bias_in,
    ffn_out,
    ffn_bias_out,
    out_grad,
    frame_segment,
    frame_action,
):
    tm, halves = lax.axis_size("tm"), lax.axis_size("space")
    slot, side = lax.axis_index("tm"), lax.axis_index("space")
    frame_count, half_grid = block_input.shape[1], block_input.shape[2]
    own_frames = frame_count // halves
    grid_all = half_grid * halves
    cut = half_grid // tm
    all_frames = frame_count * tm
    rows_dev = frame_count * half_grid
    width = MODEL // tm
    hidden_units = ffn_bias_in.shape[0]

    space_in_w, space_out_w, small, inputs = first_gather(
        (space_qkv, space_out),
        jnp.concatenate(
            [a.reshape(-1, width) for a in (action_table, norm_gain, norm_bias)]
            + [ffn_bias_out.reshape(1, width), ffn_bias_in.reshape(-1, width)]
        ),
        block_input[0],
    )
    lines = ACTIONS + 7
    by_row = small[:, :lines].transpose(1, 0, 2).reshape(lines, MODEL)
    table_full = by_row[:ACTIONS]
    gains = by_row[ACTIONS : ACTIONS + 3].astype(F32)
    shifts = by_row[ACTIONS + 3 : ACTIONS + 6].astype(F32)
    bias_out = by_row[ACTIONS + 6].astype(F32)
    bias_in = small[:, lines:].reshape(-1).astype(F32)

    actions = lax.dynamic_slice(frame_action[0], (side * own_frames,), (own_frames,))
    one_hot = (actions[:, None] == jnp.arange(ACTIONS)[None, :]).astype(BF)
    embedded = forward_dot(one_hot, table_full)

    time_block = jnp.concatenate((time_qkv, time_out), axis=1)
    if tm == 8:
        time_block = after(time_block, space_out_w)
    time_came = first_hops(time_block)

    hidden_zero = (inputs.astype(F32) + embedded[:, None, :]).reshape(rows_dev, MODEL)
    normed_one = layer_norm(hidden_zero, gains[0], shifts[0]).astype(BF)
    packed_one = forward_dot(normed_one, space_in_w).astype(BF)
    space_mixed, space_probs = attention(packed_one, grid_all)
    if tm == 8:
        space_mixed, *time_came = lax.optimization_barrier((space_mixed, *time_came))
    time_passed = second_hops(time_came)
    time_in_w, time_out_w = gather_rows(time_block, time_came, time_passed, (3 * MODEL, MODEL))
    in_block = after(ffn_in, *time_passed) if tm == 8 else ffn_in
    in_came = first_hops(in_block)
    hidden_one_own = (hidden_zero + forward_dot(space_mixed, space_out_w)).astype(BF)

    sent = hidden_one_own.reshape(own_frames, halves * tm, cut, MODEL)
    blocks_t = lax.all_to_all(sent, ("space", "tm"), 1, 0)
    hidden_one_low = lax.optimization_barrier(
        blocks_t.reshape(halves, tm, own_frames, cut, MODEL)
        .transpose(1, 0, 2, 3, 4)
        .reshape(rows_dev, MODEL)
    )
    hidden_one = hidden_one_low.astype(F32)
    groups = (
        frame_segment[0].astype(jnp.int32)[:, None] * cut + jnp.arange(cut, dtype=jnp.int32)
    ).reshape(rows_dev)

    normed_two = layer_norm(hidden_one, gains[1], shifts[1]).astype(BF)
    packed_two = forward_dot(normed_two, time_in_w).astype(BF)
    if tm == 8:
        packed_two, out_grad, *in_came = lax.optimization_barrier(
            (packed_two, out_grad, *in_came)
        )
    in_passed = second_hops(in_came)
    grad_out_low = swap_plain(True, out_grad[0])
    time_mixed, time_probs = attention(packed_two, rows_dev, groups)
    out_block = ffn_out
    if tm == 8:
        time_mixed, grad_out_low, out_block, *in_passed = lax.optimization_barrier(
            (time_mixed, grad_out_low, ffn_out, *in_passed)
        )
    grad_out_low = grad_out_low.reshape(rows_dev, MODEL)
    grad_out = grad_out_low.astype(F32)
    out_came = first_hops(out_block)
    (ffn_in_w,) = gather_rows(in_block, in_came, in_passed, (ffn_in.shape[1],))
    hidden_two = hidden_one + forward_dot(time_mixed, time_out_w)
    normed_three = layer_norm(hidden_two, gains[2], shifts[2]).astype(BF)
    act_low, act_turned, slope = activate(normed_three, ffn_in_w, bias_in)
    if tm == 8:
        slope, *out_came = lax.optimization_barrier((slope, *out_came))
    (ffn_out_w,) = gather_rows(out_block, out_came, second_hops(out_came), (MODEL,))
    bias_out_grad = jnp.sum(grad_out, axis=0)
    grad_pre_low, bias_in_grad = back_act(grad_out_low, ffn_out_w, slope)
    bias_in_grad = bias_in_grad[0]
    time_branch, sums_three = back_norm(
        grad_pre_low, ffn_in_w, hidden_two, grad_out_low, gains[2]
    )
    time_grad_mixed = back_dot(time_branch, time_out_w).astype(BF)
    block_out = (hidden_two + forward_dot(act_low, ffn_out_w) + bias_out).astype(BF)
    grad_packed_two, block_output = attention_back(
        packed_two,
        time_probs,
        time_grad_mixed,
        rows_dev,
        swap=block_out.reshape(all_frames, cut, MODEL),
    )
    block_output = block_output[None]
    grad_one_low, sums_two = back_norm(
        grad_packed_two, time_in_w, hidden_one_low, time_branch, gains[1]
    )

    sent = (
        grad_one_low.reshape(tm, halves, own_frames, cut, MODEL)
        .transpose(1, 0, 2, 3, 4)
        .reshape(halves * tm, own_frames, cut, MODEL)
    )
    space_branch = lax.all_to_all(sent, ("space", "tm"), 0, 1).reshape(rows_dev, MODEL)
    space_grad_mixed = back_dot(space_branch, space_out_w).astype(BF)
    none = jnp.zeros((1, MODEL), F32)
    by_row = jnp.concatenate(
        [jnp.zeros((ACTIONS, MODEL), F32)]
        + [
            row
            for i in range(2)
            for row in (none, sums_two[i : i + 1], sums_three[i : i + 1])
        ]
        + [bias_out_grad[None]]
    )
    shares = jnp.concatenate(
        (
            by_row.reshape(lines, tm, width).transpose(1, 0, 2),
            bias_in_grad.reshape(tm, -1, width),
        ),
        axis=1,
    )
    given = {
        "act_turned": act_turned,
        "out_low": grad_out_low,
        "normed_three": normed_three,
        "grad_pre": grad_pre_low,
        "packed": packed_one,
        "grad_mixed": space_grad_mixed,
        "normed_two": normed_two,
        "grad_packed_two": grad_packed_two,
        "time_mixed": time_mixed,
        "time_branch": time_branch,
        "weight": space_in_w,
        "inputs": inputs.reshape(rows_dev, MODEL),
        "branch": space_branch,
        "space_mixed": space_mixed,
        "normed_one": normed_one,
        "small": shares,
    }
    finish = last_stage if tm == 8 else last_stage_plain
    grads, small_grads, frames_grad = finish(
        given, space_probs, embedded, gains[0], one_hot.astype(F32).reshape(-1, 1)
    )
    ffn_out_grad, ffn_in_grad, time_qkv_grad, time_out_grad, space_out_grad, space_qkv_grad = grads
    input_grad = frames_grad.astype(F32)[None]
    return (
        block_output,
        input_grad,
        small_grads[:ACTIONS],
        small_grads[ACTIONS : ACTIONS + 3],
        small_grads[ACTIONS + 3 : ACTIONS + 6],
        space_qkv_grad,
        space_out_grad,
        time_qkv_grad,
        time_out_grad,
        ffn_in_grad,
        small_grads[lines:].reshape(hidden_units),
        ffn_out_grad,
        small_grads[ACTIONS + 6],
    )


def solution(mesh):
    placed = (
        P("row", "tm", "space", None),
        P(None, "tm"),
        P(None, "tm"),
        P(None, "tm"),
        P("tm", None),
        P("tm", None),
        P("tm", None),
        P("tm", None),
        P("tm", None),
        P("tm"),
        P("tm", None),
        P("tm"),
        P("row", "tm", "space", None),
        P("row", None),
        P("row", "tm"),
    )
    return jax.shard_map(
        body,
        mesh=mesh,
        in_specs=placed,
        out_specs=(
            P("row", "tm", "space", None),
            P("row", "tm", "space", None),
            P(None, "tm"),
            P(None, "tm"),
            P(None, "tm"),
            P("tm", None),
            P("tm", None),
            P("tm", None),
            P("tm", None),
            P("tm", None),
            P("tm"),
            P("tm", None),
            P("tm"),
        ),
        check_vma=False,
    )
```

```python
import math

import jax
import jax.numpy as jnp
from jax import lax
from jax.experimental import pallas as pl
from jax.experimental.pallas import tpu as pltpu
from jax.sharding import PartitionSpec as P

MODEL = 1024
HEADS = 16
HEAD_DIM = 64
ACTIONS = 8
TILE = 256
PAIR = 2 * HEAD_DIM
PAIRS = HEADS // 2
SCALE = 1.0 / math.sqrt(HEAD_DIM)

EPSILON = 1e-05
NEG_FILL = -1e30
BF = jnp.bfloat16
F32 = jnp.float32


def layer_norm(values, gain_row, shift_row):
    row_mean = jnp.mean(values, axis=-1, keepdims=True)
    centred = values - row_mean
    spread = jnp.mean(centred * centred, axis=-1, keepdims=True)
    return centred * lax.rsqrt(spread + EPSILON) * gain_row + shift_row


def forward_dot(values, weight):
    return jnp.dot(values, weight, preferred_element_type=F32)


def weight_grad(left_rows, right_rows):
    return lax.dot_general(
        left_rows, right_rows, (((0,), (0,)), ((), ())), preferred_element_type=F32
    )


def back_dot(grad_rows, weight):
    return lax.dot_general(
        grad_rows, weight, (((1,), (1,)), ((), ())), preferred_element_type=F32
    )


def dot_nt(a, b):
    return lax.dot_general(a, b, (((1,), (1,)), ((), ())), preferred_element_type=F32)


def dot_nn(a, b):
    return lax.dot_general(a, b, (((1,), (0,)), ((), ())), preferred_element_type=F32)


def dot_tn(a, b):
    return lax.dot_general(a, b, (((0,), (0,)), ((), ())), preferred_element_type=F32)


def of_head(half, values):
    lane = lax.broadcasted_iota(jnp.int32, values.shape, 1)
    keep = (lane < HEAD_DIM) if half == 0 else (lane >= HEAD_DIM)
    return jnp.where(keep, values, jnp.zeros_like(values))


def join_heads(first, second):
    lane = lax.broadcasted_iota(jnp.int32, first.shape, 1)
    return jnp.where(lane < HEAD_DIM, first, second)


def pair_cols(pair, part):
    if isinstance(pair, int):
        return pl.ds(part * MODEL + pair * PAIR, PAIR)
    return pl.ds(pl.multiple_of(part * MODEL + pair * PAIR, PAIR), PAIR)


def start_swap(to_all, src_ref, dst_ref, sems, local_sem):
    me, size = lax.axis_index("tm"), sems.shape[0]
    whole, part = (dst_ref, src_ref) if to_all else (src_ref, dst_ref)
    frames, cut = part.shape[0], whole.shape[1]

    def some_frames(ref, device):
        return ref.at[pl.ds(pl.multiple_of(device * frames, frames), frames)]

    def some_places(ref, device):
        return ref.at[:, pl.ds(pl.multiple_of(device * cut, cut), cut), :]

    def ends(device):
        if to_all:
            return some_places(src_ref, device), some_frames(dst_ref, me)
        return some_frames(src_ref, device), some_places(dst_ref, me)

    barrier = pltpu.get_barrier_semaphore()
    for flip in range(1, size):
        pl.semaphore_signal(
            barrier, inc=1, device_id={"tm": me ^ flip}, device_id_type=pl.DeviceIdType.MESH
        )
    pl.semaphore_wait(barrier, size - 1)
    copies = []
    for flip in range(1, size):
        src, dst = ends(me ^ flip)
        copies.append(
            pltpu.make_async_remote_copy(
                src_ref=src,
                dst_ref=dst,
                send_sem=sems.at[flip, 0],
                recv_sem=sems.at[flip, 1],
                device_id={"tm": me ^ flip},
                device_id_type=pl.DeviceIdType.MESH,
            )
        )
    src, dst = ends(me)
    copies.append(pltpu.make_async_copy(src, dst, local_sem))
    for copy in copies:
        copy.start()
    return copies


def swap_plain(to_all, block):
    split, concat = (1, 0) if to_all else (0, 1)
    return lax.all_to_all(block, "tm", split, concat, tiled=True)


def swapped_shape(to_all, block, size):
    first, second, width = block.shape
    if to_all:
        return (first * size, second // size, width)
    return (first // size, second * size, width)


def attn_fwd_kernel(tiles, masked, packed_ref, *refs):
    if masked:
        col_ref, row_ref, mixed_ref, probs_ref = refs
    else:
        mixed_ref, probs_ref = refs

    def one_pair(pair, carry):
        for t in range(tiles):
            mine = pl.ds(t * TILE, TILE)
            width = (t + 1) * TILE
            seen = pl.ds(0, width)
            query = packed_ref[mine, pair_cols(pair, 0)] * jnp.asarray(SCALE, BF)
            key = packed_ref[seen, pair_cols(pair, 1)]
            value = packed_ref[seen, pair_cols(pair, 2)]
            if masked:
                same = col_ref[mine, :] == row_ref[:, seen]
                order = lax.broadcasted_iota(
                    jnp.int32, (TILE, width), 0
                ) + t * TILE >= lax.broadcasted_iota(jnp.int32, (TILE, width), 1)
                allowed = same & order
            outs = []
            for half in range(2):
                scores = dot_nt(of_head(half, query), key)
                if masked:
                    scores = jnp.where(allowed, scores, NEG_FILL)
                top = jnp.max(scores, axis=1, keepdims=True)
                raised = jnp.exp(scores - top)
                total = jnp.sum(raised, axis=1, keepdims=True)
                probs = (raised * (1.0 / total)).astype(BF)
                probs_ref[2 * pair + half, mine, seen] = probs
                outs.append(dot_nn(probs, value))
            mixed_ref[mine, pair_cols(pair, 0)] = join_heads(*outs).astype(BF)
        return carry

    lax.fori_loop(0, PAIRS, one_pair, 0, unroll=4)


def attn_bwd_tile(
    t, tiles, pair, packed_ref, probs_ref, grad_ref, out_ref, accs=None, base=0, probs_pair=None
):
    mine = pl.ds(base + t * TILE, TILE)
    seen = pl.ds(base, (t + 1) * TILE)
    query = packed_ref[mine, pair_cols(pair, 0)] * jnp.asarray(SCALE, BF)
    key = packed_ref[seen, pair_cols(pair, 1)]
    value = packed_ref[seen, pair_cols(pair, 2)]
    grad = grad_ref[mine, pair_cols(pair, 0)]
    dqs, dks, dvs = [], [], []
    for half in range(2):
        if probs_pair is None:
            probs_low = probs_ref[2 * pair + half, mine, pl.ds(0, (t + 1) * TILE)]
        else:
            probs_low = probs_pair[half]
        probs = probs_low.astype(F32)
        dprobs = dot_nt(of_head(half, grad), value)
        delta = jnp.sum(dprobs * probs, axis=1, keepdims=True)
        dscores = (probs * (dprobs - delta)).astype(BF)
        dqs.append(dot_nn(dscores, key))
        dks.append(dot_tn(dscores, query))
        dvs.append(dot_tn(probs_low, grad))
    out_ref[mine, pair_cols(pair, 0)] = (join_heads(*dqs) * SCALE).astype(BF)
    dkey, dvalue = join_heads(*dks), join_heads(*dvs)
    if tiles == 1:
        out_ref[seen, pair_cols(pair, 1)] = dkey.astype(BF)
        out_ref[seen, pair_cols(pair, 2)] = dvalue.astype(BF)
        return
    if t == tiles - 1:
        accs[0][...] = dkey
        accs[1][...] = dvalue
    else:
        accs[0][pl.ds(0, (t + 1) * TILE), :] += dkey
        accs[1][pl.ds(0, (t + 1) * TILE), :] += dvalue
    if t == 0:
        out_ref[:, pair_cols(pair, 1)] = accs[0][...].astype(BF)
        out_ref[:, pair_cols(pair, 2)] = accs[1][...].astype(BF)


def attn_bwd_kernel(tiles, swapped, packed_ref, probs_ref, grad_ref, *refs):
    copies = []
    if swapped:
        src_ref, out_ref, dst_ref, *accs, sems, local_sem = refs
        copies = start_swap(False, src_ref, dst_ref, sems, local_sem)
    else:
        out_ref, *accs = refs

    def one_pair(pair, carry):
        for t in reversed(range(tiles)):
            attn_bwd_tile(t, tiles, pair, packed_ref, probs_ref, grad_ref, out_ref, accs)
        return carry

    lax.fori_loop(0, PAIRS, one_pair, 0, unroll=4)
    for copy in copies:
        copy.wait()


def blocks(rows, span):
    return {
        "packed": pl.BlockSpec((span, 3 * MODEL), lambda t: (t, 0)),
        "mixed": pl.BlockSpec((span, MODEL), lambda t: (t, 0)),
        "probs": pl.BlockSpec((HEADS, span, span), lambda t: (0, t, 0)),
        "col": pl.BlockSpec((span, 1), lambda t: (t, 0)),
        "row": pl.BlockSpec((1, span), lambda t: (0, t)),
    }


def swap_parts(swap, to_all):
    if swap is None:
        return [], [], [], {}
    size = lax.axis_size("tm")
    dma = pltpu.SemaphoreType.DMA
    shape = swapped_shape(to_all, swap, size)
    return (
        [swap],
        [jax.ShapeDtypeStruct(shape, swap.dtype)],
        [dma((size, 2)), dma(())],
        {"collective_id": 4 + to_all, "has_side_effects": True},
    )


def attention(packed, span, groups=None):
    rows = packed.shape[0]
    at = blocks(rows, span)
    masked = groups is not None
    extra = (groups[:, None], groups[None, :]) if masked else ()
    specs = [at["packed"]] + ([at["col"], at["row"]] if masked else [])
    return pl.pallas_call(
        lambda *refs: attn_fwd_kernel(span // TILE, masked, *refs),
        grid=(rows // span,),
        in_specs=specs,
        out_specs=[at["mixed"], at["probs"]],
        out_shape=[
            jax.ShapeDtypeStruct((rows, MODEL), BF),
            jax.ShapeDtypeStruct((HEADS, rows, span), BF),
        ],
        compiler_params=pltpu.CompilerParams(vmem_limit_bytes=48 * 2**20),
        cost_estimate=pl.CostEstimate(
            flops=80 * HEADS * rows * span * HEAD_DIM,
            bytes_accessed=rows * (8 * MODEL + 2 * HEADS * span),
            transcendentals=HEADS * rows * span,
        ),
        name="attention_forward",
    )(packed, *extra)


def attention_back(packed, probs, grad, span, swap=None):
    rows = packed.shape[0]
    at = blocks(rows, span)
    apart = swap if swap is not None and lax.axis_size("tm") != 8 else None
    more, outs, scratch, parameters = swap_parts(None if apart is not None else swap, False)
    anywhere = pl.BlockSpec(memory_space=pl.ANY)
    result = pl.pallas_call(
        lambda *refs: attn_bwd_kernel(span // TILE, bool(more), *refs),
        grid=(rows // span,),
        in_specs=[at["packed"], at["probs"], at["mixed"]] + [anywhere] * len(more),
        out_specs=[at["packed"]] + [anywhere] * len(outs),
        out_shape=[jax.ShapeDtypeStruct((rows, 3 * MODEL), BF)] + outs,
        scratch_shapes=[pltpu.VMEM((span, PAIR), F32), pltpu.VMEM((span, PAIR), F32)] + scratch,
        compiler_params=pltpu.CompilerParams(vmem_limit_bytes=48 * 2**20, **parameters),
        cost_estimate=pl.CostEstimate(
            flops=90 * HEADS * rows * span * HEAD_DIM,
            bytes_accessed=rows * (14 * MODEL + 2 * HEADS * span),
            transcendentals=0,
        ),
        name="attention_backward",
    )(packed, probs, grad, *more)
    if apart is not None:
        return [*result, swap_plain(False, apart)]
    return result if swap is not None else result[0]


def back_norm_rows(grad, weight_ref, values, carried, gain):
    back = dot_nt(grad, weight_ref[...])
    centred = values - jnp.mean(values, axis=1, keepdims=True)
    spread = jnp.mean(centred * centred, axis=1, keepdims=True)
    scale = lax.rsqrt(spread + EPSILON)
    unit = centred * scale
    along = back * gain
    level = jnp.mean(along, axis=1, keepdims=True)
    slope = jnp.mean(along * unit, axis=1, keepdims=True)
    result = carried + scale * (along - level - unit * slope)
    sums = (jnp.sum(back * unit, axis=0, keepdims=True), jnp.sum(back, axis=0, keepdims=True))
    return result, sums


def back_norm_kernel(grad_ref, weight_ref, value_ref, carried_ref, gain_ref, out_ref, sum_ref):
    result, sums = back_norm_rows(
        grad_ref[...],
        weight_ref,
        value_ref[...].astype(F32),
        carried_ref[...].astype(F32),
        gain_ref[...],
    )
    out_ref[...] = result.astype(BF)

    @pl.when(pl.program_id(0) == 0)
    def _():
        sum_ref[...] = jnp.zeros_like(sum_ref)

    for i in range(2):
        sum_ref[i : i + 1, :] += sums[i]


def back_norm(grad, weight, values, carried, gain):
    rows, width = values.shape
    tile = min(rows, TILE)

    def by_rows(columns):
        return pl.BlockSpec((tile, columns), lambda i: (i, 0))

    def whole(*shape):
        return pl.BlockSpec(shape, lambda i: (0, 0))

    return pl.pallas_call(
        back_norm_kernel,
        grid=(rows // tile,),
        in_specs=[
            by_rows(grad.shape[1]),
            whole(*weight.shape),
            by_rows(width),
            by_rows(width),
            whole(1, width),
        ],
        out_specs=[by_rows(width), whole(2, width)],
        out_shape=[
            jax.ShapeDtypeStruct((rows, width), BF),
            jax.ShapeDtypeStruct((2, width), F32),
        ],
        compiler_params=pltpu.CompilerParams(vmem_limit_bytes=40 * 2**20),
        cost_estimate=pl.CostEstimate(
            flops=2 * rows * width * grad.shape[1],
            bytes_accessed=2 * grad.shape[1] * (rows + width),
            transcendentals=0,
        ),
        name="back_norm",
    )(grad, weight, values, carried, gain[None])


def act_kernel(normed_ref, weight_ref, bias_ref, act_ref, turned_ref, slope_ref):
    hidden = dot_nn(normed_ref[...], weight_ref[...]) + bias_ref[...]
    root, cubic = math.sqrt(2.0 / math.pi), 0.044715
    square = hidden * hidden
    tanh = jnp.tanh(root * hidden * (1.0 + cubic * square))
    half = 0.5 + 0.5 * tanh
    act = (hidden * half).astype(BF)
    act_ref[...] = act
    turned_ref[...] = act.T
    slope_ref[...] = (
        half + (0.5 * root) * hidden * (1.0 - tanh * tanh) * (1.0 + 3.0 * cubic * square)
    ).astype(BF)


def activate(normed, weight, bias):
    rows, units = normed.shape[0], weight.shape[1]
    tile = 512
    return pl.pallas_call(
        act_kernel,
        grid=(units // tile,),
        in_specs=[
            pl.BlockSpec(normed.shape, lambda j: (0, 0)),
            pl.BlockSpec((weight.shape[0], tile), lambda j: (0, j)),
            pl.BlockSpec((1, tile), lambda j: (0, j)),
        ],
        out_specs=[
            pl.BlockSpec((rows, tile), lambda j: (0, j)),
            pl.BlockSpec((tile, rows), lambda j: (j, 0)),
            pl.BlockSpec((rows, tile), lambda j: (0, j)),
        ],
        out_shape=[
            pltpu.HBM((rows, units), BF),
            pltpu.HBM((units, rows), BF),
            pltpu.HBM((rows, units), BF),
        ],
        compiler_params=pltpu.CompilerParams(vmem_limit_bytes=24 * 2**20),
        cost_estimate=pl.CostEstimate(
            flops=2 * rows * units * weight.shape[0],
            bytes_accessed=2 * units * (3 * rows + weight.shape[0]),
            transcendentals=rows * units,
        ),
        name="activate",
    )(normed, weight, bias[None])


def back_act_kernel(grad_ref, weight_ref, slope_ref, out_ref, sum_ref):
    back = (dot_nt(grad_ref[...], weight_ref[...]) * slope_ref[...].astype(F32)).astype(BF)
    out_ref[...] = back
    sum_ref[...] = jnp.sum(back.astype(F32), axis=0, keepdims=True)


def back_act(grad, weight, slope):
    rows, units = slope.shape
    tile = 512
    return pl.pallas_call(
        back_act_kernel,
        grid=(units // tile,),
        in_specs=[
            pl.BlockSpec(grad.shape, lambda j: (0, 0)),
            pl.BlockSpec((tile, grad.shape[1]), lambda j: (j, 0)),
            pl.BlockSpec((rows, tile), lambda j: (0, j)),
        ],
        out_specs=[
            pl.BlockSpec((rows, tile), lambda j: (0, j)),
            pl.BlockSpec((1, tile), lambda j: (0, j)),
        ],
        out_shape=[
            jax.ShapeDtypeStruct((rows, units), BF),
            jax.ShapeDtypeStruct((1, units), F32),
        ],
        compiler_params=pltpu.CompilerParams(vmem_limit_bytes=24 * 2**20),
        cost_estimate=pl.CostEstimate(
            flops=2 * rows * units * grad.shape[1],
            bytes_accessed=2 * units * (2 * rows + grad.shape[1]),
            transcendentals=0,
        ),
        name="back_act",
    )(grad, weight, slope)


def hop(block, axis, flip):
    size = lax.axis_size(axis)
    return lax.ppermute(block, axis, [(i, i ^ flip) for i in range(size)])


def add_low(one, other):
    return (one.astype(F32) + other.astype(F32)).astype(BF)


def lay_kernel(rows, places, splits, *refs):
    count, outs = len(places), len(splits)
    parts, whole = refs[:count], refs[count : count + outs]
    stage = refs[count + outs : 2 * count + outs]
    came, left = refs[-2:]
    me = lax.axis_index("tm")
    inward = [pltpu.make_async_copy(parts[i], stage[i], came.at[i]) for i in range(count)]
    for copy in inward:
        copy.start()
    outward = []
    for i, (flip, start) in enumerate(places):
        at = pl.multiple_of((me ^ flip) * rows + start, 32)
        inward[i].wait()
        first = 0
        for j, columns in enumerate(splits):
            outward.append(
                pltpu.make_async_copy(
                    stage[i].at[:, pl.ds(first, columns)],
                    whole[j].at[pl.ds(at, parts[i].shape[0]), :],
                    left.at[i, j],
                )
            )
            outward[-1].start()
            first += columns
    for copy in outward:
        copy.wait()


def first_hops(block):
    if lax.axis_size("tm") != 8:
        return None
    return hop(block, "tm", 2), hop(block, "tm", 4)


def second_hops(came):
    if came is None:
        return None
    half = came[0].shape[0] // 2
    return hop(came[0][:half], "tm", 4), hop(came[1][half:], "tm", 2)


def gather_rows(block, came, passed, splits):
    if came is None:
        whole = lax.all_gather(block, "tm", axis=0, tiled=True)
        return jnp.split(whole, [sum(splits[:i]) for i in range(1, len(splits))], axis=1)
    rows = block.shape[0]
    half = rows // 2
    by_two, by_four = came
    low_six, high_six = passed
    pieces = ((block, 0, 0), (by_two, 2, 0), (by_four, 4, 0), (low_six, 6, 0), (high_six, 6, half))
    parts, places = [], []
    for piece, flip, start in pieces:
        for core in range(2):
            parts.append(hop(piece, "tm", 1) if core else piece)
            places.append((flip + core, start))
    return pl.pallas_call(
        lambda *refs: lay_kernel(rows, places, splits, *refs),
        in_specs=[pl.BlockSpec(memory_space=pl.ANY)] * len(parts),
        out_specs=[pl.BlockSpec(memory_space=pltpu.HBM)] * len(splits),
        out_shape=[jax.ShapeDtypeStruct((8 * rows, n), block.dtype) for n in splits],
        scratch_shapes=[pltpu.VMEM(part.shape, part.dtype) for part in parts]
        + [
            pltpu.SemaphoreType.DMA((len(parts),)),
            pltpu.SemaphoreType.DMA((len(parts), len(splits))),
        ],
        compiler_params=pltpu.CompilerParams(vmem_limit_bytes=20 * 2**20),
        cost_estimate=pl.CostEstimate(
            flops=0, bytes_accessed=32 * rows * block.shape[1], transcendentals=0
        ),
        name="lay_rows",
    )(*parts)


def after(value, *others):
    return lax.optimization_barrier((value,) + others)[0]


def first_kernel(*refs):
    blocks, small_ref, tokens_ref = refs[:2], refs[2], refs[3]
    wholes, smalls_ref, frames_ref = refs[4:6], refs[6], refs[7]
    local, small_sem, frame_sem, near, far, core = refs[8:]
    me, side = lax.axis_index("tm"), lax.axis_index("space")
    rows = blocks[0].shape[0]
    half = rows // 2
    half_grid, own_frames = tokens_ref.shape[1], tokens_ref.shape[0] // 2

    barrier = pltpu.get_barrier_semaphore()
    for flip in range(1, 8):
        pl.semaphore_signal(
            barrier, inc=1, device_id={"tm": me ^ flip}, device_id_type=pl.DeviceIdType.MESH
        )
    pl.semaphore_signal(
        barrier, inc=1, device_id={"space": 1 - side}, device_id_type=pl.DeviceIdType.MESH
    )
    pl.semaphore_wait(barrier, 8)

    sent = []

    def send(src, dst, sems, device):
        copy = pltpu.make_async_remote_copy(
            src_ref=src,
            dst_ref=dst,
            send_sem=sems.at[0],
            recv_sem=sems.at[1],
            device_id=device,
            device_id_type=pl.DeviceIdType.MESH,
        )
        copy.start()
        sent.append(copy)
        return copy

    def place(w, flip, start, length):
        at = pl.multiple_of((me ^ flip) * rows + start, half)
        return wholes[w].at[pl.ds(at, length), :]

    arrived = {}
    for w in range(2):
        for number, (flip, start) in enumerate(((2, 0), (4, half), (2, half), (4, 0))):
            arrived[w, flip, start] = send(
                blocks[w].at[pl.ds(start, half), :],
                place(w, 0, start, half),
                near.at[w, number],
                {"tm": me ^ flip},
            )
    small_copies = [
        send(small_ref, smalls_ref.at[me], small_sem.at[flip], {"tm": me ^ flip})
        for flip in range(1, 8)
    ]
    columns = pl.ds(pl.multiple_of(side * half_grid, half_grid), half_grid)
    frame_copy = send(
        tokens_ref.at[pl.ds((1 - side) * own_frames, own_frames)],
        frames_ref.at[:, columns, :],
        frame_sem,
        {"space": 1 - side},
    )
    core_copies = [
        send(blocks[w], place(w, 0, 0, rows), core.at[w, 0], {"tm": me ^ 1}) for w in range(2)
    ]
    own = [
        pltpu.make_async_copy(small_ref, smalls_ref.at[me], local.at[0]),
        pltpu.make_async_copy(
            tokens_ref.at[pl.ds(side * own_frames, own_frames)],
            frames_ref.at[:, columns, :],
            local.at[1],
        ),
    ] + [pltpu.make_async_copy(blocks[w], place(w, 0, 0, rows), local.at[2 + w]) for w in range(2)]
    for copy in own:
        copy.start()
    for w in range(2):
        for number, (flip, start) in enumerate(((2, 0), (4, half), (2, half), (4, 0))):
            arrived[w, flip, start].wait_recv()
            block = place(w, flip, start, half)
            if number < 2:
                arrived[w, 6, start] = send(
                    block, block, far.at[w, number], {"tm": me ^ (6 - flip)}
                )
            core_copies.append(send(block, block, core.at[w, 1 + number], {"tm": me ^ 1}))
    for w in range(2):
        for number, start in enumerate((0, half)):
            arrived[w, 6, start].wait_recv()
            block = place(w, 6, start, half)
            core_copies.append(send(block, block, core.at[w, 5 + number], {"tm": me ^ 1}))
    for copy in small_copies + [frame_copy] + core_copies:
        copy.wait_recv()
    for copy in own:
        copy.wait()
    for copy in sent:
        copy.wait_send()


def first_gather(weights, small, tokens):
    if lax.axis_size("tm") != 8:
        return (
            *[lax.all_gather(weight, "tm", axis=0, tiled=True) for weight in weights],
            lax.all_gather(small, "tm", axis=0),
            lax.all_to_all(tokens, "space", 0, 1, tiled=True),
        )
    used = small.shape[0]
    small = jnp.pad(small, ((0, -used % 16), (0, 0)))
    frames, half_grid, model = tokens.shape
    dma = pltpu.SemaphoreType.DMA
    first, second, smalls, whole_frames = pl.pallas_call(
        first_kernel,
        in_specs=[pl.BlockSpec(memory_space=pltpu.VMEM)] * 4,
        out_specs=[pl.BlockSpec(memory_space=pltpu.HBM)] * 4,
        out_shape=[
            pltpu.HBM((8 * weight.shape[0], weight.shape[1]), weight.dtype) for weight in weights
        ]
        + [
            jax.ShapeDtypeStruct((8,) + small.shape, small.dtype),
            jax.ShapeDtypeStruct((frames // 2, 2 * half_grid, model), tokens.dtype),
        ],
        scratch_shapes=[
            dma((4,)),
            dma((8, 2)),
            dma((2,)),
            dma((2, 4, 2)),
            dma((2, 2, 2)),
            dma((2, 7, 2)),
        ],
        compiler_params=pltpu.CompilerParams(
            vmem_limit_bytes=16 * 2**20, collective_id=3, has_side_effects=True
        ),
        cost_estimate=pl.CostEstimate(flops=0, bytes_accessed=2**24, transcendentals=0),
        name="first_gather",
    )(*weights, small, tokens)
    return first, second, smalls[:, :used], whole_frames


UNIT = 128
WIDE = 256
ORDERS = ((3, 7, 1, 5), (5, 7, 1, 3), (2, 6, 0, 4), (4, 6, 0, 2))


OPERANDS = (
    "act_turned",
    "out_low",
    "normed_three",
    "grad_pre",
    "packed",
    "grad_mixed",
    "normed_two",
    "grad_packed_two",
    "time_mixed",
    "time_branch",
    "weight",
    "inputs",
    "branch",
    "space_mixed",
    "normed_one",
    "small",
)
SMALL_ROWS, SMALL_COLUMNS = 32, 128
SLOTS = 6
FINALS = 10
DELAYS = (0, 1, 3, 5, 7, 9, 11, 13)


def last_kernel(chunks, places, *refs):
    refs = list(refs)

    def take(count):
        taken = refs[:count]
        del refs[:count]
        return taken

    count = len(OPERANDS)
    far_off = dict(zip(OPERANDS, take(count)))
    probs_ref, embedded_ref, gain_ref, one_hot_ref = take(4)
    out_refs, small_out, frames_out = take(len(chunks)), take(1)[0], take(1)[0]
    near = dict(zip(OPERANDS, take(count)))
    (grad_packed, turned, lines, kept, probs_near) = take(5)
    (far, own, from_core, from_chip, from_owner, share, from_space, from_row, final) = take(9)
    (core_sem, chip_sem, owner_sem, space_sem, row_sem, back_sem, last_sem) = take(7)
    load_sem, probs_sem, frame_sem = take(3)
    me, side, level = lax.axis_index("tm"), lax.axis_index("space"), lax.axis_index("row")
    total = len(places)
    r = UNIT
    frames = grad_packed.shape[0] // TILE
    units = frames * PAIRS

    loads = {
        name: pltpu.make_async_copy(far_off[name], near[name], load_sem.at[i])
        for i, name in enumerate(OPERANDS)
    }
    for name in OPERANDS:
        loads[name].start()
    waited = set()

    def here(name):
        if name == "grad_packed_one":
            return grad_packed
        if name not in waited:
            waited.add(name)
            loads[name].wait()
        return near[name]

    def tm_at(flip):
        return {"tm": me ^ flip}

    barrier = pltpu.get_barrier_semaphore()
    for device in (tm_at(1), tm_at(2), tm_at(4), {"space": 1 - side}, {"row": 1 - level}):
        pl.semaphore_signal(barrier, inc=1, device_id=device, device_id_type=pl.DeviceIdType.MESH)
    pl.semaphore_wait(barrier, 5)

    def start(src, dst, sems, device):
        copy = pltpu.make_async_remote_copy(
            src_ref=src,
            dst_ref=dst,
            send_sem=sems.at[0],
            recv_sem=sems.at[1],
            device_id=device,
            device_id_type=pl.DeviceIdType.MESH,
        )
        copy.start()
        return copy

    cores, chips, owners, spaces, rows, backs, lasts = ({} for _ in range(7))

    def size(t):
        return (SMALL_ROWS, SMALL_COLUMNS) if places[t][0] == len(chunks) else (UNIT, WIDE)

    def box(t, first, count=1):
        each, wide = size(t)
        return pl.ds(first * each, count * each), pl.ds(0, wide)

    def part(t, h, order):
        which, row, column, half = places[t]
        if which == len(chunks):
            return jnp.concatenate([lines[me ^ flip] for flip in order], axis=0)
        left, right = chunks[which]
        source = here(left) if left == "act_turned" else turned
        rows_each = source.shape[0] // 8
        picked = [
            source[pl.ds(pl.multiple_of((me ^ flip) * rows_each + row, r), r), :] for flip in order
        ]
        return dot_nn(
            jnp.concatenate(picked, axis=0), here(right)[:, pl.ds(column + h * half, WIDE)]
        )

    def stage_core(t):
        which, slot = places[t][0], t % SLOTS
        if which < len(chunks) and (t == 0 or places[t - 1][0] != which):
            if chunks[which][0] != "act_turned":
                turned[...] = here(chunks[which][0])[...].T
        for h in range(2):
            if t >= SLOTS:
                cores[t - SLOTS, h].wait_send()
            every = box(t, 0, 4)
            far[(slot, h, *every)] = part(t, h, ORDERS[h]).astype(BF)
            cores[t, h] = start(
                far.at[(slot, h, *every)],
                from_core.at[(slot, h, *every)],
                core_sem.at[slot, h],
                tm_at(1),
            )
        for h in range(2):
            if t >= SLOTS:
                chips[t - SLOTS, h].wait_send()
                owners[t - SLOTS, h].wait_send()
            own[(slot, h, *box(t, 0, 4))] = part(t, h, ORDERS[2 + h]).astype(BF)

    def stage_chip(t):
        slot = t % SLOTS
        for h in range(2):
            cores[t, h].wait_recv()
            every = (slot, h, *box(t, 0, 4))
            own[every] = add_low(own[every], from_core[every])
            near_half = (slot, h, *box(t, 0, 2))
            chips[t, h] = start(
                own.at[near_half],
                from_chip.at[near_half],
                chip_sem.at[slot, h],
                tm_at(4 if h else 2),
            )

    def stage_owner(t):
        slot = t % SLOTS
        for h in range(2):
            chips[t, h].wait_recv()
            upper = (slot, h, *box(t, 2, 2))
            own[upper] = add_low(own[upper], from_chip[(slot, h, *box(t, 0, 2))])
            owners[t, h] = start(
                own.at[(slot, h, *box(t, 3))],
                from_owner.at[(slot, h, *box(t, 0))],
                owner_sem.at[slot, h],
                tm_at(2 if h else 4),
            )

    def stage_space(t):
        slot = t % SLOTS
        if t >= SLOTS:
            spaces[t - SLOTS].wait_send()
            rows[t - SLOTS].wait_send()
        for h in range(2):
            owners[t, h].wait_recv()
            first = (slot, h, *box(t, 0))
            share[first] = add_low(own[(slot, h, *box(t, 2))], from_owner[first])
        spaces[t] = start(
            share.at[(slot, 1 - side, *box(t, 0))],
            from_space.at[(slot, *box(t, 0))],
            space_sem.at[slot],
            {"space": 1 - side},
        )

    def stage_row(t):
        slot = t % SLOTS
        spaces[t].wait_recv()
        first = (slot, side, *box(t, 0))
        share[first] = add_low(share[first], from_space[(slot, *box(t, 0))])
        half, wide = size(t)[0] // 2, pl.ds(0, size(t)[1])
        other = pl.ds(pl.multiple_of((1 - level) * half, half), half)
        rows[t] = start(
            share.at[slot, side, other, wide],
            from_row.at[slot, pl.ds(0, half), wide],
            row_sem.at[slot],
            {"row": 1 - level},
        )

    def stage_back(t):
        slot = t % SLOTS
        rows[t].wait_recv()
        half, wide = size(t)[0] // 2, pl.ds(0, size(t)[1])
        mine = pl.ds(pl.multiple_of(level * half, half), half)
        last = t % FINALS
        final[last, side, mine, wide] = add_low(
            share[slot, side, mine, wide], from_row[slot, pl.ds(0, half), wide]
        )
        place = final.at[last, side, mine, wide]
        backs[t] = start(place, place, back_sem.at[last], {"row": 1 - level})

    def stage_last(t):
        slot = t % FINALS
        backs[t].wait_recv()
        place = final.at[(slot, side, *box(t, 0))]
        lasts[t] = start(place, place, last_sem.at[slot], {"space": 1 - side})

    def stage_out(t):
        slot = t % FINALS
        lasts[t].wait_recv()
        out, row, column, half = places[t]
        if out == len(chunks):
            small_out[...] = final[(slot, 0, *box(t, 0))].astype(F32)
        else:
            for h in range(2):
                out_refs[out][pl.ds(row, r), pl.ds(column + h * half, WIDE)] = final[slot, h]
        backs[t].wait_send()
        lasts[t].wait_send()

    def probs_copy(unit):
        frame, pair = divmod(unit, PAIRS)
        return pltpu.make_async_copy(
            probs_ref.at[pl.ds(2 * pair, 2), pl.ds(frame * TILE, TILE), :],
            probs_near.at[unit % 2],
            probs_sem.at[unit % 2],
        )

    def attend(unit):
        frame, pair = divmod(unit, PAIRS)
        if unit + 1 < units:
            probs_copy(unit + 1).start()
        probs_copy(unit).wait()
        attn_bwd_tile(
            0,
            1,
            pair,
            here("packed"),
            None,
            here("grad_mixed"),
            grad_packed,
            base=frame * TILE,
            probs_pair=[probs_near[unit % 2, half] for half in range(2)],
        )

    def back_frame(frame):
        some = pl.ds(frame * TILE, TILE)
        values = here("inputs")[some, :].astype(F32) + embedded_ref[pl.ds(frame, 1), :]
        result, sums = back_norm_rows(
            grad_packed[some, :],
            here("weight"),
            values,
            here("branch")[some, :].astype(F32),
            gain_ref[...],
        )
        kept[frame] = result.astype(BF)
        column = jnp.sum(result, axis=0, keepdims=True)
        table = one_hot_ref[pl.ds(frame * ACTIONS, ACTIONS), :] * column
        width = MODEL // 8
        if frame == 0:
            lines[...] = here("small")[...]
        for k in range(8):
            at = slice(k * width, (k + 1) * width)
            lines[k, 0:ACTIONS, 0:width] += table[:, at]
            lines[k, ACTIONS : ACTIONS + 1, 0:width] += sums[0][:, at]
            lines[k, ACTIONS + 3 : ACTIONS + 4, 0:width] += sums[1][:, at]

    exchanged = []

    def exchange():
        half_grid = kept.shape[1] // 2
        own_frames = pl.ds(pl.multiple_of(side * frames, frames), frames)

        def columns(which):
            return pl.ds(pl.multiple_of(which * half_grid, half_grid), half_grid)

        exchanged.append(
            start(
                kept.at[:, columns(1 - side), :],
                frames_out.at[own_frames],
                frame_sem,
                {"space": 1 - side},
            )
        )
        frames_out[own_frames] = kept[:, columns(side), :]

    stages = (
        stage_core,
        stage_chip,
        stage_owner,
        stage_space,
        stage_row,
        stage_back,
        stage_last,
        stage_out,
    )
    probs_copy(0).start()
    for step in range(total + DELAYS[-1]):
        for delay, stage in zip(DELAYS, stages):
            if 0 <= step - delay < total:
                stage(step - delay)
        if 0 < step <= units:
            attend(step - 1)
        elif 0 <= step - 1 - units < frames:
            back_frame(step - 1 - units)
        elif step == 1 + units + frames:
            exchange()
    for t in range(max(0, total - SLOTS), total):
        for h in range(2):
            cores[t, h].wait_send()
            chips[t, h].wait_send()
            owners[t, h].wait_send()
        spaces[t].wait_send()
        rows[t].wait_send()
    exchanged[0].wait()


CHUNKS = (
    ("act_turned", "out_low"),
    ("normed_three", "grad_pre"),
    ("normed_two", "grad_packed_two"),
    ("time_mixed", "time_branch"),
    ("space_mixed", "branch"),
    ("normed_one", "grad_packed_one"),
)


def last_stage(given, probs, embedded, gain, one_hot):
    places, shapes = [], []
    for which, (left, right) in enumerate(CHUNKS):
        width = given[left].shape[0 if left == "act_turned" else 1]
        columns = 3 * MODEL if right == "grad_packed_one" else given[right].shape[1]
        shapes.append((width // 8, columns))
        for sub in range(width // (8 * UNIT)):
            for j in range(columns // 2 // WIDE):
                places.append((which, sub * UNIT, j * WIDE, columns // 2))
    places.append((len(CHUNKS), 0, 0, 0))
    small = given["small"]
    padding = ((0, 0), (0, SMALL_ROWS - small.shape[1]), (0, SMALL_COLUMNS - small.shape[2]))
    given = dict(given, small=jnp.pad(small, padding))
    tokens = given["packed"].shape[0]
    frames = tokens // TILE
    vmem = pltpu.VMEM
    dma = pltpu.SemaphoreType.DMA
    in_vmem, anywhere = pl.BlockSpec(memory_space=pltpu.VMEM), pl.BlockSpec(memory_space=pl.ANY)
    result = pl.pallas_call(
        lambda *refs: last_kernel(CHUNKS, places, *refs),
        in_specs=[anywhere] * (len(OPERANDS) + 1) + [in_vmem] * 3,
        out_specs=[in_vmem] * (len(shapes) + 2),
        out_shape=[jax.ShapeDtypeStruct(shape, BF) for shape in shapes]
        + [
            jax.ShapeDtypeStruct((SMALL_ROWS, SMALL_COLUMNS), F32),
            jax.ShapeDtypeStruct((2 * frames, TILE // 2, MODEL), BF),
        ],
        scratch_shapes=[vmem(given[name].shape, given[name].dtype) for name in OPERANDS]
        + [
            vmem((tokens, 3 * MODEL), BF),
            vmem((MODEL, tokens), BF),
            vmem((8, SMALL_ROWS, SMALL_COLUMNS), F32),
            vmem((frames, TILE, MODEL), BF),
            vmem((2, 2, TILE, TILE), BF),
            vmem((SLOTS, 2, 4 * UNIT, WIDE), BF),
            vmem((SLOTS, 2, 4 * UNIT, WIDE), BF),
            vmem((SLOTS, 2, 4 * UNIT, WIDE), BF),
            vmem((SLOTS, 2, 2 * UNIT, WIDE), BF),
            vmem((SLOTS, 2, UNIT, WIDE), BF),
            vmem((SLOTS, 2, UNIT, WIDE), BF),
            vmem((SLOTS, UNIT, WIDE), BF),
            vmem((SLOTS, UNIT // 2, WIDE), BF),
            vmem((FINALS, 2, UNIT, WIDE), BF),
            dma((SLOTS, 2, 2)),
            dma((SLOTS, 2, 2)),
            dma((SLOTS, 2, 2)),
            dma((SLOTS, 2)),
            dma((SLOTS, 2)),
            dma((FINALS, 2)),
            dma((FINALS, 2)),
            dma((len(OPERANDS),)),
            dma((2,)),
            dma((2,)),
        ],
        compiler_params=pltpu.CompilerParams(
            vmem_limit_bytes=60 * 2**20, collective_id=1, has_side_effects=True
        ),
        cost_estimate=pl.CostEstimate(
            flops=1024, bytes_accessed=len(places) * 8 * UNIT * WIDE, transcendentals=0
        ),
        name="last_stage",
    )(*[given[name] for name in OPERANDS], probs, embedded, gain[None], one_hot)
    grads = [grad.astype(F32) for grad in result[: len(shapes)]]
    return grads, result[-2][: small.shape[1], : small.shape[2]], result[-1]


def last_stage_plain(given, probs, embedded, gain, one_hot):
    tokens = given["packed"].shape[0]
    frames = tokens // TILE
    grad_packed = attention_back(given["packed"], probs, given["grad_mixed"], TILE)
    values = given["inputs"].astype(F32) + jnp.repeat(embedded, TILE, axis=0)
    result, sums = back_norm(grad_packed, given["weight"], values, given["branch"], gain)
    given = dict(given, grad_packed_one=grad_packed, act_turned=given["act_turned"].T)
    grads = []
    for left, right in CHUNKS:
        whole = weight_grad(given[left], given[right]).astype(BF)
        block = lax.psum_scatter(whole, "tm", scatter_dimension=0, tiled=True)
        grads.append(lax.psum(block, ("row", "space")).astype(F32))
    by_frame = jnp.sum(result.reshape(frames, TILE, MODEL).astype(F32), axis=1)
    table = jnp.dot(
        one_hot.reshape(frames, ACTIONS).T, by_frame, precision=lax.Precision.HIGHEST
    )
    none = jnp.zeros((2, MODEL), F32)
    rows = jnp.concatenate((table, sums[:1], none, sums[1:], none))
    size = lax.axis_size("tm")
    more = rows.reshape(-1, size, MODEL // size).transpose(1, 0, 2)
    small = given["small"].at[:, : more.shape[1]].add(more)
    block = lax.psum_scatter(small, "tm", scatter_dimension=0, tiled=True)[0]
    exchanged = lax.all_to_all(
        result.reshape(frames, TILE, MODEL), "space", 1, 0, tiled=True
    )
    return grads, lax.psum(block, ("row", "space")), exchanged


def body(
    block_input,
    action_table,
    norm_gain,
    norm_bias,
    space_qkv,
    space_out,
    time_qkv,
    time_out,
    ffn_in,
    ffn_bias_in,
    ffn_out,
    ffn_bias_out,
    out_grad,
    frame_segment,
    frame_action,
):
    tm, halves = lax.axis_size("tm"), lax.axis_size("space")
    slot, side = lax.axis_index("tm"), lax.axis_index("space")
    frame_count, half_grid = block_input.shape[1], block_input.shape[2]
    own_frames = frame_count // halves
    grid_all = half_grid * halves
    cut = half_grid // tm
    all_frames = frame_count * tm
    rows_dev = frame_count * half_grid
    width = MODEL // tm
    hidden_units = ffn_bias_in.shape[0]

    space_in_w, space_out_w, small, inputs = first_gather(
        (space_qkv, space_out),
        jnp.concatenate(
            [a.reshape(-1, width) for a in (action_table, norm_gain, norm_bias)]
            + [ffn_bias_out.reshape(1, width), ffn_bias_in.reshape(-1, width)]
        ),
        block_input[0],
    )
    lines = ACTIONS + 7
    by_row = small[:, :lines].transpose(1, 0, 2).reshape(lines, MODEL)
    table_full = by_row[:ACTIONS]
    gains = by_row[ACTIONS : ACTIONS + 3].astype(F32)
    shifts = by_row[ACTIONS + 3 : ACTIONS + 6].astype(F32)
    bias_out = by_row[ACTIONS + 6].astype(F32)
    bias_in = small[:, lines:].reshape(-1).astype(F32)

    actions = lax.dynamic_slice(frame_action[0], (side * own_frames,), (own_frames,))
    one_hot = (actions[:, None] == jnp.arange(ACTIONS)[None, :]).astype(BF)
    embedded = forward_dot(one_hot, table_full)

    time_block = jnp.concatenate((time_qkv, time_out), axis=1)
    if tm == 8:
        time_block = after(time_block, space_out_w)
    time_came = first_hops(time_block)

    hidden_zero = (inputs.astype(F32) + embedded[:, None, :]).reshape(rows_dev, MODEL)
    normed_one = layer_norm(hidden_zero, gains[0], shifts[0]).astype(BF)
    packed_one = forward_dot(normed_one, space_in_w).astype(BF)
    space_mixed, space_probs = attention(packed_one, grid_all)
    if tm == 8:
        space_mixed, *time_came = lax.optimization_barrier((space_mixed, *time_came))
    time_passed = second_hops(time_came)
    time_in_w, time_out_w = gather_rows(time_block, time_came, time_passed, (3 * MODEL, MODEL))
    in_block = after(ffn_in, *time_passed) if tm == 8 else ffn_in
    in_came = first_hops(in_block)
    hidden_one_own = (hidden_zero + forward_dot(space_mixed, space_out_w)).astype(BF)

    sent = hidden_one_own.reshape(own_frames, halves * tm, cut, MODEL)
    blocks_t = lax.all_to_all(sent, ("space", "tm"), 1, 0)
    hidden_one_low = lax.optimization_barrier(
        blocks_t.reshape(halves, tm, own_frames, cut, MODEL)
        .transpose(1, 0, 2, 3, 4)
        .reshape(rows_dev, MODEL)
    )
    hidden_one = hidden_one_low.astype(F32)
    groups = (
        frame_segment[0].astype(jnp.int32)[:, None] * cut + jnp.arange(cut, dtype=jnp.int32)
    ).reshape(rows_dev)

    normed_two = layer_norm(hidden_one, gains[1], shifts[1]).astype(BF)
    packed_two = forward_dot(normed_two, time_in_w).astype(BF)
    if tm == 8:
        packed_two, out_grad, *in_came = lax.optimization_barrier(
            (packed_two, out_grad, *in_came)
        )
    in_passed = second_hops(in_came)
    grad_out_low = swap_plain(True, out_grad[0])
    time_mixed, time_probs = attention(packed_two, rows_dev, groups)
    out_block = ffn_out
    if tm == 8:
        time_mixed, grad_out_low, out_block, *in_passed = lax.optimization_barrier(
            (time_mixed, grad_out_low, ffn_out, *in_passed)
        )
    grad_out_low = grad_out_low.reshape(rows_dev, MODEL)
    grad_out = grad_out_low.astype(F32)
    out_came = first_hops(out_block)
    (ffn_in_w,) = gather_rows(in_block, in_came, in_passed, (ffn_in.shape[1],))
    hidden_two = hidden_one + forward_dot(time_mixed, time_out_w)
    normed_three = layer_norm(hidden_two, gains[2], shifts[2]).astype(BF)
    act_low, act_turned, slope = activate(normed_three, ffn_in_w, bias_in)
    if tm == 8:
        slope, *out_came = lax.optimization_barrier((slope, *out_came))
    (ffn_out_w,) = gather_rows(out_block, out_came, second_hops(out_came), (MODEL,))
    bias_out_grad = jnp.sum(grad_out, axis=0)
    grad_pre_low, bias_in_grad = back_act(grad_out_low, ffn_out_w, slope)
    bias_in_grad = bias_in_grad[0]
    time_branch, sums_three = back_norm(
        grad_pre_low, ffn_in_w, hidden_two, grad_out_low, gains[2]
    )
    time_grad_mixed = back_dot(time_branch, time_out_w).astype(BF)
    block_out = (hidden_two + forward_dot(act_low, ffn_out_w) + bias_out).astype(BF)
    grad_packed_two, block_output = attention_back(
        packed_two,
        time_probs,
        time_grad_mixed,
        rows_dev,
        swap=block_out.reshape(all_frames, cut, MODEL),
    )
    block_output = block_output[None]
    grad_one_low, sums_two = back_norm(
        grad_packed_two, time_in_w, hidden_one_low, time_branch, gains[1]
    )

    sent = (
        grad_one_low.reshape(tm, halves, own_frames, cut, MODEL)
        .transpose(1, 0, 2, 3, 4)
        .reshape(halves * tm, own_frames, cut, MODEL)
    )
    space_branch = lax.all_to_all(sent, ("space", "tm"), 0, 1).reshape(rows_dev, MODEL)
    space_grad_mixed = back_dot(space_branch, space_out_w).astype(BF)
    none = jnp.zeros((1, MODEL), F32)
    by_row = jnp.concatenate(
        [jnp.zeros((ACTIONS, MODEL), F32)]
        + [
            row
            for i in range(2)
            for row in (none, sums_two[i : i + 1], sums_three[i : i + 1])
        ]
        + [bias_out_grad[None]]
    )
    shares = jnp.concatenate(
        (
            by_row.reshape(lines, tm, width).transpose(1, 0, 2),
            bias_in_grad.reshape(tm, -1, width),
        ),
        axis=1,
    )
    given = {
        "act_turned": act_turned,
        "out_low": grad_out_low,
        "normed_three": normed_three,
        "grad_pre": grad_pre_low,
        "packed": packed_one,
        "grad_mixed": space_grad_mixed,
        "normed_two": normed_two,
        "grad_packed_two": grad_packed_two,
        "time_mixed": time_mixed,
        "time_branch": time_branch,
        "weight": space_in_w,
        "inputs": inputs.reshape(rows_dev, MODEL),
        "branch": space_branch,
        "space_mixed": space_mixed,
        "normed_one": normed_one,
        "small": shares,
    }
    finish = last_stage if tm == 8 else last_stage_plain
    grads, small_grads, frames_grad = finish(
        given, space_probs, embedded, gains[0], one_hot.astype(F32).reshape(-1, 1)
    )
    ffn_out_grad, ffn_in_grad, time_qkv_grad, time_out_grad, space_out_grad, space_qkv_grad = grads
    input_grad = frames_grad.astype(F32)[None]
    return (
        block_output,
        input_grad,
        small_grads[:ACTIONS],
        small_grads[ACTIONS : ACTIONS + 3],
        small_grads[ACTIONS + 3 : ACTIONS + 6],
        space_qkv_grad,
        space_out_grad,
        time_qkv_grad,
        time_out_grad,
        ffn_in_grad,
        small_grads[lines:].reshape(hidden_units),
        ffn_out_grad,
        small_grads[ACTIONS + 6],
    )


def solution(mesh):
    placed = (
        P("row", "tm", "space", None),
        P(None, "tm"),
        P(None, "tm"),
        P(None, "tm"),
        P("tm", None),
        P("tm", None),
        P("tm", None),
        P("tm", None),
        P("tm", None),
        P("tm"),
        P("tm", None),
        P("tm"),
        P("row", "tm", "space", None),
        P("row", None),
        P("row", "tm"),
    )
    return jax.shard_map(
        body,
        mesh=mesh,
        in_specs=placed,
        out_specs=(
            P("row", "tm", "space", None),
            P("row", "tm", "space", None),
            P(None, "tm"),
            P(None, "tm"),
            P(None, "tm"),
            P("tm", None),
            P("tm", None),
            P("tm", None),
            P("tm", None),
            P("tm", None),
            P("tm"),
            P("tm", None),
            P("tm"),
        ),
        check_vma=False,
    )
```
